128 devices in a mesh: tm: 32 (over y, x_lo, z), row: 4 (over x_hi, core).
Axes of the slice: x: 4 (x_hi: 2, x_lo: 2; x = x_hi * 2 + x_lo), y: 4, z: 4, core: 2. Of those that a mesh axis runs over, the one named last changes fastest.
Arguments:
- latents: bfloat16 [256, 8, 32, 320], P('tm', 'row'), may hold values from -6 to 6
- window_shift: int32 [1], replicated, may hold values from 1 to 7
- timesteps: int32 [32], P('tm'), may hold values from 0 to 999
- motion_gain: float32 [320], replicated, may hold values from 0.25 to 1.75
- time_weight: float32 [320, 320], replicated, may hold values from -0.3125 to 0.3125
- qkv_weight: bfloat16 [320, 960], replicated, may hold values from -0.3125 to 0.3125
- attn_out_weight: bfloat16 [320, 320], replicated, may hold values from -0.3125 to 0.3125
- spatial_gain: float32 [320], replicated, may hold values from 0.25 to 1.75
- conv_weight: bfloat16 [9, 320, 1280], replicated, may hold values from -0.109375 to 0.109375
- proj_weight: bfloat16 [1280, 320], replicated, may hold values from -0.15625 to 0.15625
- out_cotangent: bfloat16 [256, 8, 32, 320], P('tm', 'row'), may hold values from -6 to 6
Outputs:
- block_output: bfloat16 [256, 8, 32, 320], P('tm', 'row')
- grad_input: float32 [256, 8, 32, 320], P('tm', 'row')
- grad_weights: float32 [512000], P(('tm', 'row'))
The draws below stay inside these ranges and needn't reach their ends.
All inputs are finite; a program needn't handle non-finite values.
Results may differ from the reference program's by a relative error of at most 0.017.
Values may be sent and summed in bfloat16 or wider, within the bound.
A program may use at most 128 MiB of HBM per device.

```python
import math
import jax
import jax.numpy as jnp
from jax import lax

CHANNELS = 320
HIDDEN_SIZE = 1280
HEADS = 8
STRIDE = 8
COLS = 32
FRAMES = 256
ROWS = 8
WINDOWS = 32


def plant(entries, rng, low, high):
    index_at = [jax.random.randint(jax.random.fold_in(rng, axis), (), 0, length) for axis, length in enumerate(entries.shape)]
    longest = entries.shape.index(max(entries.shape))
    neighbour = index_at[:longest] + [(index_at[longest] + 1) % entries.shape[longest]] + index_at[longest + 1:]
    return entries.at[tuple(index_at)].set(low).at[tuple(neighbour)].set(high)


def block_levels(own_key, extent, split, low, high):
    level = 1.0
    for position, shards_of in split:
        steps = jax.random.uniform(jax.random.fold_in(jax.random.fold_in(own_key, 6), position), (shards_of,), jnp.float32, low / len(split), high / len(split))
        level = level * jnp.repeat(jnp.exp(steps), extent[position] // shards_of).reshape((-1,) + (1,) * (len(extent) - 1 - position))
    return level


def scatter_about(own_key, extent, deviation, bound, cuts=(), kind=jnp.bfloat16):
    factor_of = block_levels(own_key, extent, cuts, -0.22, 0.18) if cuts else 1.0
    values = jax.random.normal(own_key, extent, jnp.float32) * deviation * factor_of
    return jnp.minimum(jnp.maximum(values, -bound), bound).astype(kind)


def setup_inputs(seed: int = 0) -> dict:
    streams_of = jax.random.split(jax.random.key(seed), 12)
    return {
        "latents": scatter_about(streams_of[0], (FRAMES, ROWS, COLS, CHANNELS), 1.0, 6.0, ((0, 32), (1, 4))),
        "window_shift": jax.random.randint(streams_of[1], (1,), 1, STRIDE).astype(jnp.int32),
        "timesteps": plant(jax.random.randint(streams_of[2], (WINDOWS,), 0, 1000), jax.random.fold_in(streams_of[2], 1), 0, 999).astype(jnp.int32),
        "motion_gain": jnp.clip(1.0 + 0.15 * jax.random.normal(streams_of[3], (CHANNELS,), jnp.float32), 0.25, 1.75),
        "time_weight": scatter_about(streams_of[4], (CHANNELS, CHANNELS), CHANNELS ** -0.5, 0.3125, (), jnp.float32),
        "qkv_weight": scatter_about(streams_of[5], (CHANNELS, 3 * CHANNELS), CHANNELS ** -0.5, 0.3125),
        "attn_out_weight": scatter_about(streams_of[6], (CHANNELS, CHANNELS), CHANNELS ** -0.5, 0.3125),
        "spatial_gain": jnp.clip(1.0 + 0.15 * jax.random.normal(streams_of[7], (CHANNELS,), jnp.float32), 0.25, 1.75),
        "conv_weight": scatter_about(streams_of[8], (9, CHANNELS, HIDDEN_SIZE), (9 * CHANNELS) ** -0.5, 0.109375),
        "proj_weight": scatter_about(streams_of[9], (HIDDEN_SIZE, CHANNELS), HIDDEN_SIZE ** -0.5, 0.15625),
        "out_cotangent": scatter_about(streams_of[10], (FRAMES, ROWS, COLS, CHANNELS), 1.0, 6.0, ((0, 32), (1, 4))),
    }


HIGHEST = lax.Precision.HIGHEST

def rounded(values):
    return lax.optimization_barrier(values.astype(jnp.bfloat16))

def rms_gain(values, gain_vector):
    return values * lax.rsqrt(lax.optimization_barrier(jnp.mean(values * values, axis=-1, keepdims=True)) + 1e-06) * gain_vector

def embedding(timestep_ids, channels):
    half_width = channels // 2
    frequency = jnp.exp(-math.log(10000.0) * jnp.arange(half_width, dtype=jnp.float32) / half_width)
    angles = timestep_ids.astype(jnp.float32)[:, None] * frequency[None, :]
    return jnp.concatenate([jnp.cos(angles), jnp.sin(angles)], axis=-1)

def split_heads(joined, head_count):
    return joined.reshape(joined.shape[0], joined.shape[1], head_count, joined.shape[2] // head_count)

def attend(joined, head_count):
    channels = joined.shape[-1] // 3
    query_part = split_heads(joined[..., :channels], head_count)
    key_part = split_heads(joined[..., channels:2 * channels], head_count)
    value_part = split_heads(joined[..., 2 * channels:], head_count)
    scaling = 1.0 / math.sqrt(channels // head_count)
    scores = jnp.einsum('fphd,gphd->phfg', query_part, key_part, precision=HIGHEST) * scaling
    weights = jnp.exp(scores)
    weights = weights / lax.optimization_barrier(jnp.sum(weights, axis=-1, keepdims=True))
    return (weights, value_part)

def window_core(packed_rows, offset_vec, out_weight, head_count):
    joined = packed_rows + offset_vec
    weights, value_part = attend(joined, head_count)
    mixture = jnp.einsum('phfg,gphd->fphd', weights, value_part, precision=HIGHEST)
    mixture = mixture.reshape(joined.shape[0], joined.shape[1], joined.shape[2] // 3)
    return jnp.einsum('fpc,cd->fpd', mixture, out_weight, precision=HIGHEST)

def window_rounded(packed_rows, offset_vec, out_weight, head_count):
    joined = rounded(packed_rows.astype(jnp.float32) + offset_vec).astype(jnp.float32)
    weights, value_part = attend(joined, head_count)
    weights = rounded(weights).astype(jnp.float32)
    mixture = jnp.einsum('phfg,gphd->fphd', weights, value_part, precision=HIGHEST)
    mixture = rounded(mixture.reshape(joined.shape[0], joined.shape[1], joined.shape[2] // 3))
    return jnp.dot(mixture, out_weight, preferred_element_type=jnp.float32)

def conv_forward(normed, kernel):
    row_count, col_count = (normed.shape[1], normed.shape[2])
    padded = jnp.pad(normed, ((0, 0), (1, 1), (1, 1), (0, 0)))
    totals = jnp.zeros(normed.shape[:3] + (kernel.shape[2],), jnp.float32)
    for row_tap in range(3):
        for col_tap in range(3):
            window = padded[:, row_tap:row_tap + row_count, col_tap:col_tap + col_count]
            totals = totals + jnp.dot(window, kernel[row_tap * 3 + col_tap], preferred_element_type=jnp.float32)
    return totals

def conv_backward(cotangent, kernel):
    row_count, col_count = (cotangent.shape[1], cotangent.shape[2])
    padded = jnp.pad(cotangent, ((0, 0), (1, 1), (1, 1), (0, 0)))
    totals = jnp.zeros(cotangent.shape[:3] + (kernel.shape[1],), jnp.float32)
    for row_tap in range(3):
        for col_tap in range(3):
            window = padded[:, 2 - row_tap:2 - row_tap + row_count, 2 - col_tap:2 - col_tap + col_count]
            totals = totals + jnp.dot(window, kernel[row_tap * 3 + col_tap].T, preferred_element_type=jnp.float32)
    return totals

def reference(latents, window_shift, timesteps, motion_gain, time_weight, qkv_weight, attn_out_weight, spatial_gain, conv_weight, proj_weight, out_cotangent):
    places = ROWS * COLS
    input_f32 = latents.astype(jnp.float32).reshape(FRAMES, places, CHANNELS)
    hidden = rounded(rms_gain(input_f32, motion_gain))
    packed = jnp.dot(hidden, qkv_weight, preferred_element_type=jnp.float32).astype(jnp.bfloat16)
    embedded = embedding(timesteps, CHANNELS)
    extra_term = jnp.dot(embedded, time_weight, precision=HIGHEST)
    qkv_f32 = qkv_weight.astype(jnp.float32)
    offsets = jnp.dot(extra_term, qkv_f32, precision=HIGHEST)
    start_shift = window_shift[0]

    def frames_of(window_id):
        first = STRIDE * (window_id - 1) + start_shift
        return jnp.mod(first + jnp.arange(2 * STRIDE, dtype=jnp.int32), FRAMES).astype(jnp.int32)

    def add_window(window_id, sums):
        frame_ids = frames_of(window_id)
        result_rows = window_rounded(jnp.take(packed, frame_ids, axis=0), offsets[window_id], attn_out_weight, HEADS)
        return sums.at[frame_ids].add(result_rows)
    sums = lax.fori_loop(0, WINDOWS, add_window, jnp.zeros((FRAMES, places, CHANNELS), jnp.float32))
    motion = rounded(input_f32 + 0.5 * sums).reshape(FRAMES, ROWS, COLS, CHANNELS)
    motion_f32 = motion.astype(jnp.float32)
    normed = rounded(rms_gain(motion_f32, spatial_gain))
    pre_act = conv_forward(normed, conv_weight)
    activated = rounded(jax.nn.gelu(pre_act))
    block_output = (motion_f32 + jnp.dot(activated, proj_weight, preferred_element_type=jnp.float32)).astype(jnp.bfloat16)
    d_act = jnp.dot(out_cotangent, proj_weight.T, preferred_element_type=jnp.float32)
    gelu_out, gelu_back = jax.vjp(jax.nn.gelu, pre_act)
    d_pre = gelu_back(d_act)[0].astype(jnp.bfloat16)
    d_normed = conv_backward(d_pre, conv_weight)
    norm_out, norm_back = jax.vjp(lambda values: rms_gain(values, spatial_gain), motion_f32)
    d_motion = out_cotangent.astype(jnp.float32) + norm_back(d_normed)[0]
    window_cot = 0.5 * d_motion.reshape(FRAMES, places, CHANNELS)
    out_f32 = attn_out_weight.astype(jnp.float32)

    def back_window(carry, window_id):
        d_packed_sum, d_out_sum = carry
        frame_ids = frames_of(window_id)
        packed_rows = jnp.take(packed, frame_ids, axis=0).astype(jnp.float32)
        core_out, core_back = jax.vjp(lambda rows_in, offs_in, weight_in: window_core(rows_in, offs_in, weight_in, HEADS), packed_rows, offsets[window_id], out_f32)
        grad_rows, grad_offset, grad_weight = core_back(jnp.take(window_cot, frame_ids, axis=0))
        return ((d_packed_sum.at[frame_ids].add(grad_rows), d_out_sum + grad_weight), grad_offset)
    start_carry = (jnp.zeros((FRAMES, places, 3 * CHANNELS), jnp.float32), jnp.zeros((CHANNELS, CHANNELS), jnp.float32))
    (d_packed, d_out_weight), d_offsets = lax.scan(back_window, start_carry, jnp.arange(WINDOWS, dtype=jnp.int32))
    d_qkv = jnp.einsum('fpc,fpd->cd', hidden.astype(jnp.float32), d_packed, precision=HIGHEST)
    d_qkv = d_qkv + jnp.dot(extra_term.T, d_offsets, precision=HIGHEST)
    d_extra = jnp.dot(d_offsets, qkv_f32.T, precision=HIGHEST)
    d_time = jnp.dot(embedded.T, d_extra, precision=HIGHEST)
    d_hidden = jnp.dot(d_packed, qkv_f32.T, precision=HIGHEST)
    motion_out, motion_back = jax.vjp(lambda values: rms_gain(values, motion_gain), input_f32)
    grad_input = (d_motion.reshape(FRAMES, places, CHANNELS) + motion_back(d_hidden)[0]).reshape(FRAMES, ROWS, COLS, CHANNELS)
    scaling = 1.0 / math.sqrt(FRAMES * places)
    grad_weights = jnp.concatenate([d_qkv.reshape(-1), d_out_weight.reshape(-1), d_time.reshape(-1)]) * scaling
    return (block_output, grad_input, grad_weights)
```

```python
import math

import jax
import jax.numpy as jnp
from jax import lax
from jax.experimental import pallas as pl
from jax.experimental.pallas import tpu as pltpu
from jax.sharding import PartitionSpec as P

BF = jnp.bfloat16
F32 = jnp.float32
MESH = pl.DeviceIdType.MESH
VMEM = pltpu.VMEM

FR = 8
CELLS = 64
COLS = 32
CH = 320
HID = 1280
HEADS = 8
HD = 40
HP = 64
BLOCKS = 4
BC = CELLS // BLOCKS
PADQ = HEADS * HP
PADZ = 3 * PADQ
SCALE = 1.0 / math.sqrt(HD)
EXP2 = SCALE * math.log2(math.e)
EPS = 1e-06
VLIM = 56 * 1024 * 1024


def mm(a, b):
    return jnp.dot(a, b, preferred_element_type=F32)


def mm_nt(a, b):
    return lax.dot_general(a, b, (((1,), (1,)), ((), ())), preferred_element_type=F32)


def mm_tn(a, b):
    return lax.dot_general(a, b, (((0,), (0,)), ((), ())), preferred_element_type=F32)


def rms_scale(values):
    return lax.rsqrt(jnp.mean(values * values, axis=-1, keepdims=True) + EPS)


def rms_back(values, gain, cotangent):
    r = rms_scale(values)
    g = cotangent * gain
    return r * g - values * (r * r * r) * jnp.mean(g * values, axis=-1, keepdims=True)


def parts_of(row):
    first = row.astype(BF).astype(F32)
    rest = row - first
    second = rest.astype(BF).astype(F32)
    return first, second, rest - second


def stack_parts(row):
    a, b, c = parts_of(row)
    at = lax.broadcasted_iota(jnp.int32, (16, row.shape[1]), 0)
    return jnp.where(at == 0, a, jnp.where(at == 1, b, jnp.where(at == 2, c, 0.0))).astype(BF)


def outer(left, right):
    a, b, _ = parts_of(left)
    c, d, _ = parts_of(right)
    at = lax.broadcasted_iota(jnp.int32, (16, left.shape[1]), 0)
    lhs = jnp.where(at < 4, jnp.where(at % 2 == 0, a, b), 0.0).astype(BF)
    at = lax.broadcasted_iota(jnp.int32, (16, right.shape[1]), 0)
    rhs = jnp.where(at < 4, jnp.where(at < 2, c, d), 0.0).astype(BF)
    return mm_tn(lhs, rhs)


def greet(peers):
    barrier = pltpu.get_barrier_semaphore()
    for peer in peers:
        pl.semaphore_signal(barrier, inc=1, device_id=peer, device_id_type=MESH)
    pl.semaphore_wait(barrier, len(peers))


def remote(src, dst, send, recv, peer):
    return pltpu.make_async_remote_copy(
        src_ref=src, dst_ref=dst, send_sem=send, recv_sem=recv, device_id=peer, device_id_type=MESH
    )


def ring():
    at, count = lax.axis_index("tm"), lax.axis_size("tm")
    row = lax.axis_index("row")
    return ((at + count - 1) % count, row), ((at + 1) % count, row)


def pair_masks():
    lane = lax.broadcasted_iota(jnp.int32, (128, 128), 1)
    return lane < HP


def both_heads(x, first):
    zero = jnp.zeros_like(x)
    return jnp.concatenate([jnp.where(first, x, zero), jnp.where(first, zero, x)], axis=0)


def pair_probs(q, kst, same):
    s = mm_nt(q, kst)
    e = jnp.where(same, jnp.exp2(s * EXP2), 0.0)
    ea, eb = e[:, :128], e[:, 128:]
    return jnp.concatenate(
        [
            ea * (1.0 / jnp.sum(ea, axis=-1, keepdims=True)),
            eb * (1.0 / jnp.sum(eb, axis=-1, keepdims=True)),
        ],
        axis=1,
    )


def same_cell():
    row = lax.broadcasted_iota(jnp.int32, (128, 256), 0)
    lane = lax.broadcasted_iota(jnp.int32, (128, 256), 1)
    return row % 8 == lane % 8


def halo_copies(ext, send, recv, b, before, after):
    return (
        remote(ext.at[9:16], ext.at[1:8], send.at[0, b], recv.at[0, b], after),
        remote(ext.at[8:15], ext.at[16:23], send.at[1, b], recv.at[1, b], before),
    )


def return_copies(out, back, send, recv, b, before, after):
    return (
        remote(out.at[0:7], back.at[8:15], send.at[0, b], recv.at[0, b], before),
        remote(out.at[9:16], back.at[1:8], send.at[1, b], recv.at[1, b], after),
    )


def motion_kernel(
    shift_ref, lat_ref, mgain_ref, sgain_ref, extra_ref, w_ref, wo_ref,
    motion_ref, normed_ref, hwin_ref, wp_ref, wop_ref, off_ref,
    wo32, *rest,
):
    hext, wout, back = rest[0:4], rest[4:8], rest[8:12]
    send1, recv1, send2, recv2 = rest[12:16]
    before, after = ring()
    shift = shift_ref[0]
    mgain, sgain = mgain_ref[...], sgain_ref[...]
    for b in range(BLOCKS):
        x = lat_ref[:, BC * b : BC * b + BC, :].astype(F32)
        hext[b][8:16] = (x * rms_scale(x) * mgain).astype(BF)
    greet((before, after))
    ins = [halo_copies(hext[b], send1, recv1, b, before, after) for b in range(BLOCKS)]
    for pair in ins:
        for copy in pair:
            copy.start()
    wp_ref[...] = jnp.zeros_like(wp_ref)
    for j in range(3 * HEADS):
        wp_ref[:, HP * j : HP * j + HD] = w_ref[:, HD * j : HD * j + HD]
    wo32[...] = jnp.zeros_like(wo32)
    wo_f = wo_ref[...].astype(F32)
    for h in range(HEADS):
        wo32[HP * h : HP * h + HD, :] = wo_f[HD * h : HD * h + HD]
    wop_ref[...] = wo32[...].astype(BF)
    off_ref[...] = jnp.sum(mm(stack_parts(extra_ref[...]), wp_ref[...]), axis=0, keepdims=True)
    first, same = pair_masks(), same_cell()
    outs = []
    for b in range(BLOCKS):
        for copy in ins[b]:
            copy.wait_recv()
        hw = hext[b][pl.ds(shift, 16)]
        hwin_ref[b] = hw
        z = (mm(hw.reshape(16 * BC, CH), wp_ref[...]) + off_ref[...]).reshape(16, BC, PADZ)
        found = []
        for g in range(BC // 8):
            zg = z[:, 8 * g : 8 * g + 8, :].reshape(128, PADZ).astype(BF)
            mixed = []
            for i in range(HEADS // 2):
                q = zg[:, 128 * i : 128 * i + 128]
                k = zg[:, PADQ + 128 * i : PADQ + 128 * i + 128]
                v = zg[:, 2 * PADQ + 128 * i : 2 * PADQ + 128 * i + 128]
                p = pair_probs(q, both_heads(k, first), same).astype(BF)
                mixed.append(mm(p, both_heads(v, first)).astype(BF))
            found.append(mm(jnp.concatenate(mixed, axis=1), wop_ref[...]).reshape(16, 8, CH))
        wout[b][...] = jnp.concatenate(found, axis=1).astype(BF)
        pair = return_copies(wout[b], back[b], send2, recv2, b, before, after)
        for copy in pair:
            copy.start()
        outs.append(pair)
    for b in range(BLOCKS):
        for copy in outs[b]:
            copy.wait_recv()
        x = lat_ref[:, BC * b : BC * b + BC, :].astype(F32)
        both = wout[b][pl.ds(8 - shift, 8)].astype(F32) + back[b][pl.ds(8 - shift, 8)].astype(F32)
        m = (x + 0.5 * both).astype(BF)
        motion_ref[:, BC * b : BC * b + BC, :] = m
        m = m.astype(F32)
        normed_ref[:, BC * b : BC * b + BC, :] = (m * rms_scale(m) * sgain).astype(BF)
    for pair in ins + outs:
        for copy in pair:
            copy.wait_send()


def column_shifts(flat):
    count = flat.shape[0]
    col = lax.broadcasted_iota(jnp.int32, flat.shape, 0) % COLS
    left = jnp.where(col == 0, 0.0, pltpu.roll(flat, 1, 0))
    right = jnp.where(col == COLS - 1, 0.0, pltpu.roll(flat, count - 1, 0))
    return left, right


def spatial_kernel(
    normed_ref, motion_ref, cot_ref, sgain_ref, conv_ref, proj_ref,
    out_ref, dmot_ref,
    wbuf, x3, top, bot, pre, dpre, gtop, gbot, stop, sbot, keep,
    wsem, send, recv,
):
    row, rows = lax.axis_index("row"), lax.axis_size("row")
    tm = lax.axis_index("tm")
    above, below = (tm, row - 1), (tm, row + 1)
    has_above, has_below = row > 0, row < rows - 1
    loads = []
    for dy in (1, 0, 2):
        for t in range(3):
            loads.append((conv_ref.at[3 * dy + t, 0:256, :], wbuf.at[dy, 256 * t : 256 * t + 256, :]))
            loads.append((conv_ref.at[3 * dy + t, 256:320, :], wbuf.at[dy, 768 + 64 * t : 832 + 64 * t, :]))
    loads = [pltpu.make_async_copy(a, c, wsem.at[j]) for j, (a, c) in enumerate(loads)]
    for load in loads:
        load.start()
    for dy in range(3):
        wbuf[dy, 960:1024, :] = jnp.zeros((64, HID), BF)
    barrier = pltpu.get_barrier_semaphore()

    @pl.when(has_above)
    def _():
        pl.semaphore_signal(barrier, inc=1, device_id=above, device_id_type=MESH)

    @pl.when(has_below)
    def _():
        pl.semaphore_signal(barrier, inc=1, device_id=below, device_id_type=MESH)

    pl.semaphore_wait(barrier, (row > 0).astype(jnp.int32) + (row < rows - 1).astype(jnp.int32))
    up = remote(normed_ref.at[:, 0:32, :], bot, send.at[0], recv.at[0], above)
    down = remote(normed_ref.at[:, 32:64, :], top, send.at[1], recv.at[1], below)
    gup = remote(stop, gbot, send.at[2], recv.at[2], above)
    gdown = remote(sbot, gtop, send.at[3], recv.at[3], below)
    pl.when(has_above)(lambda: up.start())
    pl.when(has_below)(lambda: down.start())

    def place(at, plane):
        flat = plane.astype(F32).reshape(FR * COLS, CH)
        left, right = column_shifts(flat)
        for t, values in enumerate((left, flat, right)):
            values = values.astype(BF).reshape(FR, COLS, CH)
            x3[:, at, :, 256 * t : 256 * t + 256] = values[:, :, :256]
            x3[:, at, :, 768 + 64 * t : 832 + 64 * t] = values[:, :, 256:]
        x3[:, at, :, 960:1024] = jnp.zeros((FR, COLS, 64), BF)

    place(1, normed_ref[:, 0:32, :])
    place(2, normed_ref[:, 32:64, :])

    def add_taps(dy, n):
        taps = x3[:, dy : dy + 2].reshape(FR * CELLS, 1024)
        return mm(taps, wbuf[dy, :, 256 * n : 256 * n + 256])

    for load in loads[:6]:
        load.wait()
    for n in range(5):
        pre[:, 256 * n : 256 * n + 256] = add_taps(1, n)

    @pl.when(has_below)
    def _():
        up_in = remote(normed_ref.at[:, 0:32, :], bot, send.at[0], recv.at[0], below)
        up_in.wait_recv()
        place(3, bot[...])

    @pl.when(jnp.logical_not(has_below))
    def _():
        x3[:, 3] = jnp.zeros((FR, COLS, 1024), BF)

    @pl.when(has_above)
    def _():
        down_in = remote(normed_ref.at[:, 32:64, :], top, send.at[1], recv.at[1], above)
        down_in.wait_recv()
        place(0, top[...])

    @pl.when(jnp.logical_not(has_above))
    def _():
        x3[:, 0] = jnp.zeros((FR, COLS, 1024), BF)

    for load in loads[6:]:
        load.wait()
    cot = cot_ref[...].reshape(FR * CELLS, CH)
    total = motion_ref[...].astype(F32).reshape(FR * CELLS, CH)
    c0, c1 = math.sqrt(2.0 / math.pi), 0.044715
    for n in range(5):
        u = pre[:, 256 * n : 256 * n + 256] + add_taps(0, n) + add_taps(2, n)
        proj = proj_ref[256 * n : 256 * n + 256, :]
        dact = mm_nt(cot, proj)
        sq = u * u
        th = jnp.tanh(c0 * u * (1.0 + c1 * sq))
        half = 0.5 + 0.5 * th
        act = u * half
        slope = half + 0.5 * u * (1.0 - th * th) * (c0 + (3.0 * c0 * c1) * sq)
        dpre[:, 256 * n : 256 * n + 256] = (slope * dact).astype(BF)
        total = total + mm(act.astype(BF), proj)
    out_ref[...] = total.astype(BF).reshape(FR, CELLS, CH)

    def back_taps(dy):
        g = [mm_nt(dpre[...], wbuf[dy, 256 * j : 256 * j + 256, :]) for j in range(4)]
        col = lax.broadcasted_iota(jnp.int32, (FR * CELLS, 256), 0) % COLS
        count = FR * CELLS

        def from_right(x, c):
            return jnp.where(c == COLS - 1, 0.0, pltpu.roll(x, count - 1, 0))

        def from_left(x, c):
            return jnp.where(c == 0, 0.0, pltpu.roll(x, 1, 0))

        low = from_right(g[0], col) + g[1] + from_left(g[2], col)
        high = (
            from_right(g[3][:, :64], col[:, :64])
            + g[3][:, 64:128]
            + from_left(g[3][:, 128:192], col[:, :64])
        )
        return jnp.concatenate([low, high], axis=1).reshape(FR, 2, COLS, CH)

    y = back_taps(0)
    stop[...] = y[:, 0].astype(BF)
    pl.when(has_above)(lambda: gup.start())
    keep[:, 0] = y[:, 1]
    y = back_taps(2)
    sbot[...] = y[:, 1].astype(BF)
    pl.when(has_below)(lambda: gdown.start())
    keep[:, 1] = y[:, 0]
    y = back_taps(1)
    keep[...] = keep[...] + y

    @pl.when(has_below)
    def _():
        gup_in = remote(stop, gbot, send.at[2], recv.at[2], below)
        gup_in.wait_recv()
        keep[:, 1] = keep[:, 1] + gbot[...].astype(F32)

    @pl.when(has_above)
    def _():
        gdown_in = remote(sbot, gtop, send.at[3], recv.at[3], above)
        gdown_in.wait_recv()
        keep[:, 0] = keep[:, 0] + gtop[...].astype(F32)

    d_normed = keep[...].reshape(FR, CELLS, CH)
    dmot_ref[...] = cot_ref[...].astype(F32) + rms_back(
        motion_ref[...].astype(F32), sgain_ref[...], d_normed
    )

    @pl.when(has_above)
    def _():
        up.wait_send()
        gup.wait_send()

    @pl.when(has_below)
    def _():
        down.wait_send()
        gdown.wait_send()


def grad_kernel(
    shift_ref, lat_ref, mgain_ref, dmot_ref, hwin_ref, wp_ref, wop_ref, off_ref, extra_ref, emb_ref,
    gin_ref, flat0, flat1, flat2,
    hall, mall, call, dzall, *rest,
):
    cext, dh, back = rest[0:4], rest[4:8], rest[8:12]
    send1, recv1, send2, recv2 = rest[12:16]
    before, after = ring()
    shift = shift_ref[0]
    for b in range(BLOCKS):
        cext[b][8:16] = (0.5 * dmot_ref[:, BC * b : BC * b + BC, :]).astype(BF)
    greet((before, after))
    ins = [halo_copies(cext[b], send1, recv1, b, before, after) for b in range(BLOCKS)]
    for pair in ins:
        for copy in pair:
            copy.start()
    first, same = pair_masks(), same_cell()
    rows = 16 * BC
    lane = lax.broadcasted_iota(jnp.int32, (rows, 64), 1)
    ones = jnp.where(lane == 0, 1.0, 0.0).astype(BF)
    outs = []
    for b in range(BLOCKS):
        hw = hwin_ref[b].reshape(rows, CH)
        hall[rows * b : rows * b + rows, 0:CH] = hw
        hall[rows * b : rows * b + rows, CH : CH + 64] = ones
        z = (mm(hw, wp_ref[...]) + off_ref[...]).reshape(16, BC, PADZ)
        for copy in ins[b]:
            copy.wait_recv()
        cw = cext[b][pl.ds(shift, 16)].reshape(rows, CH)
        call[rows * b : rows * b + rows, :] = cw
        dm = mm_nt(cw, wop_ref[...]).reshape(16, BC, PADQ)
        dzs, mixes = [], []
        for g in range(BC // 8):
            zg = z[:, 8 * g : 8 * g + 8, :].reshape(128, PADZ).astype(BF)
            dmg = dm[:, 8 * g : 8 * g + 8, :].reshape(128, PADQ)
            dqs, dks, dvs, mixed = [], [], [], []
            for i in range(HEADS // 2):
                q = zg[:, 128 * i : 128 * i + 128]
                kst = both_heads(zg[:, PADQ + 128 * i : PADQ + 128 * i + 128], first)
                vst = both_heads(zg[:, 2 * PADQ + 128 * i : 2 * PADQ + 128 * i + 128], first)
                p = pair_probs(q, kst, same)
                pb = p.astype(BF)
                mix = mm(pb, vst)
                mixed.append(mix)
                dmi = dmg[:, 128 * i : 128 * i + 128]
                dmb = dmi.astype(BF)
                prod = mix * dmi
                da = jnp.sum(jnp.where(first, prod, 0.0), axis=-1, keepdims=True)
                db = jnp.sum(jnp.where(first, 0.0, prod), axis=-1, keepdims=True)
                dp = mm_nt(dmb, vst)
                ds = jnp.concatenate(
                    [
                        p[:, :128] * (dp[:, :128] - da) * SCALE,
                        p[:, 128:] * (dp[:, 128:] - db) * SCALE,
                    ],
                    axis=1,
                ).astype(BF)
                dqs.append(mm(ds, kst))
                dk = mm_tn(ds, q)
                dks.append(jnp.where(first, dk[:128], dk[128:]))
                dv = mm_tn(pb, dmb)
                dvs.append(jnp.where(first, dv[:128], dv[128:]))
            dzs.append(jnp.concatenate(dqs + dks + dvs, axis=1).reshape(16, 8, PADZ))
            mixes.append(jnp.concatenate(mixed, axis=1).reshape(16, 8, PADQ))
        dz = jnp.concatenate(dzs, axis=1).reshape(rows, PADZ).astype(BF)
        dzall[rows * b : rows * b + rows, :] = dz
        mall[rows * b : rows * b + rows, :] = (
            jnp.concatenate(mixes, axis=1).reshape(rows, PADQ).astype(BF)
        )
        dh[b][...] = mm_nt(dz, wp_ref[...]).reshape(16, BC, CH).astype(BF)
        pair = return_copies(dh[b], back[b], send2, recv2, b, before, after)
        for copy in pair:
            copy.start()
        outs.append(pair)
    dw = mm_tn(hall[...], dzall[...])
    doff = dw[CH : CH + 1]
    dwq = dw[:CH] + outer(extra_ref[...], doff)
    at = lax.broadcasted_iota(jnp.int32, (PADQ, 384), 0)
    lane = lax.broadcasted_iota(jnp.int32, (PADQ, 384), 1)
    pick = (lane == HD * (at // HP) + at % HP) & (at % HP < HD)
    pick = jnp.where(pick, 1.0, 0.0).astype(BF)
    flats = (flat0, flat1, flat2)
    for part in range(3):
        block = mm(dwq[:, PADQ * part : PADQ * part + PADQ].astype(BF), pick)
        for j in range(3):
            flats[j][pl.ds(part, CH, stride=3), :] = block[:, 128 * j : 128 * j + 128]
    zeros = jnp.zeros((CH, 64), F32)
    dwo = mm_tn(mall[...], call[...])
    dext = jnp.sum(mm_nt(stack_parts(doff), wp_ref[...]), axis=0, keepdims=True)
    dtime = outer(emb_ref[...], dext)
    for j in range(3):
        wide = 128 if j < 2 else 64
        for h in range(HEADS):
            flats[j][960 + HD * h : 960 + HD * h + HD, 0:wide] = dwo[
                HP * h : HP * h + HD, 128 * j : 128 * j + wide
            ]
        flats[j][1280:1600, 0:wide] = dtime[:, 128 * j : 128 * j + wide]
        flats[j][1600:1608, :] = jnp.zeros((8, 128), F32)
    flat2[960:1280, 64:128] = zeros
    flat2[1280:1600, 64:128] = zeros
    for b in range(BLOCKS):
        for copy in outs[b]:
            copy.wait_recv()
        d_hidden = dh[b][pl.ds(8 - shift, 8)].astype(F32) + back[b][pl.ds(8 - shift, 8)].astype(F32)
        x = lat_ref[:, BC * b : BC * b + BC, :].astype(F32)
        gin_ref[:, BC * b : BC * b + BC, :] = dmot_ref[:, BC * b : BC * b + BC, :] + rms_back(
            x, mgain_ref[...], d_hidden
        )
    for pair in ins + outs:
        for copy in pair:
            copy.wait_send()


ORDERS = (("x", "y", "z"), ("y", "z", "x"), ("z", "x", "y"))


def place_of(tm, row):
    return {"y": tm // 8, "x": (row // 2) * 2 + (tm // 4) % 2, "z": tm % 4, "core": row % 2}


def device_at(at):
    return (at["y"] * 8 + (at["x"] % 2) * 4 + at["z"], (at["x"] // 2) * 2 + at["core"])


def sum_kernel(flat0, flat1, flat2, out_ref, *rest):
    a0, r0, a1, r1, a2, r2, a3, r3 = (rest[3 * j : 3 * j + 3] for j in range(8))
    send, recv = rest[24:26]
    me = place_of(lax.axis_index("tm"), lax.axis_index("row"))
    core = me["core"]
    twin = device_at({**me, "core": 1 - core})
    peers = {
        axis: [device_at({**me, axis: (me[axis] + d) % 4}) for d in (1, 2, 3)] for axis in "xyz"
    }
    greet((twin, *peers["x"], *peers["y"], *peers["z"]))

    def gather(j, carry):
        at = place_of(j // 2, (j % 2) * 2)
        for c in range(2):
            for part, (flat, order) in enumerate(zip((flat0, flat1, flat2), ORDERS)):
                index = (at[order[0]] * 4 + at[order[1]]) * 4 + at[order[2]]
                a0[part][c, index] = flat[pl.ds(25 * j + 12 * c, 16), :].astype(BF)
        return carry

    lax.fori_loop(0, 64, gather, 0)
    copies = []
    stage = []
    for part in range(3):
        copy = remote(a0[part].at[1 - core], r0[part], send.at[part, 0], recv.at[part, 0], twin)
        copy.start()
        stage.append([copy])
    for part in range(3):
        stage[part][0].wait_recv()
        a1[part][...] = (a0[part][core].astype(F32) + r0[part][...].astype(F32)).astype(BF)
        copies += stage[part]
        stage[part] = []
        axis = ORDERS[part][0]
        for d in range(3):
            to = (me[axis] + d + 1) % 4
            stage[part].append(
                remote(
                    a1[part].at[pl.ds(to * 16, 16)], r1[part].at[d],
                    send.at[part, 1 + d], recv.at[part, 1 + d], peers[axis][d],
                )
            )
            stage[part][-1].start()
    for level, (here, got, there, size) in enumerate(((a1, r1, a2, 16), (a2, r2, a3, 4))):
        for part in range(3):
            for copy in stage[part]:
                copy.wait_recv()
            copies += stage[part]
            stage[part] = []
            own = me[ORDERS[part][level]]
            total = here[part][pl.ds(own * size, size)].astype(F32)
            for d in range(3):
                total = total + got[part][d].astype(F32)
            there[part][...] = total.astype(BF)
            axis = ORDERS[part][level + 1]
            landing = (r2, r3)[level]
            for d in range(3):
                to = (me[axis] + d + 1) % 4
                step = size // 4
                sem = 4 + 3 * level + d
                stage[part].append(
                    remote(
                        there[part].at[pl.ds(to * step, step)], landing[part].at[d],
                        send.at[part, sem], recv.at[part, sem], peers[axis][d],
                    )
                )
                stage[part][-1].start()
    for part in range(3):
        for copy in stage[part]:
            copy.wait_recv()
        copies += stage[part]
        own = me[ORDERS[part][2]]
        total = a3[part][own].astype(F32)
        for d in range(3):
            total = total + r3[part][d, 0].astype(F32)
        out_ref[:, 128 * part : 128 * part + 128] = total * (1.0 / 256.0)
    for copy in copies:
        copy.wait_send()


def embedding(timestep_ids, channels):
    half_width = channels // 2
    frequency = jnp.exp(-math.log(10000.0) * jnp.arange(half_width, dtype=F32) / half_width)
    angles = timestep_ids.astype(F32)[:, None] * frequency[None, :]
    return jnp.concatenate([jnp.cos(angles), jnp.sin(angles)], axis=-1)


def vmem(count):
    return [pl.BlockSpec(memory_space=VMEM)] * count


def params(ident):
    return pltpu.CompilerParams(
        collective_id=ident, has_side_effects=True, vmem_limit_bytes=VLIM
    )


def shaped(*shape, dtype=BF):
    return jax.ShapeDtypeStruct(shape, dtype)


def halo_scratch():
    dma = pltpu.SemaphoreType.DMA
    return (
        [VMEM((24, BC, CH), BF)] * 4
        + [VMEM((16, BC, CH), BF)] * 8
        + [dma((2, 4)), dma((2, 4)), dma((2, 4)), dma((2, 4))]
    )


def on_device(
    latents,
    window_shift,
    timesteps,
    motion_gain,
    time_weight,
    qkv_weight,
    attn_out_weight,
    spatial_gain,
    conv_weight,
    proj_weight,
    out_cotangent,
):
    dma = pltpu.SemaphoreType.DMA
    smem = pl.BlockSpec(memory_space=pltpu.SMEM)
    lat = latents.reshape(FR, CELLS, CH)
    cot = out_cotangent.reshape(FR, CELLS, CH)
    mgain, sgain = motion_gain[None], spatial_gain[None]
    embedded = embedding(timesteps, CH)
    extra = jnp.dot(embedded, time_weight, precision=lax.Precision.HIGHEST)
    motion, normed, hwin, wp, wop, off = pl.pallas_call(
        motion_kernel,
        out_shape=(
            shaped(FR, CELLS, CH), shaped(FR, CELLS, CH), shaped(4, 16, BC, CH),
            shaped(CH, PADZ), shaped(PADQ, CH), shaped(1, PADZ, dtype=F32),
        ),
        in_specs=[smem] + vmem(6),
        out_specs=tuple(vmem(6)),
        scratch_shapes=[VMEM((PADQ, CH), F32)] + halo_scratch(),
        compiler_params=params(0),
        name="motion",
    )(window_shift, lat, mgain, sgain, extra, qkv_weight, attn_out_weight)
    plane = VMEM((FR, COLS, CH), BF)
    block_output, d_motion = pl.pallas_call(
        spatial_kernel,
        out_shape=(shaped(FR, CELLS, CH), shaped(FR, CELLS, CH, dtype=F32)),
        in_specs=vmem(4) + [pl.BlockSpec(memory_space=pl.ANY)] + vmem(1),
        out_specs=tuple(vmem(2)),
        scratch_shapes=[
            VMEM((3, 1024, HID), BF), VMEM((FR, 4, COLS, 1024), BF), plane, plane,
            VMEM((FR * CELLS, HID), F32), VMEM((FR * CELLS, HID), BF),
            plane, plane, plane, plane, VMEM((FR, 2, COLS, CH), F32),
            dma((18,)), dma((4,)), dma((4,)),
        ],
        compiler_params=params(1),
        name="spatial",
    )(normed, motion, cot, sgain, conv_weight, proj_weight)
    grad_input, *flats = pl.pallas_call(
        grad_kernel,
        out_shape=(shaped(FR, CELLS, CH, dtype=F32),) + (shaped(1608, 128, dtype=F32),) * 3,
        in_specs=[smem] + vmem(9),
        out_specs=tuple(vmem(4)),
        scratch_shapes=[
            VMEM((1024, 384), BF), VMEM((1024, PADQ), BF), VMEM((1024, CH), BF),
            VMEM((1024, PADZ), BF),
        ] + halo_scratch(),
        compiler_params=params(2),
        name="motion_grad",
    )(window_shift, lat, mgain, d_motion, hwin, wp, wop, off, extra, embedded)
    tile = (16, 128)
    total = pl.pallas_call(
        sum_kernel,
        out_shape=shaped(16, 384, dtype=F32),
        in_specs=vmem(3),
        out_specs=vmem(1)[0],
        scratch_shapes=[VMEM((2, 64) + tile, BF)] * 3
        + [VMEM((64,) + tile, BF)] * 6
        + [VMEM((3, 16) + tile, BF)] * 3
        + [VMEM((16,) + tile, BF)] * 3
        + [VMEM((3, 4) + tile, BF)] * 3
        + [VMEM((4,) + tile, BF)] * 3
        + [VMEM((3, 1) + tile, BF)] * 3
        + [dma((3, 10)), dma((3, 10))],
        compiler_params=params(3),
        name="weight_sums",
    )(*flats)
    odd = lax.axis_index("row") % 2
    grad_weights = lax.dynamic_slice_in_dim(total[:13, :CH].reshape(-1), 160 * odd, 4000)
    return (
        block_output.reshape(latents.shape),
        grad_input.reshape(latents.shape),
        grad_weights,
    )


def solution(mesh):
    placed = (
        P("tm", "row", None, None),
        P(),
        P("tm"),
        P(),
        P(),
        P(),
        P(),
        P(),
        P(),
        P(),
        P("tm", "row", None, None),
    )
    return jax.shard_map(
        on_device,
        mesh=mesh,
        in_specs=placed,
        out_specs=(P("tm", "row", None, None), P("tm", "row", None, None), P(("tm", "row"))),
        check_vma=False,
    )
```

```python
import math

import jax
import jax.numpy as jnp
from jax import lax
from jax.experimental import pallas as pl
from jax.experimental.pallas import tpu as pltpu
from jax.sharding import PartitionSpec as P

BF = jnp.bfloat16
F32 = jnp.float32
MESH = pl.DeviceIdType.MESH
VMEM = pltpu.VMEM

FR = 8
CELLS = 64
COLS = 32
CH = 320
HID = 1280
HEADS = 8
HD = 40
HP = 64
BLOCKS = 4
BC = CELLS // BLOCKS
PADQ = HEADS * HP
PADZ = 3 * PADQ
SCALE = 1.0 / math.sqrt(HD)
EXP2 = SCALE * math.log2(math.e)
EPS = 1e-06
VLIM = 56 * 1024 * 1024


def mm(a, b):
    return jnp.dot(a, b, preferred_element_type=F32)


def mm_nt(a, b):
    return lax.dot_general(a, b, (((1,), (1,)), ((), ())), preferred_element_type=F32)


def mm_tn(a, b):
    return lax.dot_general(a, b, (((0,), (0,)), ((), ())), preferred_element_type=F32)


def rms_scale(values):
    return lax.rsqrt(jnp.mean(values * values, axis=-1, keepdims=True) + EPS)


def rms_back(values, gain, cotangent):
    r = rms_scale(values)
    g = cotangent * gain
    return r * g - values * (r * r * r) * jnp.mean(g * values, axis=-1, keepdims=True)


def parts_of(row):
    first = row.astype(BF).astype(F32)
    rest = row - first
    second = rest.astype(BF).astype(F32)
    return first, second, rest - second


def stack_parts(row):
    a, b, c = parts_of(row)
    at = lax.broadcasted_iota(jnp.int32, (16, row.shape[1]), 0)
    return jnp.where(at == 0, a, jnp.where(at == 1, b, jnp.where(at == 2, c, 0.0))).astype(BF)


def outer(left, right):
    a, b, _ = parts_of(left)
    c, d, _ = parts_of(right)
    at = lax.broadcasted_iota(jnp.int32, (16, left.shape[1]), 0)
    lhs = jnp.where(at < 4, jnp.where(at % 2 == 0, a, b), 0.0).astype(BF)
    at = lax.broadcasted_iota(jnp.int32, (16, right.shape[1]), 0)
    rhs = jnp.where(at < 4, jnp.where(at < 2, c, d), 0.0).astype(BF)
    return mm_tn(lhs, rhs)


def greet(peers):
    barrier = pltpu.get_barrier_semaphore()
    for peer in peers:
        pl.semaphore_signal(barrier, inc=1, device_id=peer, device_id_type=MESH)
    pl.semaphore_wait(barrier, len(peers))


def remote(src, dst, send, recv, peer):
    return pltpu.make_async_remote_copy(
        src_ref=src, dst_ref=dst, send_sem=send, recv_sem=recv, device_id=peer, device_id_type=MESH
    )


def ring():
    at, count = lax.axis_index("tm"), lax.axis_size("tm")
    row = lax.axis_index("row")
    return ((at + count - 1) % count, row), ((at + 1) % count, row)


def pair_masks():
    lane = lax.broadcasted_iota(jnp.int32, (128, 128), 1)
    return lane < HP


def both_heads(x, first):
    zero = jnp.zeros_like(x)
    return jnp.concatenate([jnp.where(first, x, zero), jnp.where(first, zero, x)], axis=0)


def pair_probs(q, kst, same):
    s = mm_nt(q, kst)
    e = jnp.where(same, jnp.exp2(s * EXP2), 0.0)
    ea, eb = e[:, :128], e[:, 128:]
    return jnp.concatenate(
        [
            ea * (1.0 / jnp.sum(ea, axis=-1, keepdims=True)),
            eb * (1.0 / jnp.sum(eb, axis=-1, keepdims=True)),
        ],
        axis=1,
    )


def same_cell():
    row = lax.broadcasted_iota(jnp.int32, (128, 256), 0)
    lane = lax.broadcasted_iota(jnp.int32, (128, 256), 1)
    return row % 8 == lane % 8


def halo_copies(ext, send, recv, b, before, after):
    return (
        remote(ext.at[9:16], ext.at[1:8], send.at[0, b], recv.at[0, b], after),
        remote(ext.at[8:15], ext.at[16:23], send.at[1, b], recv.at[1, b], before),
    )


def return_copies(out, back, send, recv, b, before, after):
    return (
        remote(out.at[0:7], back.at[8:15], send.at[0, b], recv.at[0, b], before),
        remote(out.at[9:16], back.at[1:8], send.at[1, b], recv.at[1, b], after),
    )


def column_shifts(flat):
    count = flat.shape[0]
    col = lax.broadcasted_iota(jnp.int32, flat.shape, 0) % COLS
    left = jnp.where(col == 0, 0.0, pltpu.roll(flat, 1, 0))
    right = jnp.where(col == COLS - 1, 0.0, pltpu.roll(flat, count - 1, 0))
    return left, right


ORDERS = (("x", "y", "z"), ("y", "z", "x"), ("z", "x", "y"))


def place_of(tm, row):
    return {"y": tm // 8, "x": (row // 2) * 2 + (tm // 4) % 2, "z": tm % 4, "core": row % 2}


def device_at(at):
    return (at["y"] * 8 + (at["x"] % 2) * 4 + at["z"], (at["x"] // 2) * 2 + at["core"])


def cell_groups(block):
    wide = block.astype(F32)
    return [wide[:, 8 * g : 8 * g + 8].reshape(128, wide.shape[2]) for g in range(2)]


def from_groups(rows):
    return jnp.concatenate(
        [rows[128 * g : 128 * g + 128].reshape(16, 8, rows.shape[1]) for g in range(2)], axis=1
    )


def scratch_list():
    dma = pltpu.SemaphoreType.DMA
    plane = VMEM((FR, COLS, CH), BF)
    tile = (16, 128)
    return {
        "wo32": VMEM((PADQ, CH), F32),
        "wp": VMEM((CH, PADZ), BF),
        "wop": VMEM((PADQ, CH), BF),
        **{f"hext{b}": VMEM((24, BC, CH), BF) for b in range(4)},
        **{f"wout{b}": VMEM((16, BC, CH), BF) for b in range(4)},
        **{f"back{b}": VMEM((16, BC, CH), BF) for b in range(4)},
        **{f"cext{b}": VMEM((24, BC, CH), BF) for b in range(4)},
        **{f"dh{b}": VMEM((16, BC, CH), BF) for b in range(4)},
        **{f"dback{b}": VMEM((16, BC, CH), BF) for b in range(4)},
        "z": VMEM((1024, PADZ), BF),
        "hall": VMEM((1024, 384), BF),
        "mall": VMEM((1024, PADQ), BF),
        "call": VMEM((1024, CH), BF),
        "dz": VMEM((1024, PADZ), BF),
        "pt": VMEM((32, 256, 128), BF),
        "motion": VMEM((FR, CELLS, CH), BF),
        "normed": VMEM((FR, CELLS, CH), BF),
        "dmot": VMEM((FR, CELLS, CH), F32),
        "wbuf": VMEM((3, 1024, HID), BF),
        "x3": VMEM((FR, 4, COLS, 1024), BF),
        "top": plane,
        "bot": plane,
        "pre": VMEM((FR * CELLS, HID), F32),
        "dpre": VMEM((FR * CELLS, HID), BF),
        "gtop": plane,
        "gbot": plane,
        "stop": plane,
        "sbot": plane,
        "keep": VMEM((FR, 2, COLS, CH), F32),
        **{f"flat{j}": VMEM((1608, 128), F32) for j in range(3)},
        **{f"a0{j}": VMEM((2, 64) + tile, BF) for j in range(3)},
        **{f"r0{j}": VMEM((64,) + tile, BF) for j in range(3)},
        **{f"a1{j}": VMEM((64,) + tile, BF) for j in range(3)},
        **{f"r1{j}": VMEM((3, 16) + tile, BF) for j in range(3)},
        **{f"a2{j}": VMEM((16,) + tile, BF) for j in range(3)},
        **{f"r2{j}": VMEM((3, 4) + tile, BF) for j in range(3)},
        **{f"a3{j}": VMEM((4,) + tile, BF) for j in range(3)},
        **{f"r3{j}": VMEM((3, 1) + tile, BF) for j in range(3)},
        "wsem": dma((18,)),
        **{name: dma((2, 4)) for name in ("s1", "q1", "s2", "q2", "s3", "q3", "s4", "q4")},
        "srow": dma((4,)),
        "qrow": dma((4,)),
        "ssum": dma((3, 10)),
        "qsum": dma((3, 10)),
    }


def step_kernel(
    shift_ref, lat_ref, mgain_ref, sgain_ref, emb_ref, tw_ref, w_ref, wo_ref, conv_ref, projt_ref, cot_ref,
    out_ref, gin_ref, sum_ref, *rest,
):
    m = dict(zip(scratch_list(), rest))
    blocks = {name: [m[f"{name}{b}"] for b in range(4)] for name in ("hext", "wout", "back", "cext", "dh", "dback")}
    wp, wop, wbuf, x3, dpre = m["wp"], m["wop"], m["wbuf"], m["x3"], m["dpre"]
    tm, row = lax.axis_index("tm"), lax.axis_index("row")
    rows = lax.axis_size("row")
    before, after = ring()
    above, below = (tm, row - 1), (tm, row + 1)
    has_above, has_below = row > 0, row < rows - 1
    me = place_of(tm, row)
    twin = device_at({**me, "core": 1 - me["core"]})
    peers = {
        axis: [device_at({**me, axis: (me[axis] + d) % 4}) for d in (1, 2, 3)] for axis in "xyz"
    }
    shift = shift_ref[0]
    mgain, sgain = mgain_ref[...].reshape(1, CH), sgain_ref[...].reshape(1, CH)

    loads = []
    for dy in (1, 0, 2):
        for t in range(3):
            loads.append((conv_ref.at[3 * dy + t, 0:256, :], wbuf.at[dy, 256 * t : 256 * t + 256, :]))
            loads.append((conv_ref.at[3 * dy + t, 256:320, :], wbuf.at[dy, 768 + 64 * t : 832 + 64 * t, :]))
    loads = [pltpu.make_async_copy(a, c, m["wsem"].at[j]) for j, (a, c) in enumerate(loads)]
    for load in loads:
        load.start()

    for b in range(BLOCKS):
        x = lat_ref[:, BC * b : BC * b + BC, :].astype(F32)
        blocks["hext"][b][8:16] = (x * rms_scale(x) * mgain).astype(BF)
    greet(
        (before, after, (tm, (row + 1) % rows), (tm, (row + rows - 1) % rows), twin)
        + tuple(peers["x"] + peers["y"] + peers["z"])
    )
    sends = []

    def start(*copies):
        for copy in copies:
            copy.start()
        sends.extend(copies)
        return copies

    def halos(name, send, recv):
        return [
            start(*halo_copies(blocks[name][b], m[send], m[recv], b, before, after))
            for b in range(BLOCKS)
        ]

    def arrive(pair):
        for copy in pair:
            copy.wait_recv()

    ins = halos("hext", "s1", "q1")
    wp[...] = jnp.zeros_like(wp)
    for j in range(3 * HEADS):
        wp[:, HP * j : HP * j + HD] = w_ref[:, HD * j : HD * j + HD]
    m["wo32"][...] = jnp.zeros_like(m["wo32"])
    wo_f = wo_ref[...].astype(F32)
    for h in range(HEADS):
        m["wo32"][HP * h : HP * h + HD, :] = wo_f[HD * h : HD * h + HD]
    wop[...] = m["wo32"][...].astype(BF)
    emb = emb_ref[...]
    three = stack_parts(emb)
    extra = sum(mm(three, part.astype(BF)) for part in parts_of(tw_ref[...]))
    extra = jnp.sum(extra, axis=0, keepdims=True)
    off = jnp.sum(mm(stack_parts(extra), wp[...]), axis=0, keepdims=True)
    for dy in range(3):
        wbuf[dy, 960:1024, :] = jnp.zeros((64, HID), BF)
    first, same = pair_masks(), same_cell()
    same_t = (
        lax.broadcasted_iota(jnp.int32, (256, 128), 0) % 8
        == lax.broadcasted_iota(jnp.int32, (256, 128), 1) % 8
    )
    lane = lax.broadcasted_iota(jnp.int32, (256, 64), 1)
    ones = jnp.where(lane == 0, 1.0, 0.0).astype(BF)

    def z_pair(g, i, part):
        return m["z"][128 * g : 128 * g + 128, PADQ * part + 128 * i : PADQ * part + 128 * i + 128]

    outs = []
    for b in range(BLOCKS):
        arrive(ins[b])
        for g, found in enumerate(cell_groups(blocks["hext"][b][pl.ds(shift, 16)])):
            m["hall"][256 * b + 128 * g : 256 * b + 128 * g + 128, 0:CH] = found.astype(BF)
        m["hall"][256 * b : 256 * b + 256, CH:384] = ones
        m["z"][256 * b : 256 * b + 256, :] = (
            mm(m["hall"][256 * b : 256 * b + 256, 0:CH], wp[...]) + off
        ).astype(BF)
        for g in (2 * b, 2 * b + 1):
            for i in range(HEADS // 2):
                p = pair_probs(z_pair(g, i, 0), both_heads(z_pair(g, i, 1), first), same).astype(BF)
                m["mall"][128 * g : 128 * g + 128, 128 * i : 128 * i + 128] = mm(
                    p, both_heads(z_pair(g, i, 2), first)
                ).astype(BF)
        found = mm(m["mall"][256 * b : 256 * b + 256, :], wop[...])
        blocks["wout"][b][...] = from_groups(found).astype(BF)
        outs.append(
            start(*return_copies(blocks["wout"][b], blocks["back"][b], m["s2"], m["q2"], b, before, after))
        )

    def transposed_probs(b):
        for g in (2 * b, 2 * b + 1):
            for i in range(HEADS // 2):
                s = mm_nt(both_heads(z_pair(g, i, 1), first), z_pair(g, i, 0))
                e = jnp.where(same_t, jnp.exp2(s * EXP2), 0.0)
                ea, eb = e[:128], e[128:]
                ea = ea * (1.0 / jnp.sum(ea, axis=0, keepdims=True))
                eb = eb * (1.0 / jnp.sum(eb, axis=0, keepdims=True))
                m["pt"][4 * g + i, 0:128] = ea.astype(BF)
                m["pt"][4 * g + i, 128:256] = eb.astype(BF)

    transposed_probs(0)
    transposed_probs(1)

    up = remote(m["normed"].at[:, 0:32, :], m["bot"], m["srow"].at[0], m["qrow"].at[0], above)
    down = remote(m["normed"].at[:, 32:64, :], m["top"], m["srow"].at[1], m["qrow"].at[1], below)
    gup = remote(m["stop"], m["gbot"], m["srow"].at[2], m["qrow"].at[2], above)
    gdown = remote(m["sbot"], m["gtop"], m["srow"].at[3], m["qrow"].at[3], below)
    for b in range(BLOCKS):
        arrive(outs[b])
        x = lat_ref[:, BC * b : BC * b + BC, :].astype(F32)
        both = blocks["wout"][b][pl.ds(8 - shift, 8)].astype(F32)
        both = both + blocks["back"][b][pl.ds(8 - shift, 8)].astype(F32)
        moved = (x + 0.5 * both).astype(BF)
        m["motion"][:, BC * b : BC * b + BC, :] = moved
        moved = moved.astype(F32)
        m["normed"][:, BC * b : BC * b + BC, :] = (moved * rms_scale(moved) * sgain).astype(BF)
        if b == 1:
            pl.when(has_above)(lambda: up.start())
        if b == 3:
            pl.when(has_below)(lambda: down.start())

    def place(at, plane):
        flat = plane.astype(F32).reshape(FR * COLS, CH)
        left, right = column_shifts(flat)
        for t, values in enumerate((left, flat, right)):
            values = values.astype(BF).reshape(FR, COLS, CH)
            x3[:, at, :, 256 * t : 256 * t + 256] = values[:, :, :256]
            x3[:, at, :, 768 + 64 * t : 832 + 64 * t] = values[:, :, 256:]
        x3[:, at, :, 960:1024] = jnp.zeros((FR, COLS, 64), BF)

    place(1, m["normed"][:, 0:32, :])
    place(2, m["normed"][:, 32:64, :])

    def add_taps(dy, n):
        taps = x3[:, dy : dy + 2].reshape(FR * CELLS, 1024)
        return mm(taps, wbuf[dy, :, 256 * n : 256 * n + 256])

    for load in loads[:6]:
        load.wait()
    for n in range(5):
        m["pre"][:, 256 * n : 256 * n + 256] = add_taps(1, n)

    @pl.when(has_below)
    def _():
        remote(m["normed"].at[:, 0:32, :], m["bot"], m["srow"].at[0], m["qrow"].at[0], below).wait_recv()
        place(3, m["bot"][...])

    @pl.when(jnp.logical_not(has_below))
    def _():
        x3[:, 3] = jnp.zeros((FR, COLS, 1024), BF)

    @pl.when(has_above)
    def _():
        remote(m["normed"].at[:, 32:64, :], m["top"], m["srow"].at[1], m["qrow"].at[1], above).wait_recv()
        place(0, m["top"][...])

    @pl.when(jnp.logical_not(has_above))
    def _():
        x3[:, 0] = jnp.zeros((FR, COLS, 1024), BF)

    for load in loads[6:]:
        load.wait()
    cot = cot_ref[...].reshape(FR * CELLS, CH)
    total = m["motion"][...].astype(F32).reshape(FR * CELLS, CH)
    c0, c1 = math.sqrt(2.0 / math.pi), 0.044715
    for n in range(5):
        u = m["pre"][:, 256 * n : 256 * n + 256] + add_taps(0, n) + add_taps(2, n)
        proj = projt_ref[:, 256 * n : 256 * n + 256]
        dact = mm(cot, proj)
        sq = u * u
        th = jnp.tanh(c0 * u * (1.0 + c1 * sq))
        half = 0.5 + 0.5 * th
        act = u * half
        slope = half + 0.5 * u * (1.0 - th * th) * (c0 + (3.0 * c0 * c1) * sq)
        dpre[:, 256 * n : 256 * n + 256] = (slope * dact).astype(BF)
        total = total + mm_nt(act.astype(BF), proj)
    out_ref[...] = total.astype(BF).reshape(FR, CELLS, CH)

    def back_taps(dy):
        g = [mm_nt(dpre[...], wbuf[dy, 256 * j : 256 * j + 256, :]) for j in range(4)]
        col = lax.broadcasted_iota(jnp.int32, (FR * CELLS, 256), 0) % COLS
        count = FR * CELLS

        def from_right(x, c):
            return jnp.where(c == COLS - 1, 0.0, pltpu.roll(x, count - 1, 0))

        def from_left(x, c):
            return jnp.where(c == 0, 0.0, pltpu.roll(x, 1, 0))

        low = from_right(g[0], col) + g[1] + from_left(g[2], col)
        high = (
            from_right(g[3][:, :64], col[:, :64])
            + g[3][:, 64:128]
            + from_left(g[3][:, 128:192], col[:, :64])
        )
        return jnp.concatenate([low, high], axis=1).reshape(FR, 2, COLS, CH)

    keep = m["keep"]
    y = back_taps(0)
    m["stop"][...] = y[:, 0].astype(BF)
    pl.when(has_above)(lambda: gup.start())
    keep[:, 0] = y[:, 1]
    y = back_taps(2)
    m["sbot"][...] = y[:, 1].astype(BF)
    pl.when(has_below)(lambda: gdown.start())
    keep[:, 1] = y[:, 0]
    keep[...] = keep[...] + back_taps(1)

    def row_cotangent(r):
        cells = slice(32 * r, 32 * r + 32)
        d = cot_ref[:, cells, :].astype(F32) + rms_back(
            m["motion"][:, cells, :].astype(F32), sgain, keep[:, r]
        )
        m["dmot"][:, cells, :] = d
        d = (0.5 * d).astype(BF)
        for b in (2 * r, 2 * r + 1):
            blocks["cext"][b][8:16] = d[:, BC * (b - 2 * r) : BC * (b - 2 * r) + BC]

    @pl.when(has_above)
    def _():
        remote(m["sbot"], m["gtop"], m["srow"].at[3], m["qrow"].at[3], above).wait_recv()
        keep[:, 0] = keep[:, 0] + m["gtop"][...].astype(F32)

    row_cotangent(0)

    def send_halo(b):
        return start(*halo_copies(blocks["cext"][b], m["s3"], m["q3"], b, before, after))

    ins = [send_halo(0), send_halo(1)]

    @pl.when(has_below)
    def _():
        remote(m["stop"], m["gbot"], m["srow"].at[2], m["qrow"].at[2], below).wait_recv()
        keep[:, 1] = keep[:, 1] + m["gbot"][...].astype(F32)

    row_cotangent(1)
    ins += [send_halo(2), send_halo(3)]

    transposed_probs(2)
    transposed_probs(3)
    outs = []
    for b in range(BLOCKS):
        arrive(ins[b])
        for g, found in enumerate(cell_groups(blocks["cext"][b][pl.ds(shift, 16)])):
            m["call"][256 * b + 128 * g : 256 * b + 128 * g + 128, :] = found.astype(BF)
        dm = mm_nt(m["call"][256 * b : 256 * b + 256, :], wop[...]).astype(BF)
        for g in (2 * b, 2 * b + 1):
            at = slice(128 * g, 128 * g + 128)
            for i in range(HEADS // 2):
                lanes = slice(128 * i, 128 * i + 128)
                q = z_pair(g, i, 0)
                kst = both_heads(z_pair(g, i, 1), first)
                vst = both_heads(z_pair(g, i, 2), first)
                dmi = dm[128 * (g - 2 * b) : 128 * (g - 2 * b) + 128, lanes]
                pt = m["pt"][4 * g + i]
                pf = pt.astype(F32)
                dp = mm_nt(vst, dmi)
                t = pf * dp
                ds = jnp.concatenate(
                    [
                        (t[:128] - pf[:128] * jnp.sum(t[:128], axis=0, keepdims=True)) * SCALE,
                        (t[128:] - pf[128:] * jnp.sum(t[128:], axis=0, keepdims=True)) * SCALE,
                    ],
                    axis=0,
                ).astype(BF)
                m["dz"][at, lanes] = mm_tn(ds, kst).astype(BF)
                dk = mm(ds, q)
                m["dz"][at, PADQ + 128 * i : PADQ + 128 * i + 128] = jnp.where(
                    first, dk[:128], dk[128:]
                ).astype(BF)
                dv = mm(pt, dmi)
                m["dz"][at, 2 * PADQ + 128 * i : 2 * PADQ + 128 * i + 128] = jnp.where(
                    first, dv[:128], dv[128:]
                ).astype(BF)
        found = mm_nt(m["dz"][256 * b : 256 * b + 256, :], wp[...])
        blocks["dh"][b][...] = from_groups(found).astype(BF)
        outs.append(
            start(*return_copies(blocks["dh"][b], blocks["dback"][b], m["s4"], m["q4"], b, before, after))
        )

    flats = [m[f"flat{j}"] for j in range(3)]
    dw = mm_tn(m["hall"][...], m["dz"][...])
    doff = dw[CH : CH + 1]
    dwq = dw[:CH] + outer(extra, doff)
    at = lax.broadcasted_iota(jnp.int32, (PADQ, 384), 0)
    lane = lax.broadcasted_iota(jnp.int32, (PADQ, 384), 1)
    pick = (lane == HD * (at // HP) + at % HP) & (at % HP < HD)
    pick = jnp.where(pick, 1.0, 0.0).astype(BF)
    for part in range(3):
        block = mm(dwq[:, PADQ * part : PADQ * part + PADQ].astype(BF), pick)
        for j in range(3):
            flats[j][pl.ds(part, CH, stride=3), :] = block[:, 128 * j : 128 * j + 128]
    zeros = jnp.zeros((CH, 64), F32)
    dwo = mm_tn(m["mall"][...], m["call"][...])
    dext = jnp.sum(mm_nt(stack_parts(doff), wp[...]), axis=0, keepdims=True)
    dtime = outer(emb, dext)
    for j in range(3):
        wide = 128 if j < 2 else 64
        for h in range(HEADS):
            flats[j][960 + HD * h : 960 + HD * h + HD, 0:wide] = dwo[
                HP * h : HP * h + HD, 128 * j : 128 * j + wide
            ]
        flats[j][1280:1600, 0:wide] = dtime[:, 128 * j : 128 * j + wide]
        flats[j][1600:1608, :] = jnp.zeros((8, 128), F32)
    flats[2][960:1280, 64:128] = zeros
    flats[2][1280:1600, 64:128] = zeros

    a = [[m[f"a{k}{j}"] for j in range(3)] for k in range(4)]
    r = [[m[f"r{k}{j}"] for j in range(3)] for k in range(4)]

    def gather(j, carry):
        to = place_of(j // 2, (j % 2) * 2)
        for c in range(2):
            for part, order in enumerate(ORDERS):
                index = (to[order[0]] * 4 + to[order[1]]) * 4 + to[order[2]]
                a[0][part][c, index] = flats[part][pl.ds(25 * j + 12 * c, 16), :].astype(BF)
        return carry

    lax.fori_loop(0, 64, gather, 0)
    core = me["core"]
    stage = [
        start(
            remote(a[0][p].at[1 - core], r[0][p], m["ssum"].at[p, 0], m["qsum"].at[p, 0], twin)
        )
        for p in range(3)
    ]

    def fan_out(part, level):
        axis = ORDERS[part][level - 1]
        step = 16 >> (2 * (level - 1))
        copies = []
        for d in range(3):
            to = (me[axis] + d + 1) % 4
            sem = 3 * level - 2 + d
            copies.append(
                remote(
                    a[level][part].at[pl.ds(to * step, step)], r[level][part].at[d],
                    m["ssum"].at[part, sem], m["qsum"].at[part, sem], peers[axis][d],
                )
            )
        return start(*copies)

    def gathered(part, level):
        step = 16 >> (2 * (level - 1))
        own = me[ORDERS[part][level - 1]]
        total = a[level][part][pl.ds(own * step, step)].astype(F32)
        for d in range(3):
            total = total + r[level][part][d].astype(F32)
        return total

    def finish(b):
        arrive(outs[b])
        d_hidden = blocks["dh"][b][pl.ds(8 - shift, 8)].astype(F32)
        d_hidden = d_hidden + blocks["dback"][b][pl.ds(8 - shift, 8)].astype(F32)
        x = lat_ref[:, BC * b : BC * b + BC, :].astype(F32)
        gin_ref[:, BC * b : BC * b + BC, :] = m["dmot"][:, BC * b : BC * b + BC, :] + rms_back(
            x, mgain, d_hidden
        )

    finish(0)
    for p in range(3):
        arrive(stage[p])
        a[1][p][...] = (a[0][p][core].astype(F32) + r[0][p][...].astype(F32)).astype(BF)
        stage[p] = fan_out(p, 1)
    finish(1)
    finish(2)
    finish(3)
    for level in (2, 3):
        for p in range(3):
            arrive(stage[p])
            a[level][p][...] = gathered(p, level - 1).astype(BF)
            stage[p] = fan_out(p, level)
    for p in range(3):
        arrive(stage[p])
        sum_ref[:, 128 * p : 128 * p + 128] = gathered(p, 3)[0] * (1.0 / 256.0)
    for copy in sends:
        copy.wait_send()

    @pl.when(has_above)
    def _():
        up.wait_send()
        gup.wait_send()

    @pl.when(has_below)
    def _():
        down.wait_send()
        gdown.wait_send()


def embedding(timestep_ids, channels):
    half_width = channels // 2
    frequency = jnp.exp(-math.log(10000.0) * jnp.arange(half_width, dtype=F32) / half_width)
    angles = timestep_ids.astype(F32)[:, None] * frequency[None, :]
    return jnp.concatenate([jnp.cos(angles), jnp.sin(angles)], axis=-1)


def vmem(count):
    return [pl.BlockSpec(memory_space=VMEM)] * count


def params(ident):
    return pltpu.CompilerParams(
        collective_id=ident, has_side_effects=True, vmem_limit_bytes=VLIM
    )


def shaped(*shape, dtype=BF):
    return jax.ShapeDtypeStruct(shape, dtype)


def on_device(
    latents,
    window_shift,
    timesteps,
    motion_gain,
    time_weight,
    qkv_weight,
    attn_out_weight,
    spatial_gain,
    conv_weight,
    proj_weight,
    out_cotangent,
):
    smem = pl.BlockSpec(memory_space=pltpu.SMEM)
    block_output, grad_input, total = pl.pallas_call(
        step_kernel,
        out_shape=(
            shaped(FR, CELLS, CH), shaped(FR, CELLS, CH, dtype=F32), shaped(16, 384, dtype=F32),
        ),
        in_specs=[smem] + vmem(7) + [pl.BlockSpec(memory_space=pl.ANY)] + vmem(2),
        out_specs=tuple(vmem(3)),
        scratch_shapes=list(scratch_list().values()),
        compiler_params=params(0),
        name="step",
    )(
        window_shift, latents.reshape(FR, CELLS, CH), motion_gain, spatial_gain,
        embedding(timesteps, CH), time_weight, qkv_weight, attn_out_weight, conv_weight,
        proj_weight.T, out_cotangent.reshape(FR, CELLS, CH),
    )
    odd = lax.axis_index("row") % 2
    grad_weights = lax.dynamic_slice_in_dim(total[:13, :CH].reshape(-1), 160 * odd, 4000)
    return (
        block_output.reshape(latents.shape),
        grad_input.reshape(latents.shape),
        grad_weights,
    )


def solution(mesh):
    placed = (
        P("tm", "row", None, None),
        P(),
        P("tm"),
        P(),
        P(),
        P(),
        P(),
        P(),
        P(),
        P(),
        P("tm", "row", None, None),
    )
    return jax.shard_map(
        on_device,
        mesh=mesh,
        in_specs=placed,
        out_specs=(P("tm", "row", None, None), P("tm", "row", None, None), P(("tm", "row"))),
        check_vma=False,
    )
```

```python
import math

import jax
import jax.numpy as jnp
from jax import lax
from jax.experimental import pallas as pl
from jax.experimental.pallas import tpu as pltpu
from jax.sharding import PartitionSpec as P

BF = jnp.bfloat16
F32 = jnp.float32
MESH = pl.DeviceIdType.MESH
VMEM = pltpu.VMEM

FR = 8
CELLS = 64
COLS = 32
CH = 320
HID = 1280
HEADS = 8
HD = 40
HP = 64
BLOCKS = 4
BC = CELLS // BLOCKS
PADQ = HEADS * HP
PADZ = 3 * PADQ
SCALE = 1.0 / math.sqrt(HD)
EXP2 = SCALE * math.log2(math.e)
EPS = 1e-06
VLIM = 60 * 1024 * 1024


def mm(a, b):
    return jnp.dot(a, b, preferred_element_type=F32)


def mm_nt(a, b):
    return lax.dot_general(a, b, (((1,), (1,)), ((), ())), preferred_element_type=F32)


def mm_tn(a, b):
    return lax.dot_general(a, b, (((0,), (0,)), ((), ())), preferred_element_type=F32)


def rms_scale(values):
    return lax.rsqrt(jnp.mean(values * values, axis=-1, keepdims=True) + EPS)


def rms_back(values, gain, cotangent):
    r = rms_scale(values)
    g = cotangent * gain
    return r * g - values * (r * r * r) * jnp.mean(g * values, axis=-1, keepdims=True)


def parts_of(row):
    first = row.astype(BF).astype(F32)
    rest = row - first
    second = rest.astype(BF).astype(F32)
    return first, second, rest - second


def stack_parts(row):
    a, b, c = parts_of(row)
    at = lax.broadcasted_iota(jnp.int32, (16, row.shape[1]), 0)
    return jnp.where(at == 0, a, jnp.where(at == 1, b, jnp.where(at == 2, c, 0.0))).astype(BF)


def outer(left, right):
    a, b, _ = parts_of(left)
    c, d, _ = parts_of(right)
    at = lax.broadcasted_iota(jnp.int32, (16, left.shape[1]), 0)
    lhs = jnp.where(at < 4, jnp.where(at % 2 == 0, a, b), 0.0).astype(BF)
    at = lax.broadcasted_iota(jnp.int32, (16, right.shape[1]), 0)
    rhs = jnp.where(at < 4, jnp.where(at < 2, c, d), 0.0).astype(BF)
    return mm_tn(lhs, rhs)


def greet(barrier, peers):
    for peer in peers:
        pl.semaphore_signal(barrier, inc=1, device_id=peer, device_id_type=MESH)


def remote(src, dst, send, recv, peer):
    return pltpu.make_async_remote_copy(
        src_ref=src, dst_ref=dst, send_sem=send, recv_sem=recv, device_id=peer, device_id_type=MESH
    )


def ring():
    at, count = lax.axis_index("tm"), lax.axis_size("tm")
    row = lax.axis_index("row")
    return ((at + count - 1) % count, row), ((at + 1) % count, row)


def pair_masks():
    lane = lax.broadcasted_iota(jnp.int32, (128, 128), 1)
    return lane < HP


def both_heads(x, first):
    zero = jnp.zeros_like(x)
    return jnp.concatenate([jnp.where(first, x, zero), jnp.where(first, zero, x)], axis=0)


def pair_probs(q, kst, same):
    s = mm_nt(q, kst)
    e = jnp.where(same, jnp.exp2(s * EXP2), 0.0)
    ea, eb = e[:, :128], e[:, 128:]
    return jnp.concatenate(
        [
            ea * (1.0 / jnp.sum(ea, axis=-1, keepdims=True)),
            eb * (1.0 / jnp.sum(eb, axis=-1, keepdims=True)),
        ],
        axis=1,
    )


def same_cell():
    row = lax.broadcasted_iota(jnp.int32, (128, 256), 0)
    lane = lax.broadcasted_iota(jnp.int32, (128, 256), 1)
    return row % 8 == lane % 8


def halo_copies(ext, send, recv, b, before, after):
    return (
        remote(ext.at[9:16], ext.at[1:8], send.at[0, b], recv.at[0, b], after),
        remote(ext.at[8:15], ext.at[16:23], send.at[1, b], recv.at[1, b], before),
    )


def return_copies(out, back, send, recv, b, before, after):
    return (
        remote(out.at[0:7], back.at[8:15], send.at[0, b], recv.at[0, b], before),
        remote(out.at[9:16], back.at[1:8], send.at[1, b], recv.at[1, b], after),
    )


def column_shifts(flat):
    count = flat.shape[0]
    col = lax.broadcasted_iota(jnp.int32, flat.shape, 0) % COLS
    left = jnp.where(col == 0, 0.0, pltpu.roll(flat, 1, 0))
    right = jnp.where(col == COLS - 1, 0.0, pltpu.roll(flat, count - 1, 0))
    return left, right


ORDERS = (("x", "y", "z"), ("y", "z", "x"), ("z", "x", "y"))


def place_of(tm, row):
    return {"y": tm // 8, "x": (row // 2) * 2 + (tm // 4) % 2, "z": tm % 4, "core": row % 2}


def device_at(at):
    return (at["y"] * 8 + (at["x"] % 2) * 4 + at["z"], (at["x"] // 2) * 2 + at["core"])


def cell_groups(block):
    wide = block.astype(F32)
    return [wide[:, 8 * g : 8 * g + 8].reshape(128, wide.shape[2]) for g in range(2)]


def from_groups(rows):
    return jnp.concatenate(
        [rows[128 * g : 128 * g + 128].reshape(16, 8, rows.shape[1]) for g in range(2)], axis=1
    )


def flat_line(sums, line, half):
    lane = lax.broadcasted_iota(jnp.int32, (8, 128), 1)
    even = [sums[p, pl.ds(0, 8, stride=2), :] for p in range(3)]
    odd = [sums[p, pl.ds(1, 8, stride=2), :] for p in range(3)]
    turned = [pltpu.roll(x, 64, 1) for x in odd]
    low = lane < 64
    pieces = (
        even[0],
        even[1],
        jnp.where(low, even[2], turned[0]),
        jnp.where(low, turned[0], turned[1]),
        jnp.where(low, turned[1], turned[2]),
    )
    line[40:48, :] = jnp.zeros((8, 128), F32)
    for j, piece in enumerate(pieces):
        line[pl.ds(j, 8, stride=5), :] = piece
    lane = lax.broadcasted_iota(jnp.int32, (32, 128), 1)
    later = jnp.where(
        lane < 96, pltpu.roll(line[1:33, :], 96, 1), pltpu.roll(line[2:34, :], 96, 1)
    )
    return jnp.where(half, later, line[0:32, :])


def copy_kernel(out_in, gin_in, line_in, out_ref, gin_ref, line_ref, sems):
    copies = [
        pltpu.make_async_copy(out_in, out_ref, sems.at[0]),
        pltpu.make_async_copy(gin_in, gin_ref, sems.at[1]),
    ]
    for copy in copies:
        copy.start()
    for j in range(31):
        line_ref[128 * j : 128 * j + 128] = line_in[j]
    line_ref[3968:4000] = line_in[31, 0:32]
    for copy in copies:
        copy.wait()


def scratch_list():
    dma = pltpu.SemaphoreType.DMA
    plane = VMEM((FR, COLS, CH), BF)
    tile = (16, 128)
    return {
        "wo32": VMEM((PADQ, CH), F32),
        "wp": VMEM((CH, PADZ), BF),
        "wop": VMEM((PADQ, CH), BF),
        **{f"hext{b}": VMEM((24, BC, CH), BF) for b in range(4)},
        **{f"wout{b}": VMEM((16, BC, CH), BF) for b in range(4)},
        **{f"back{b}": VMEM((16, BC, CH), BF) for b in range(4)},
        **{f"cext{b}": VMEM((24, BC, CH), BF) for b in range(4)},
        **{f"dh{b}": VMEM((16, BC, CH), BF) for b in range(4)},
        **{f"dback{b}": VMEM((16, BC, CH), BF) for b in range(4)},
        "z": VMEM((1024, PADZ), BF),
        "hall": VMEM((1024, 384), BF),
        "mall": VMEM((1024, PADQ), BF),
        "call": VMEM((1024, CH), BF),
        "dz": VMEM((1024, PADZ), BF),
        "pt": VMEM((32, 256, 128), BF),
        "motion": VMEM((FR, CELLS, CH), BF),
        "normed": VMEM((FR, CELLS, CH), BF),
        "dmot": VMEM((FR, CELLS, CH), F32),
        "wbuf": VMEM((3, 1024, HID), BF),
        "x3": VMEM((FR, 4, COLS, 1024), BF),
        "top": plane,
        "bot": plane,
        "pre": VMEM((FR * CELLS, HID), F32),
        "dpre": VMEM((FR * CELLS, HID), BF),
        "gtop": plane,
        "gbot": plane,
        "stop": plane,
        "sbot": plane,
        "keep": VMEM((FR, 2, COLS, CH), F32),
        **{f"flat{j}": VMEM((1608, 128), F32) for j in range(3)},
        **{f"a0{j}": VMEM((2, 64) + tile, BF) for j in range(3)},
        **{f"r0{j}": VMEM((64,) + tile, BF) for j in range(3)},
        **{f"a1{j}": VMEM((64,) + tile, BF) for j in range(3)},
        **{f"r1{j}": VMEM((3, 16) + tile, BF) for j in range(3)},
        **{f"a2{j}": VMEM((16,) + tile, BF) for j in range(3)},
        **{f"r2{j}": VMEM((3, 4) + tile, BF) for j in range(3)},
        **{f"a3{j}": VMEM((4,) + tile, BF) for j in range(3)},
        **{f"r3{j}": VMEM((3, 1) + tile, BF) for j in range(3)},
        "dact": VMEM((FR * CELLS, HID), F32),
        "hallt": VMEM((384, 1024), BF),
        "mallt": VMEM((PADQ, 1024), BF),
        "pick": VMEM((PADQ, 384), BF),
        "tw": VMEM((CH, CH), F32),
        "w": VMEM((CH, 3 * CH), BF),
        "wo": VMEM((CH, CH), BF),
        "projt": VMEM((CH, HID), BF),
        "cot": VMEM((FR, CELLS, CH), BF),
        "line": VMEM((48, 128), F32),
        "sums": VMEM((3, 16, 128), F32),
        "osem": dma((5,)),
        "wsem": dma((18,)),
        **{name: dma((2, 4)) for name in ("s1", "q1", "s2", "q2", "s3", "q3", "s4", "q4")},
        "srow": dma((4,)),
        "qrow": dma((4,)),
        "ssum": dma((3, 10)),
        "qsum": dma((3, 10)),
    }


def step_kernel(
    shift_ref, lat_ref, mgain_ref, sgain_ref, emb_ref, tw_hbm, w_hbm, wo_hbm, conv_ref, projt_hbm, cot_hbm,
    out_ref, gin_ref, sum_ref, *rest,
):
    m = dict(zip(scratch_list(), rest))
    blocks = {name: [m[f"{name}{b}"] for b in range(4)] for name in ("hext", "wout", "back", "cext", "dh", "dback")}
    wp, wop, wbuf, x3, dpre = m["wp"], m["wop"], m["wbuf"], m["x3"], m["dpre"]
    tm, row = lax.axis_index("tm"), lax.axis_index("row")
    rows = lax.axis_size("row")
    before, after = ring()
    above, below = (tm, row - 1), (tm, row + 1)
    has_above, has_below = row > 0, row < rows - 1
    me = place_of(tm, row)
    twin = device_at({**me, "core": 1 - me["core"]})
    peers = {
        axis: [device_at({**me, axis: (me[axis] + d) % 4}) for d in (1, 2, 3)] for axis in "xyz"
    }
    shift = shift_ref[0]
    mgain, sgain = mgain_ref[...].reshape(1, CH), sgain_ref[...].reshape(1, CH)

    barrier = pltpu.get_barrier_semaphore()
    neighbours = (before, after, (tm, (row + 1) % rows), (tm, (row + rows - 1) % rows), twin)
    neighbours += tuple(peers["x"] + peers["y"] + peers["z"])
    greet(barrier, neighbours)
    small = {}
    for j, (name, ref) in enumerate(
        (("w", w_hbm), ("wo", wo_hbm), ("tw", tw_hbm), ("cot", cot_hbm), ("projt", projt_hbm))
    ):
        small[name] = pltpu.make_async_copy(ref, m[name], m["osem"].at[j])
        small[name].start()
    w_ref, wo_ref, tw_ref, cot_ref, projt_ref = (m[k] for k in ("w", "wo", "tw", "cot", "projt"))
    loads = []
    for dy in (1, 0, 2):
        for t in range(3):
            loads.append((conv_ref.at[3 * dy + t, 0:256, :], wbuf.at[dy, 256 * t : 256 * t + 256, :]))
            loads.append((conv_ref.at[3 * dy + t, 256:320, :], wbuf.at[dy, 768 + 64 * t : 832 + 64 * t, :]))
    loads = [pltpu.make_async_copy(a, c, m["wsem"].at[j]) for j, (a, c) in enumerate(loads)]
    for load in loads:
        load.start()

    for b in range(BLOCKS):
        x = lat_ref[:, BC * b : BC * b + BC, :].astype(F32)
        blocks["hext"][b][8:16] = (x * rms_scale(x) * mgain).astype(BF)
    pl.semaphore_wait(barrier, len(neighbours))
    sends = []

    def start(*copies):
        for copy in copies:
            copy.start()
        sends.extend(copies)
        return copies

    def halos(name, send, recv):
        return [
            start(*halo_copies(blocks[name][b], m[send], m[recv], b, before, after))
            for b in range(BLOCKS)
        ]

    def arrive(pair):
        for copy in pair:
            copy.wait_recv()

    ins = halos("hext", "s1", "q1")
    small["w"].wait()
    wp[...] = jnp.zeros_like(wp)
    for j in range(3 * HEADS):
        wp[:, HP * j : HP * j + HD] = w_ref[:, HD * j : HD * j + HD]
    m["wo32"][...] = jnp.zeros_like(m["wo32"])
    small["wo"].wait()
    wo_f = wo_ref[...].astype(F32)
    for h in range(HEADS):
        m["wo32"][HP * h : HP * h + HD, :] = wo_f[HD * h : HD * h + HD]
    wop[...] = m["wo32"][...].astype(BF)
    small["tw"].wait()
    emb = emb_ref[...]
    three = stack_parts(emb)
    extra = sum(mm(three, part.astype(BF)) for part in parts_of(tw_ref[...]))
    extra = jnp.sum(extra, axis=0, keepdims=True)
    off = jnp.sum(mm(stack_parts(extra), wp[...]), axis=0, keepdims=True)
    for dy in range(3):
        wbuf[dy, 960:1024, :] = jnp.zeros((64, HID), BF)
    first, same = pair_masks(), same_cell()
    same_t = (
        lax.broadcasted_iota(jnp.int32, (256, 128), 0) % 8
        == lax.broadcasted_iota(jnp.int32, (256, 128), 1) % 8
    )
    at = lax.broadcasted_iota(jnp.int32, (PADQ, 384), 0)
    lane = lax.broadcasted_iota(jnp.int32, (PADQ, 384), 1)
    pick = (lane == HD * (at // HP) + at % HP) & (at % HP < HD)
    m["pick"][...] = jnp.where(pick, 1.0, 0.0).astype(BF)
    lane = lax.broadcasted_iota(jnp.int32, (256, 64), 1)
    ones = jnp.where(lane == 0, 1.0, 0.0).astype(BF)

    def z_pair(g, i, part):
        return m["z"][128 * g : 128 * g + 128, PADQ * part + 128 * i : PADQ * part + 128 * i + 128]

    outs = []
    for b in range(BLOCKS):
        arrive(ins[b])
        for g, found in enumerate(cell_groups(blocks["hext"][b][pl.ds(shift, 16)])):
            m["hall"][256 * b + 128 * g : 256 * b + 128 * g + 128, 0:CH] = found.astype(BF)
        m["hall"][256 * b : 256 * b + 256, CH:384] = ones
        m["z"][256 * b : 256 * b + 256, :] = (
            mm(m["hall"][256 * b : 256 * b + 256, 0:CH], wp[...]) + off
        ).astype(BF)
        for g in (2 * b, 2 * b + 1):
            for i in range(HEADS // 2):
                p = pair_probs(z_pair(g, i, 0), both_heads(z_pair(g, i, 1), first), same).astype(BF)
                m["mall"][128 * g : 128 * g + 128, 128 * i : 128 * i + 128] = mm(
                    p, both_heads(z_pair(g, i, 2), first)
                ).astype(BF)
        found = mm(m["mall"][256 * b : 256 * b + 256, :], wop[...])
        blocks["wout"][b][...] = from_groups(found).astype(BF)
        outs.append(
            start(*return_copies(blocks["wout"][b], blocks["back"][b], m["s2"], m["q2"], b, before, after))
        )

    def transposed_probs(b):
        for g in (2 * b, 2 * b + 1):
            for i in range(HEADS // 2):
                s = mm_nt(both_heads(z_pair(g, i, 1), first), z_pair(g, i, 0))
                e = jnp.where(same_t, jnp.exp2(s * EXP2), 0.0)
                ea, eb = e[:128], e[128:]
                ea = ea * (1.0 / jnp.sum(ea, axis=0, keepdims=True))
                eb = eb * (1.0 / jnp.sum(eb, axis=0, keepdims=True))
                m["pt"][4 * g + i, 0:128] = ea.astype(BF)
                m["pt"][4 * g + i, 128:256] = eb.astype(BF)

    small["cot"].wait()
    small["projt"].wait()
    cot = cot_ref[...].reshape(FR * CELLS, CH)
    for n in range(5):
        m["dact"][:, 256 * n : 256 * n + 256] = mm(cot, projt_ref[:, 256 * n : 256 * n + 256])
    m["hallt"][...] = m["hall"][...].T
    m["mallt"][...] = m["mall"][...].T
    transposed_probs(2)
    transposed_probs(3)

    up = remote(m["normed"].at[:, 0:32, :], m["bot"], m["srow"].at[0], m["qrow"].at[0], above)
    down = remote(m["normed"].at[:, 32:64, :], m["top"], m["srow"].at[1], m["qrow"].at[1], below)
    gup = remote(m["stop"], m["gbot"], m["srow"].at[2], m["qrow"].at[2], above)
    gdown = remote(m["sbot"], m["gtop"], m["srow"].at[3], m["qrow"].at[3], below)
    for b in range(BLOCKS):
        arrive(outs[b])
        x = lat_ref[:, BC * b : BC * b + BC, :].astype(F32)
        both = blocks["wout"][b][pl.ds(8 - shift, 8)].astype(F32)
        both = both + blocks["back"][b][pl.ds(8 - shift, 8)].astype(F32)
        moved = (x + 0.5 * both).astype(BF)
        m["motion"][:, BC * b : BC * b + BC, :] = moved
        moved = moved.astype(F32)
        m["normed"][:, BC * b : BC * b + BC, :] = (moved * rms_scale(moved) * sgain).astype(BF)
        if b == 1:
            pl.when(has_above)(lambda: up.start())
        if b == 3:
            pl.when(has_below)(lambda: down.start())

    def place(at, plane):
        flat = plane.astype(F32).reshape(FR * COLS, CH)
        left, right = column_shifts(flat)
        for t, values in enumerate((left, flat, right)):
            values = values.astype(BF).reshape(FR, COLS, CH)
            x3[:, at, :, 256 * t : 256 * t + 256] = values[:, :, :256]
            x3[:, at, :, 768 + 64 * t : 832 + 64 * t] = values[:, :, 256:]
        x3[:, at, :, 960:1024] = jnp.zeros((FR, COLS, 64), BF)

    place(1, m["normed"][:, 0:32, :])
    place(2, m["normed"][:, 32:64, :])

    def add_taps(dy, n):
        taps = x3[:, dy : dy + 2].reshape(FR * CELLS, 1024)
        return mm(taps, wbuf[dy, :, 256 * n : 256 * n + 256])

    for load in loads[:6]:
        load.wait()
    for n in range(5):
        m["pre"][:, 256 * n : 256 * n + 256] = add_taps(1, n)

    @pl.when(has_below)
    def _():
        remote(m["normed"].at[:, 0:32, :], m["bot"], m["srow"].at[0], m["qrow"].at[0], below).wait_recv()
        place(3, m["bot"][...])

    @pl.when(jnp.logical_not(has_below))
    def _():
        x3[:, 3] = jnp.zeros((FR, COLS, 1024), BF)

    @pl.when(has_above)
    def _():
        remote(m["normed"].at[:, 32:64, :], m["top"], m["srow"].at[1], m["qrow"].at[1], above).wait_recv()
        place(0, m["top"][...])

    @pl.when(jnp.logical_not(has_above))
    def _():
        x3[:, 0] = jnp.zeros((FR, COLS, 1024), BF)

    for load in loads[6:]:
        load.wait()
    total = m["motion"][...].astype(F32).reshape(FR * CELLS, CH)
    c0, c1 = math.sqrt(2.0 / math.pi), 0.044715
    for n in range(5):
        u = m["pre"][:, 256 * n : 256 * n + 256] + add_taps(0, n) + add_taps(2, n)
        proj = projt_ref[:, 256 * n : 256 * n + 256]
        dact = m["dact"][:, 256 * n : 256 * n + 256]
        sq = u * u
        th = jnp.tanh(c0 * u * (1.0 + c1 * sq))
        half = 0.5 + 0.5 * th
        act = u * half
        slope = half + 0.5 * u * (1.0 - th * th) * (c0 + (3.0 * c0 * c1) * sq)
        dpre[:, 256 * n : 256 * n + 256] = (slope * dact).astype(BF)
        total = total + mm_nt(act.astype(BF), proj)
    out_ref[...] = total.astype(BF).reshape(FR, CELLS, CH)

    def back_taps(dy):
        g = [mm_nt(dpre[...], wbuf[dy, 256 * j : 256 * j + 256, :]) for j in range(4)]
        col = lax.broadcasted_iota(jnp.int32, (FR * CELLS, 256), 0) % COLS
        count = FR * CELLS

        def from_right(x, c):
            return jnp.where(c == COLS - 1, 0.0, pltpu.roll(x, count - 1, 0))

        def from_left(x, c):
            return jnp.where(c == 0, 0.0, pltpu.roll(x, 1, 0))

        low = from_right(g[0], col) + g[1] + from_left(g[2], col)
        high = (
            from_right(g[3][:, :64], col[:, :64])
            + g[3][:, 64:128]
            + from_left(g[3][:, 128:192], col[:, :64])
        )
        return jnp.concatenate([low, high], axis=1).reshape(FR, 2, COLS, CH)

    keep = m["keep"]
    y = back_taps(0)
    m["stop"][...] = y[:, 0].astype(BF)
    pl.when(has_above)(lambda: gup.start())
    keep[:, 0] = y[:, 1]
    y = back_taps(2)
    m["sbot"][...] = y[:, 1].astype(BF)
    pl.when(has_below)(lambda: gdown.start())
    keep[:, 1] = y[:, 0]
    keep[...] = keep[...] + back_taps(1)

    def row_cotangent(r):
        cells = slice(32 * r, 32 * r + 32)
        d = cot_ref[:, cells, :].astype(F32) + rms_back(
            m["motion"][:, cells, :].astype(F32), sgain, keep[:, r]
        )
        m["dmot"][:, cells, :] = d
        d = (0.5 * d).astype(BF)
        for b in (2 * r, 2 * r + 1):
            blocks["cext"][b][8:16] = d[:, BC * (b - 2 * r) : BC * (b - 2 * r) + BC]

    def send_halo(b):
        return start(*halo_copies(blocks["cext"][b], m["s3"], m["q3"], b, before, after))

    @pl.when(has_below)
    def _():
        remote(m["stop"], m["gbot"], m["srow"].at[2], m["qrow"].at[2], below).wait_recv()
        keep[:, 1] = keep[:, 1] + m["gbot"][...].astype(F32)

    row_cotangent(1)
    ins = {b: send_halo(b) for b in (2, 3)}

    @pl.when(has_above)
    def _():
        remote(m["sbot"], m["gtop"], m["srow"].at[3], m["qrow"].at[3], above).wait_recv()
        keep[:, 0] = keep[:, 0] + m["gtop"][...].astype(F32)

    row_cotangent(0)
    ins.update({b: send_halo(b) for b in (0, 1)})

    transposed_probs(0)
    transposed_probs(1)
    outs = {}

    def give_back(b):
        found = mm_nt(m["dz"][256 * b : 256 * b + 256, :], wp[...])
        blocks["dh"][b][...] = from_groups(found).astype(BF)
        outs[b] = start(
            *return_copies(blocks["dh"][b], blocks["dback"][b], m["s4"], m["q4"], b, before, after)
        )

    for b in (2, 3, 0, 1):
        arrive(ins[b])
        for g, found in enumerate(cell_groups(blocks["cext"][b][pl.ds(shift, 16)])):
            m["call"][256 * b + 128 * g : 256 * b + 128 * g + 128, :] = found.astype(BF)
        dm = mm_nt(m["call"][256 * b : 256 * b + 256, :], wop[...]).astype(BF)
        for g in (2 * b, 2 * b + 1):
            at = slice(128 * g, 128 * g + 128)
            for i in range(HEADS // 2):
                lanes = slice(128 * i, 128 * i + 128)
                q = z_pair(g, i, 0)
                kst = both_heads(z_pair(g, i, 1), first)
                vst = both_heads(z_pair(g, i, 2), first)
                dmi = dm[128 * (g - 2 * b) : 128 * (g - 2 * b) + 128, lanes]
                pt = m["pt"][4 * g + i]
                pf = pt.astype(F32)
                dp = mm_nt(vst, dmi)
                t = pf * dp
                ds = jnp.concatenate(
                    [
                        (t[:128] - pf[:128] * jnp.sum(t[:128], axis=0, keepdims=True)) * SCALE,
                        (t[128:] - pf[128:] * jnp.sum(t[128:], axis=0, keepdims=True)) * SCALE,
                    ],
                    axis=0,
                ).astype(BF)
                m["dz"][at, lanes] = mm_tn(ds, kst).astype(BF)
                dk = mm(ds, q)
                m["dz"][at, PADQ + 128 * i : PADQ + 128 * i + 128] = jnp.where(
                    first, dk[:128], dk[128:]
                ).astype(BF)
                dv = mm(pt, dmi)
                m["dz"][at, 2 * PADQ + 128 * i : 2 * PADQ + 128 * i + 128] = jnp.where(
                    first, dv[:128], dv[128:]
                ).astype(BF)
        if b > 1:
            give_back(b)

    flats = [m[f"flat{j}"] for j in range(3)]
    dw = mm(m["hallt"][...], m["dz"][...])
    doff = dw[CH : CH + 1]
    dwq = dw[:CH] + outer(extra, doff)
    for part in range(3):
        block = mm(dwq[:, PADQ * part : PADQ * part + PADQ].astype(BF), m["pick"][...])
        for j in range(3):
            flats[j][pl.ds(part, CH, stride=3), :] = block[:, 128 * j : 128 * j + 128]
    zeros = jnp.zeros((CH, 64), F32)
    dwo = mm(m["mallt"][...], m["call"][...])
    dext = jnp.sum(mm_nt(stack_parts(doff), wp[...]), axis=0, keepdims=True)
    dtime = outer(emb, dext)
    for j in range(3):
        wide = 128 if j < 2 else 64
        for h in range(HEADS):
            flats[j][960 + HD * h : 960 + HD * h + HD, 0:wide] = dwo[
                HP * h : HP * h + HD, 128 * j : 128 * j + wide
            ]
        flats[j][1280:1600, 0:wide] = dtime[:, 128 * j : 128 * j + wide]
        flats[j][1600:1608, :] = jnp.zeros((8, 128), F32)
    flats[2][960:1280, 64:128] = zeros
    flats[2][1280:1600, 64:128] = zeros

    a = [[m[f"a{k}{j}"] for j in range(3)] for k in range(4)]
    r = [[m[f"r{k}{j}"] for j in range(3)] for k in range(4)]

    def gather(j, carry):
        to = place_of(j // 2, (j % 2) * 2)
        for c in range(2):
            for part, order in enumerate(ORDERS):
                index = (to[order[0]] * 4 + to[order[1]]) * 4 + to[order[2]]
                a[0][part][c, index] = flats[part][pl.ds(25 * j + 12 * c, 16), :].astype(BF)
        return carry

    lax.fori_loop(0, 64, gather, 0)
    core = me["core"]
    stage = [
        start(
            remote(a[0][p].at[1 - core], r[0][p], m["ssum"].at[p, 0], m["qsum"].at[p, 0], twin)
        )
        for p in range(3)
    ]

    def fan_out(part, level):
        axis = ORDERS[part][level - 1]
        step = 16 >> (2 * (level - 1))
        copies = []
        for d in range(3):
            to = (me[axis] + d + 1) % 4
            sem = 3 * level - 2 + d
            copies.append(
                remote(
                    a[level][part].at[pl.ds(to * step, step)], r[level][part].at[d],
                    m["ssum"].at[part, sem], m["qsum"].at[part, sem], peers[axis][d],
                )
            )
        return start(*copies)

    def gathered(part, level):
        step = 16 >> (2 * (level - 1))
        own = me[ORDERS[part][level - 1]]
        total = a[level][part][pl.ds(own * step, step)].astype(F32)
        for d in range(3):
            total = total + r[level][part][d].astype(F32)
        return total

    def finish(b):
        arrive(outs[b])
        d_hidden = blocks["dh"][b][pl.ds(8 - shift, 8)].astype(F32)
        d_hidden = d_hidden + blocks["dback"][b][pl.ds(8 - shift, 8)].astype(F32)
        x = lat_ref[:, BC * b : BC * b + BC, :].astype(F32)
        gin_ref[:, BC * b : BC * b + BC, :] = m["dmot"][:, BC * b : BC * b + BC, :] + rms_back(
            x, mgain, d_hidden
        )

    give_back(0)
    give_back(1)
    for p in range(3):
        arrive(stage[p])
        a[1][p][...] = (a[0][p][core].astype(F32) + r[0][p][...].astype(F32)).astype(BF)
        stage[p] = fan_out(p, 1)
    for b in (2, 3, 0, 1):
        finish(b)
    for level in (2, 3):
        for p in range(3):
            arrive(stage[p])
            a[level][p][...] = gathered(p, level - 1).astype(BF)
            stage[p] = fan_out(p, level)
    for p in range(3):
        arrive(stage[p])
        m["sums"][p] = gathered(p, 3)[0] * (1.0 / 256.0)
    sum_ref[...] = flat_line(m["sums"], m["line"], core == 1)
    for copy in sends:
        copy.wait_send()

    @pl.when(has_above)
    def _():
        up.wait_send()
        gup.wait_send()

    @pl.when(has_below)
    def _():
        down.wait_send()
        gdown.wait_send()


def embedding(timestep_ids, channels):
    half_width = channels // 2
    frequency = jnp.exp(-math.log(10000.0) * jnp.arange(half_width, dtype=F32) / half_width)
    angles = timestep_ids.astype(F32)[:, None] * frequency[None, :]
    return jnp.concatenate([jnp.cos(angles), jnp.sin(angles)], axis=-1)


def vmem(count):
    return [pl.BlockSpec(memory_space=VMEM)] * count


def anywhere(count):
    return [pl.BlockSpec(memory_space=pl.ANY)] * count


def params(ident):
    return pltpu.CompilerParams(
        collective_id=ident, has_side_effects=True, vmem_limit_bytes=VLIM
    )


def shaped(*shape, dtype=BF):
    return jax.ShapeDtypeStruct(shape, dtype)


def on_device(
    latents,
    window_shift,
    timesteps,
    motion_gain,
    time_weight,
    qkv_weight,
    attn_out_weight,
    spatial_gain,
    conv_weight,
    proj_weight,
    out_cotangent,
):
    smem = pl.BlockSpec(memory_space=pltpu.SMEM)
    block_output, grad_input, total = pl.pallas_call(
        step_kernel,
        out_shape=(
            VMEM((FR, CELLS, CH), BF), VMEM((FR, CELLS, CH), F32), VMEM((32, 128), F32),
        ),
        in_specs=[smem] + vmem(4) + anywhere(6),
        out_specs=tuple(vmem(3)),
        scratch_shapes=list(scratch_list().values()),
        compiler_params=params(0),
        name="step",
    )(
        window_shift, latents.reshape(FR, CELLS, CH), motion_gain, spatial_gain,
        embedding(timesteps, CH), time_weight, qkv_weight, attn_out_weight, conv_weight,
        proj_weight.T, out_cotangent.reshape(FR, CELLS, CH),
    )
    block_output, grad_input, grad_weights = pl.pallas_call(
        copy_kernel,
        out_shape=(
            shaped(FR, CELLS, CH), shaped(FR, CELLS, CH, dtype=F32), shaped(4000, dtype=F32),
        ),
        in_specs=vmem(3),
        out_specs=tuple(anywhere(2) + vmem(1)),
        scratch_shapes=[pltpu.SemaphoreType.DMA((2,))],
        compiler_params=pltpu.CompilerParams(vmem_limit_bytes=4 * 1024 * 1024),
        name="results",
    )(*(pltpu.with_memory_space_constraint(x, VMEM) for x in (block_output, grad_input, total)))
    return (
        block_output.reshape(latents.shape),
        grad_input.reshape(latents.shape),
        grad_weights,
    )


def solution(mesh):
    placed = (
        P("tm", "row", None, None),
        P(),
        P("tm"),
        P(),
        P(),
        P(),
        P(),
        P(),
        P(),
        P(),
        P("tm", "row", None, None),
    )
    return jax.shard_map(
        on_device,
        mesh=mesh,
        in_specs=placed,
        out_specs=(P("tm", "row", None, None), P("tm", "row", None, None), P(("tm", "row"))),
        check_vma=False,
    )
```

```python
import math

import jax
import jax.numpy as jnp
from jax import lax
from jax.experimental import pallas as pl
from jax.experimental.pallas import tpu as pltpu
from jax.sharding import PartitionSpec as P

BF = jnp.bfloat16
F32 = jnp.float32
MESH = pl.DeviceIdType.MESH
VMEM = pltpu.VMEM

FR = 8
CELLS = 64
COLS = 32
CH = 320
HID = 1280
HEADS = 8
HD = 40
HP = 64
BLOCKS = 4
HALF = BLOCKS // 2
BC = CELLS // BLOCKS
BG = BC // 8
BR = 16 * BC
PADQ = HEADS * HP
PADZ = 3 * PADQ
SCALE = 1.0 / math.sqrt(HD)
EXP2 = SCALE * math.log2(math.e)
EPS = 1e-06
VLIM = 60 * 1024 * 1024


def mm(a, b):
    return jnp.dot(a, b, preferred_element_type=F32)


def mm_nt(a, b):
    return lax.dot_general(a, b, (((1,), (1,)), ((), ())), preferred_element_type=F32)


def mm_tn(a, b):
    return lax.dot_general(a, b, (((0,), (0,)), ((), ())), preferred_element_type=F32)


def rms_scale(values):
    return lax.rsqrt(jnp.mean(values * values, axis=-1, keepdims=True) + EPS)


def rms_back(values, gain, cotangent):
    r = rms_scale(values)
    g = cotangent * gain
    return r * g - values * (r * r * r) * jnp.mean(g * values, axis=-1, keepdims=True)


def parts_of(row):
    first = row.astype(BF).astype(F32)
    rest = row - first
    second = rest.astype(BF).astype(F32)
    return first, second, rest - second


def stack_parts(row):
    a, b, c = parts_of(row)
    at = lax.broadcasted_iota(jnp.int32, (16, row.shape[1]), 0)
    return jnp.where(at == 0, a, jnp.where(at == 1, b, jnp.where(at == 2, c, 0.0))).astype(BF)


def outer(left, right):
    a, b, _ = parts_of(left)
    c, d, _ = parts_of(right)
    at = lax.broadcasted_iota(jnp.int32, (16, left.shape[1]), 0)
    lhs = jnp.where(at < 4, jnp.where(at % 2 == 0, a, b), 0.0).astype(BF)
    at = lax.broadcasted_iota(jnp.int32, (16, right.shape[1]), 0)
    rhs = jnp.where(at < 4, jnp.where(at < 2, c, d), 0.0).astype(BF)
    return mm_tn(lhs, rhs)


def greet(barrier, peers):
    for peer in peers:
        pl.semaphore_signal(barrier, inc=1, device_id=peer, device_id_type=MESH)


def remote(src, dst, send, recv, peer):
    return pltpu.make_async_remote_copy(
        src_ref=src, dst_ref=dst, send_sem=send, recv_sem=recv, device_id=peer, device_id_type=MESH
    )


def ring():
    at, count = lax.axis_index("tm"), lax.axis_size("tm")
    row = lax.axis_index("row")
    return ((at + count - 1) % count, row), ((at + 1) % count, row)


def pair_masks():
    lane = lax.broadcasted_iota(jnp.int32, (128, 128), 1)
    return lane < HP


def both_heads(x, first):
    zero = jnp.zeros_like(x)
    return jnp.concatenate([jnp.where(first, x, zero), jnp.where(first, zero, x)], axis=0)


def pair_probs(q, kst, same):
    s = mm_nt(q, kst)
    e = jnp.where(same, jnp.exp2(s * EXP2), 0.0)
    ea, eb = e[:, :128], e[:, 128:]
    return jnp.concatenate(
        [
            ea * (1.0 / jnp.sum(ea, axis=-1, keepdims=True)),
            eb * (1.0 / jnp.sum(eb, axis=-1, keepdims=True)),
        ],
        axis=1,
    )


def same_cell():
    row = lax.broadcasted_iota(jnp.int32, (128, 256), 0)
    lane = lax.broadcasted_iota(jnp.int32, (128, 256), 1)
    return row % 8 == lane % 8


def halo_copies(ext, send, recv, b, before, after):
    return (
        remote(ext.at[9:16], ext.at[1:8], send.at[0, b], recv.at[0, b], after),
        remote(ext.at[8:15], ext.at[16:23], send.at[1, b], recv.at[1, b], before),
    )


def return_copies(out, back, send, recv, b, before, after):
    return (
        remote(out.at[0:7], back.at[8:15], send.at[0, b], recv.at[0, b], before),
        remote(out.at[9:16], back.at[1:8], send.at[1, b], recv.at[1, b], after),
    )


def column_shifts(flat):
    count = flat.shape[0]
    col = lax.broadcasted_iota(jnp.int32, flat.shape, 0) % COLS
    left = jnp.where(col == 0, 0.0, pltpu.roll(flat, 1, 0))
    right = jnp.where(col == COLS - 1, 0.0, pltpu.roll(flat, count - 1, 0))
    return left, right


ORDERS = (("x", "y", "z"), ("y", "z", "x"), ("z", "x", "y"))


def place_of(tm, row):
    return {"y": tm // 8, "x": (row // 2) * 2 + (tm // 4) % 2, "z": tm % 4, "core": row % 2}


def device_at(at):
    return (at["y"] * 8 + (at["x"] % 2) * 4 + at["z"], (at["x"] // 2) * 2 + at["core"])


def cell_groups(block):
    wide = block.astype(F32)
    return [wide[:, 8 * g : 8 * g + 8].reshape(128, wide.shape[2]) for g in range(BG)]


def from_groups(rows):
    return jnp.concatenate(
        [rows[128 * g : 128 * g + 128].reshape(16, 8, rows.shape[1]) for g in range(BG)], axis=1
    )


def flat_line(sums, line, half):
    lane = lax.broadcasted_iota(jnp.int32, (8, 128), 1)
    even = [sums[p, pl.ds(0, 8, stride=2), :] for p in range(3)]
    odd = [sums[p, pl.ds(1, 8, stride=2), :] for p in range(3)]
    turned = [pltpu.roll(x, 64, 1) for x in odd]
    low = lane < 64
    pieces = (
        even[0],
        even[1],
        jnp.where(low, even[2], turned[0]),
        jnp.where(low, turned[0], turned[1]),
        jnp.where(low, turned[1], turned[2]),
    )
    line[40:48, :] = jnp.zeros((8, 128), F32)
    for j, piece in enumerate(pieces):
        line[pl.ds(j, 8, stride=5), :] = piece
    lane = lax.broadcasted_iota(jnp.int32, (32, 128), 1)
    later = jnp.where(
        lane < 96, pltpu.roll(line[1:33, :], 96, 1), pltpu.roll(line[2:34, :], 96, 1)
    )
    return jnp.where(half, later, line[0:32, :])


def copy_kernel(out_in, gin_in, line_in, out_ref, gin_ref, line_ref, sems):
    copies = [
        pltpu.make_async_copy(out_in, out_ref, sems.at[0]),
        pltpu.make_async_copy(gin_in, gin_ref, sems.at[1]),
    ]
    for copy in copies:
        copy.start()
    for j in range(31):
        line_ref[128 * j : 128 * j + 128] = line_in[j]
    line_ref[3968:4000] = line_in[31, 0:32]
    for copy in copies:
        copy.wait()


def scratch_list():
    dma = pltpu.SemaphoreType.DMA
    plane = VMEM((FR, COLS, CH), BF)
    tile = (16, 128)
    return {
        "wo32": VMEM((PADQ, CH), F32),
        "wp": VMEM((CH, PADZ), BF),
        "wop": VMEM((PADQ, CH), BF),
        **{f"hext{b}": VMEM((24, BC, CH), BF) for b in range(BLOCKS)},
        **{f"wout{b}": VMEM((16, BC, CH), BF) for b in range(BLOCKS)},
        **{f"back{b}": VMEM((16, BC, CH), BF) for b in range(BLOCKS)},
        **{f"cext{b}": VMEM((24, BC, CH), BF) for b in range(BLOCKS)},
        **{f"dh{b}": VMEM((16, BC, CH), BF) for b in range(BLOCKS)},
        **{f"dback{b}": VMEM((16, BC, CH), BF) for b in range(BLOCKS)},
        "z": VMEM((1024, PADZ), BF),
        "hall": VMEM((1024, 384), BF),
        "mall": VMEM((1024, PADQ), BF),
        "call": VMEM((1024, CH), BF),
        "dz": VMEM((1024, PADZ), BF),
        "pt": VMEM((32, 256, 128), BF),
        "motion": VMEM((FR, CELLS, CH), BF),
        "normed": VMEM((FR, CELLS, CH), BF),
        "dmot": VMEM((FR, CELLS, CH), F32),
        "wbuf": VMEM((3, 1024, HID), BF),
        "x3": VMEM((FR, 4, COLS, 1024), BF),
        "top": plane,
        "bot": plane,
        "pre": VMEM((FR * CELLS, HID), F32),
        "dpre": VMEM((FR * CELLS, HID), BF),
        "gtop": plane,
        "gbot": plane,
        "stop": plane,
        "sbot": plane,
        "keep": VMEM((FR, 2, COLS, CH), F32),
        **{f"flat{j}": VMEM((1608, 128), F32) for j in range(3)},
        **{f"a0{j}": VMEM((2, 64) + tile, BF) for j in range(3)},
        **{f"r0{j}": VMEM((64,) + tile, BF) for j in range(3)},
        **{f"a1{j}": VMEM((64,) + tile, BF) for j in range(3)},
        **{f"r1{j}": VMEM((3, 16) + tile, BF) for j in range(3)},
        **{f"a2{j}": VMEM((16,) + tile, BF) for j in range(3)},
        **{f"r2{j}": VMEM((3, 4) + tile, BF) for j in range(3)},
        **{f"a3{j}": VMEM((4,) + tile, BF) for j in range(3)},
        **{f"r3{j}": VMEM((3, 1) + tile, BF) for j in range(3)},
        "act": VMEM((FR * CELLS, HID), BF),
        "dact": VMEM((FR * CELLS, HID), F32),
        "hallt": VMEM((384, 1024), BF),
        "mallt": VMEM((PADQ, 1024), BF),
        "pick": VMEM((PADQ, 384), BF),
        "tw": VMEM((CH, CH), F32),
        "w": VMEM((CH, 3 * CH), BF),
        "wo": VMEM((CH, CH), BF),
        "projt": VMEM((CH, HID), BF),
        "cot": VMEM((FR, CELLS, CH), BF),
        "line": VMEM((48, 128), F32),
        "sums": VMEM((3, 16, 128), F32),
        "osem": dma((5,)),
        "wsem": dma((18,)),
        **{name: dma((2, BLOCKS)) for name in ("s1", "q1", "s2", "q2", "s3", "q3", "s4", "q4")},
        "srow": dma((4,)),
        "qrow": dma((4,)),
        "ssum": dma((3, 10)),
        "qsum": dma((3, 10)),
    }


def step_kernel(
    shift_ref, lat_ref, mgain_ref, sgain_ref, emb_ref, tw_hbm, w_hbm, wo_hbm, conv_ref, projt_hbm, cot_hbm,
    out_ref, gin_ref, sum_ref, *rest,
):
    m = dict(zip(scratch_list(), rest))
    blocks = {name: [m[f"{name}{b}"] for b in range(BLOCKS)] for name in ("hext", "wout", "back", "cext", "dh", "dback")}
    wp, wop, wbuf, x3, dpre = m["wp"], m["wop"], m["wbuf"], m["x3"], m["dpre"]
    tm, row = lax.axis_index("tm"), lax.axis_index("row")
    rows = lax.axis_size("row")
    before, after = ring()
    above, below = (tm, row - 1), (tm, row + 1)
    has_above, has_below = row > 0, row < rows - 1
    me = place_of(tm, row)
    twin = device_at({**me, "core": 1 - me["core"]})
    peers = {
        axis: [device_at({**me, axis: (me[axis] + d) % 4}) for d in (1, 2, 3)] for axis in "xyz"
    }
    shift = shift_ref[0]
    mgain, sgain = mgain_ref[...].reshape(1, CH), sgain_ref[...].reshape(1, CH)

    barrier = pltpu.get_barrier_semaphore()
    neighbours = (before, after, (tm, (row + 1) % rows), (tm, (row + rows - 1) % rows), twin)
    neighbours += tuple(peers["x"] + peers["y"] + peers["z"])
    greet(barrier, neighbours)
    small = {}
    for j, (name, ref) in enumerate(
        (("w", w_hbm), ("wo", wo_hbm), ("tw", tw_hbm), ("cot", cot_hbm), ("projt", projt_hbm))
    ):
        small[name] = pltpu.make_async_copy(ref, m[name], m["osem"].at[j])
        small[name].start()
    w_ref, wo_ref, tw_ref, cot_ref, projt_ref = (m[k] for k in ("w", "wo", "tw", "cot", "projt"))
    loads = []
    for dy in (1, 0, 2):
        for t in range(3):
            loads.append((conv_ref.at[3 * dy + t, 0:256, :], wbuf.at[dy, 256 * t : 256 * t + 256, :]))
            loads.append((conv_ref.at[3 * dy + t, 256:320, :], wbuf.at[dy, 768 + 64 * t : 832 + 64 * t, :]))
    loads = [pltpu.make_async_copy(a, c, m["wsem"].at[j]) for j, (a, c) in enumerate(loads)]
    for load in loads:
        load.start()

    for b in range(BLOCKS):
        x = lat_ref[:, BC * b : BC * b + BC, :].astype(F32)
        blocks["hext"][b][8:16] = (x * rms_scale(x) * mgain).astype(BF)
    pl.semaphore_wait(barrier, len(neighbours))
    sends = []

    def start(*copies):
        for copy in copies:
            copy.start()
        sends.extend(copies)
        return copies

    def halos(name, send, recv):
        return [
            start(*halo_copies(blocks[name][b], m[send], m[recv], b, before, after))
            for b in range(BLOCKS)
        ]

    def arrive(pair):
        for copy in pair:
            copy.wait_recv()

    ins = halos("hext", "s1", "q1")
    small["w"].wait()
    wp[...] = jnp.zeros_like(wp)
    for j in range(3 * HEADS):
        wp[:, HP * j : HP * j + HD] = w_ref[:, HD * j : HD * j + HD]
    m["wo32"][...] = jnp.zeros_like(m["wo32"])
    small["wo"].wait()
    wo_f = wo_ref[...].astype(F32)
    for h in range(HEADS):
        m["wo32"][HP * h : HP * h + HD, :] = wo_f[HD * h : HD * h + HD]
    wop[...] = m["wo32"][...].astype(BF)
    small["tw"].wait()
    emb = emb_ref[...]
    three = stack_parts(emb)
    extra = sum(mm(three, part.astype(BF)) for part in parts_of(tw_ref[...]))
    extra = jnp.sum(extra, axis=0, keepdims=True)
    off = jnp.sum(mm(stack_parts(extra), wp[...]), axis=0, keepdims=True)
    for dy in range(3):
        wbuf[dy, 960:1024, :] = jnp.zeros((64, HID), BF)
    first, same = pair_masks(), same_cell()
    same_t = (
        lax.broadcasted_iota(jnp.int32, (256, 128), 0) % 8
        == lax.broadcasted_iota(jnp.int32, (256, 128), 1) % 8
    )
    at = lax.broadcasted_iota(jnp.int32, (PADQ, 384), 0)
    lane = lax.broadcasted_iota(jnp.int32, (PADQ, 384), 1)
    pick = (lane == HD * (at // HP) + at % HP) & (at % HP < HD)
    m["pick"][...] = jnp.where(pick, 1.0, 0.0).astype(BF)
    lane = lax.broadcasted_iota(jnp.int32, (BR, 64), 1)
    ones = jnp.where(lane == 0, 1.0, 0.0).astype(BF)

    def z_pair(g, i, part):
        return m["z"][128 * g : 128 * g + 128, PADQ * part + 128 * i : PADQ * part + 128 * i + 128]

    small["cot"].wait()
    small["projt"].wait()
    cot = cot_ref[...].reshape(FR * CELLS, CH)
    for n in range(5):
        m["dact"][:, 256 * n : 256 * n + 256] = mm(cot, projt_ref[:, 256 * n : 256 * n + 256])
    outs = []
    for b in range(BLOCKS):
        arrive(ins[b])
        for g, found in enumerate(cell_groups(blocks["hext"][b][pl.ds(shift, 16)])):
            m["hall"][BR * b + 128 * g : BR * b + 128 * g + 128, 0:CH] = found.astype(BF)
        m["hall"][BR * b : BR * b + BR, CH:384] = ones
        m["z"][BR * b : BR * b + BR, :] = (
            mm(m["hall"][BR * b : BR * b + BR, 0:CH], wp[...]) + off
        ).astype(BF)
        for g in range(BG * b, BG * b + BG):
            for i in range(HEADS // 2):
                p = pair_probs(z_pair(g, i, 0), both_heads(z_pair(g, i, 1), first), same).astype(BF)
                m["mall"][128 * g : 128 * g + 128, 128 * i : 128 * i + 128] = mm(
                    p, both_heads(z_pair(g, i, 2), first)
                ).astype(BF)
        found = mm(m["mall"][BR * b : BR * b + BR, :], wop[...])
        blocks["wout"][b][...] = from_groups(found).astype(BF)
        outs.append(
            start(*return_copies(blocks["wout"][b], blocks["back"][b], m["s2"], m["q2"], b, before, after))
        )

    def transposed_probs(b):
        for g in range(BG * b, BG * b + BG):
            for i in range(HEADS // 2):
                s = mm_nt(both_heads(z_pair(g, i, 1), first), z_pair(g, i, 0))
                e = jnp.where(same_t, jnp.exp2(s * EXP2), 0.0)
                ea, eb = e[:128], e[128:]
                ea = ea * (1.0 / jnp.sum(ea, axis=0, keepdims=True))
                eb = eb * (1.0 / jnp.sum(eb, axis=0, keepdims=True))
                m["pt"][4 * g + i, 0:128] = ea.astype(BF)
                m["pt"][4 * g + i, 128:256] = eb.astype(BF)

    m["hallt"][...] = m["hall"][...].T
    m["mallt"][...] = m["mall"][...].T
    for b in range(HALF, BLOCKS):
        transposed_probs(b)

    up = remote(m["normed"].at[:, 0:32, :], m["bot"], m["srow"].at[0], m["qrow"].at[0], above)
    down = remote(m["normed"].at[:, 32:64, :], m["top"], m["srow"].at[1], m["qrow"].at[1], below)
    gup = remote(m["stop"], m["gbot"], m["srow"].at[2], m["qrow"].at[2], above)
    gdown = remote(m["sbot"], m["gtop"], m["srow"].at[3], m["qrow"].at[3], below)
    def place(at, plane):
        flat = plane.astype(F32).reshape(FR * COLS, CH)
        left, right = column_shifts(flat)
        for t, values in enumerate((left, flat, right)):
            values = values.astype(BF).reshape(FR, COLS, CH)
            x3[:, at, :, 256 * t : 256 * t + 256] = values[:, :, :256]
            x3[:, at, :, 768 + 64 * t : 832 + 64 * t] = values[:, :, 256:]
        x3[:, at, :, 960:1024] = jnp.zeros((FR, COLS, 64), BF)

    for b in range(BLOCKS):
        arrive(outs[b])
        x = lat_ref[:, BC * b : BC * b + BC, :].astype(F32)
        both = blocks["wout"][b][pl.ds(8 - shift, 8)].astype(F32)
        both = both + blocks["back"][b][pl.ds(8 - shift, 8)].astype(F32)
        moved = (x + 0.5 * both).astype(BF)
        m["motion"][:, BC * b : BC * b + BC, :] = moved
        moved = moved.astype(F32)
        m["normed"][:, BC * b : BC * b + BC, :] = (moved * rms_scale(moved) * sgain).astype(BF)
        if b == BLOCKS // 2 - 1:
            pl.when(has_above)(lambda: up.start())
            place(1, m["normed"][:, 0:32, :])
        if b == BLOCKS - 1:
            pl.when(has_below)(lambda: down.start())

    place(2, m["normed"][:, 32:64, :])

    def add_taps(dy, n):
        taps = x3[:, dy : dy + 2].reshape(FR * CELLS, 1024)
        return mm(taps, wbuf[dy, :, 256 * n : 256 * n + 256])

    for load in loads[:6]:
        load.wait()
    for n in range(5):
        m["pre"][:, 256 * n : 256 * n + 256] = add_taps(1, n)

    @pl.when(has_below)
    def _():
        remote(m["normed"].at[:, 0:32, :], m["bot"], m["srow"].at[0], m["qrow"].at[0], below).wait_recv()
        place(3, m["bot"][...])

    @pl.when(jnp.logical_not(has_below))
    def _():
        x3[:, 3] = jnp.zeros((FR, COLS, 1024), BF)

    @pl.when(has_above)
    def _():
        remote(m["normed"].at[:, 32:64, :], m["top"], m["srow"].at[1], m["qrow"].at[1], above).wait_recv()
        place(0, m["top"][...])

    @pl.when(jnp.logical_not(has_above))
    def _():
        x3[:, 0] = jnp.zeros((FR, COLS, 1024), BF)

    for load in loads[6:]:
        load.wait()
    c0, c1 = math.sqrt(2.0 / math.pi), 0.044715
    for n in range(5):
        u = m["pre"][:, 256 * n : 256 * n + 256] + add_taps(0, n) + add_taps(2, n)
        dact = m["dact"][:, 256 * n : 256 * n + 256]
        sq = u * u
        th = jnp.tanh(c0 * u * (1.0 + c1 * sq))
        half = 0.5 + 0.5 * th
        act = u * half
        slope = half + 0.5 * u * (1.0 - th * th) * (c0 + (3.0 * c0 * c1) * sq)
        dpre[:, 256 * n : 256 * n + 256] = (slope * dact).astype(BF)
        m["act"][:, 256 * n : 256 * n + 256] = act.astype(BF)

    def back_taps(dy):
        g = [mm_nt(dpre[...], wbuf[dy, 256 * j : 256 * j + 256, :]) for j in range(4)]
        col = lax.broadcasted_iota(jnp.int32, (FR * CELLS, 256), 0) % COLS
        count = FR * CELLS

        def from_right(x, c):
            return jnp.where(c == COLS - 1, 0.0, pltpu.roll(x, count - 1, 0))

        def from_left(x, c):
            return jnp.where(c == 0, 0.0, pltpu.roll(x, 1, 0))

        low = from_right(g[0], col) + g[1] + from_left(g[2], col)
        high = (
            from_right(g[3][:, :64], col[:, :64])
            + g[3][:, 64:128]
            + from_left(g[3][:, 128:192], col[:, :64])
        )
        return jnp.concatenate([low, high], axis=1).reshape(FR, 2, COLS, CH)

    keep = m["keep"]
    y = back_taps(0)
    m["stop"][...] = y[:, 0].astype(BF)
    pl.when(has_above)(lambda: gup.start())
    keep[:, 0] = y[:, 1]
    y = back_taps(2)
    m["sbot"][...] = y[:, 1].astype(BF)
    pl.when(has_below)(lambda: gdown.start())
    keep[:, 1] = y[:, 0]
    keep[...] = keep[...] + back_taps(1)

    def row_cotangent(r):
        cells = slice(32 * r, 32 * r + 32)
        d = cot_ref[:, cells, :].astype(F32) + rms_back(
            m["motion"][:, cells, :].astype(F32), sgain, keep[:, r]
        )
        m["dmot"][:, cells, :] = d
        d = (0.5 * d).astype(BF)
        for j in range(HALF):
            blocks["cext"][HALF * r + j][8:16] = d[:, BC * j : BC * j + BC]

    def send_halo(b):
        return start(*halo_copies(blocks["cext"][b], m["s3"], m["q3"], b, before, after))

    @pl.when(has_below)
    def _():
        remote(m["stop"], m["gbot"], m["srow"].at[2], m["qrow"].at[2], below).wait_recv()
        keep[:, 1] = keep[:, 1] + m["gbot"][...].astype(F32)

    row_cotangent(1)
    ins = {b: send_halo(b) for b in range(HALF, BLOCKS)}

    @pl.when(has_above)
    def _():
        remote(m["sbot"], m["gtop"], m["srow"].at[3], m["qrow"].at[3], above).wait_recv()
        keep[:, 0] = keep[:, 0] + m["gtop"][...].astype(F32)

    row_cotangent(0)
    ins.update({b: send_halo(b) for b in range(HALF)})

    total = mm_nt(m["act"][...], projt_ref[...]).reshape(FR, CELLS, CH)
    out_ref[...] = (m["motion"][...].astype(F32) + total).astype(BF)

    for b in range(HALF):
        transposed_probs(b)
    outs = {}

    def give_back(b):
        found = mm_nt(m["dz"][BR * b : BR * b + BR, :], wp[...])
        blocks["dh"][b][...] = from_groups(found).astype(BF)
        outs[b] = start(
            *return_copies(blocks["dh"][b], blocks["dback"][b], m["s4"], m["q4"], b, before, after)
        )

    for b in (*range(HALF, BLOCKS), *range(HALF)):
        arrive(ins[b])
        for g, found in enumerate(cell_groups(blocks["cext"][b][pl.ds(shift, 16)])):
            m["call"][BR * b + 128 * g : BR * b + 128 * g + 128, :] = found.astype(BF)
        dm = mm_nt(m["call"][BR * b : BR * b + BR, :], wop[...]).astype(BF)
        for g in range(BG * b, BG * b + BG):
            at = slice(128 * g, 128 * g + 128)
            for i in range(HEADS // 2):
                lanes = slice(128 * i, 128 * i + 128)
                q = z_pair(g, i, 0)
                kst = both_heads(z_pair(g, i, 1), first)
                vst = both_heads(z_pair(g, i, 2), first)
                dmi = dm[128 * (g - BG * b) : 128 * (g - BG * b) + 128, lanes]
                pt = m["pt"][4 * g + i]
                pf = pt.astype(F32)
                dp = mm_nt(vst, dmi)
                t = pf * dp
                ds = jnp.concatenate(
                    [
                        (t[:128] - pf[:128] * jnp.sum(t[:128], axis=0, keepdims=True)) * SCALE,
                        (t[128:] - pf[128:] * jnp.sum(t[128:], axis=0, keepdims=True)) * SCALE,
                    ],
                    axis=0,
                ).astype(BF)
                m["dz"][at, lanes] = mm_tn(ds, kst).astype(BF)
                dk = mm(ds, q)
                m["dz"][at, PADQ + 128 * i : PADQ + 128 * i + 128] = jnp.where(
                    first, dk[:128], dk[128:]
                ).astype(BF)
                dv = mm(pt, dmi)
                m["dz"][at, 2 * PADQ + 128 * i : 2 * PADQ + 128 * i + 128] = jnp.where(
                    first, dv[:128], dv[128:]
                ).astype(BF)
        give_back(b)

    flats = [m[f"flat{j}"] for j in range(3)]
    dw = mm(m["hallt"][...], m["dz"][...])
    doff = dw[CH : CH + 1]
    dwq = dw[:CH] + outer(extra, doff)
    for part in range(3):
        block = mm(dwq[:, PADQ * part : PADQ * part + PADQ].astype(BF), m["pick"][...])
        for j in range(3):
            flats[j][pl.ds(part, CH, stride=3), :] = block[:, 128 * j : 128 * j + 128]
    zeros = jnp.zeros((CH, 64), F32)
    dwo = mm(m["mallt"][...], m["call"][...])
    dext = jnp.sum(mm_nt(stack_parts(doff), wp[...]), axis=0, keepdims=True)
    dtime = outer(emb, dext)
    for j in range(3):
        wide = 128 if j < 2 else 64
        for h in range(HEADS):
            flats[j][960 + HD * h : 960 + HD * h + HD, 0:wide] = dwo[
                HP * h : HP * h + HD, 128 * j : 128 * j + wide
            ]
        flats[j][1280:1600, 0:wide] = dtime[:, 128 * j : 128 * j + wide]
        flats[j][1600:1608, :] = jnp.zeros((8, 128), F32)
    flats[2][960:1280, 64:128] = zeros
    flats[2][1280:1600, 64:128] = zeros

    a = [[m[f"a{k}{j}"] for j in range(3)] for k in range(4)]
    r = [[m[f"r{k}{j}"] for j in range(3)] for k in range(4)]

    core = me["core"]
    stage = []
    for p, order in enumerate(ORDERS):
        for j in range(64):
            to = place_of(j // 2, (j % 2) * 2)
            index = (to[order[0]] * 4 + to[order[1]]) * 4 + to[order[2]]
            for c in range(2):
                first_row = 25 * j + 12 * c
                a[0][p][c, index] = flats[p][first_row : first_row + 16, :].astype(BF)
        stage.append(
            start(
                remote(a[0][p].at[1 - core], r[0][p], m["ssum"].at[p, 0], m["qsum"].at[p, 0], twin)
            )
        )

    def fan_out(part, level):
        axis = ORDERS[part][level - 1]
        step = 16 >> (2 * (level - 1))
        copies = []
        for d in range(3):
            to = (me[axis] + d + 1) % 4
            sem = 3 * level - 2 + d
            copies.append(
                remote(
                    a[level][part].at[pl.ds(to * step, step)], r[level][part].at[d],
                    m["ssum"].at[part, sem], m["qsum"].at[part, sem], peers[axis][d],
                )
            )
        return start(*copies)

    def gathered(part, level):
        step = 16 >> (2 * (level - 1))
        own = me[ORDERS[part][level - 1]]
        total = a[level][part][pl.ds(own * step, step)].astype(F32)
        for d in range(3):
            total = total + r[level][part][d].astype(F32)
        return total

    def finish(b):
        arrive(outs[b])
        d_hidden = blocks["dh"][b][pl.ds(8 - shift, 8)].astype(F32)
        d_hidden = d_hidden + blocks["dback"][b][pl.ds(8 - shift, 8)].astype(F32)
        x = lat_ref[:, BC * b : BC * b + BC, :].astype(F32)
        gin_ref[:, BC * b : BC * b + BC, :] = m["dmot"][:, BC * b : BC * b + BC, :] + rms_back(
            x, mgain, d_hidden
        )

    for p in range(3):
        arrive(stage[p])
        a[1][p][...] = (a[0][p][core].astype(F32) + r[0][p][...].astype(F32)).astype(BF)
        stage[p] = fan_out(p, 1)
    for b in range(HALF, BLOCKS):
        finish(b)
    for level in (2, 3):
        for p in range(3):
            arrive(stage[p])
            a[level][p][...] = gathered(p, level - 1).astype(BF)
            stage[p] = fan_out(p, level)
        if level - 2 < HALF:
            finish(level - 2)
    for p in range(3):
        arrive(stage[p])
        m["sums"][p] = gathered(p, 3)[0] * (1.0 / 256.0)
    sum_ref[...] = flat_line(m["sums"], m["line"], core == 1)
    for copy in sends:
        copy.wait_send()

    @pl.when(has_above)
    def _():
        up.wait_send()
        gup.wait_send()

    @pl.when(has_below)
    def _():
        down.wait_send()
        gdown.wait_send()


def embedding(timestep_ids, channels):
    half_width = channels // 2
    frequency = jnp.exp(-math.log(10000.0) * jnp.arange(half_width, dtype=F32) / half_width)
    angles = timestep_ids.astype(F32)[:, None] * frequency[None, :]
    return jnp.concatenate([jnp.cos(angles), jnp.sin(angles)], axis=-1)


def vmem(count):
    return [pl.BlockSpec(memory_space=VMEM)] * count


def anywhere(count):
    return [pl.BlockSpec(memory_space=pl.ANY)] * count


def params(ident):
    return pltpu.CompilerParams(
        collective_id=ident, has_side_effects=True, vmem_limit_bytes=VLIM
    )


def shaped(*shape, dtype=BF):
    return jax.ShapeDtypeStruct(shape, dtype)


def on_device(
    latents,
    window_shift,
    timesteps,
    motion_gain,
    time_weight,
    qkv_weight,
    attn_out_weight,
    spatial_gain,
    conv_weight,
    proj_weight,
    out_cotangent,
):
    smem = pl.BlockSpec(memory_space=pltpu.SMEM)
    block_output, grad_input, total = pl.pallas_call(
        step_kernel,
        out_shape=(
            VMEM((FR, CELLS, CH), BF), VMEM((FR, CELLS, CH), F32), VMEM((32, 128), F32),
        ),
        in_specs=[smem] + vmem(4) + anywhere(6),
        out_specs=tuple(vmem(3)),
        scratch_shapes=list(scratch_list().values()),
        compiler_params=params(0),
        name="step",
    )(
        window_shift, latents.reshape(FR, CELLS, CH), motion_gain, spatial_gain,
        embedding(timesteps, CH), time_weight, qkv_weight, attn_out_weight, conv_weight,
        proj_weight.T, out_cotangent.reshape(FR, CELLS, CH),
    )
    block_output, grad_input, grad_weights = pl.pallas_call(
        copy_kernel,
        out_shape=(
            shaped(FR, CELLS, CH), shaped(FR, CELLS, CH, dtype=F32), shaped(4000, dtype=F32),
        ),
        in_specs=vmem(3),
        out_specs=tuple(anywhere(2) + vmem(1)),
        scratch_shapes=[pltpu.SemaphoreType.DMA((2,))],
        compiler_params=pltpu.CompilerParams(vmem_limit_bytes=4 * 1024 * 1024),
        name="results",
    )(*(pltpu.with_memory_space_constraint(x, VMEM) for x in (block_output, grad_input, total)))
    return (
        block_output.reshape(latents.shape),
        grad_input.reshape(latents.shape),
        grad_weights,
    )


def solution(mesh):
    placed = (
        P("tm", "row", None, None),
        P(),
        P("tm"),
        P(),
        P(),
        P(),
        P(),
        P(),
        P(),
        P(),
        P("tm", "row", None, None),
    )
    return jax.shard_map(
        on_device,
        mesh=mesh,
        in_specs=placed,
        out_specs=(P("tm", "row", None, None), P("tm", "row", None, None), P(("tm", "row"))),
        check_vma=False,
    )
```

```python
import math

import jax
import jax.numpy as jnp
from jax import lax
from jax.experimental import pallas as pl
from jax.experimental.pallas import tpu as pltpu
from jax.sharding import PartitionSpec as P

BF = jnp.bfloat16
F32 = jnp.float32
MESH = pl.DeviceIdType.MESH
VMEM = pltpu.VMEM

FR = 8
CELLS = 64
COLS = 32
CH = 320
HID = 1280
HEADS = 8
HD = 40
HP = 64
BLOCKS = 4
HALF = BLOCKS // 2
BC = CELLS // BLOCKS
BG = BC // 8
BR = 16 * BC
PADQ = HEADS * HP
PADZ = 3 * PADQ
SCALE = 1.0 / math.sqrt(HD)
EXP2 = SCALE * math.log2(math.e)
EPS = 1e-06
VLIM = 60 * 1024 * 1024


def mm(a, b):
    return jnp.dot(a, b, preferred_element_type=F32)


def mm_nt(a, b):
    return lax.dot_general(a, b, (((1,), (1,)), ((), ())), preferred_element_type=F32)


def mm_tn(a, b):
    return lax.dot_general(a, b, (((0,), (0,)), ((), ())), preferred_element_type=F32)


def rms_scale(values):
    return lax.rsqrt(jnp.mean(values * values, axis=-1, keepdims=True) + EPS)


def rms_back(values, gain, cotangent):
    r = rms_scale(values)
    g = cotangent * gain
    return r * g - values * (r * r * r) * jnp.mean(g * values, axis=-1, keepdims=True)


def parts_of(row):
    first = row.astype(BF).astype(F32)
    rest = row - first
    second = rest.astype(BF).astype(F32)
    return first, second, rest - second


def stack_parts(row):
    a, b, c = parts_of(row)
    at = lax.broadcasted_iota(jnp.int32, (16, row.shape[1]), 0)
    return jnp.where(at == 0, a, jnp.where(at == 1, b, jnp.where(at == 2, c, 0.0))).astype(BF)


def outer(left, right):
    a, b, _ = parts_of(left)
    c, d, _ = parts_of(right)
    at = lax.broadcasted_iota(jnp.int32, (16, left.shape[1]), 0)
    lhs = jnp.where(at < 4, jnp.where(at % 2 == 0, a, b), 0.0).astype(BF)
    at = lax.broadcasted_iota(jnp.int32, (16, right.shape[1]), 0)
    rhs = jnp.where(at < 4, jnp.where(at < 2, c, d), 0.0).astype(BF)
    return mm_tn(lhs, rhs)


def greet(barrier, peers):
    for peer in peers:
        pl.semaphore_signal(barrier, inc=1, device_id=peer, device_id_type=MESH)


def remote(src, dst, send, recv, peer):
    return pltpu.make_async_remote_copy(
        src_ref=src, dst_ref=dst, send_sem=send, recv_sem=recv, device_id=peer, device_id_type=MESH
    )


def ring():
    at, count = lax.axis_index("tm"), lax.axis_size("tm")
    row = lax.axis_index("row")
    return ((at + count - 1) % count, row), ((at + 1) % count, row)


def pair_masks():
    lane = lax.broadcasted_iota(jnp.int32, (128, 128), 1)
    return lane < HP


def both_heads(x, first):
    zero = jnp.zeros_like(x)
    return jnp.concatenate([jnp.where(first, x, zero), jnp.where(first, zero, x)], axis=0)


def pair_probs(q, kst, same):
    s = mm_nt(q, kst)
    e = jnp.where(same, jnp.exp2(s * EXP2), 0.0)
    ea, eb = e[:, :128], e[:, 128:]
    return jnp.concatenate(
        [
            ea * (1.0 / jnp.sum(ea, axis=-1, keepdims=True)),
            eb * (1.0 / jnp.sum(eb, axis=-1, keepdims=True)),
        ],
        axis=1,
    )


def same_cell():
    row = lax.broadcasted_iota(jnp.int32, (128, 256), 0)
    lane = lax.broadcasted_iota(jnp.int32, (128, 256), 1)
    return row % 8 == lane % 8


def halo_copies(ext, send, recv, b, before, after):
    return (
        remote(ext.at[9:16], ext.at[1:8], send.at[0, b], recv.at[0, b], after),
        remote(ext.at[8:15], ext.at[16:23], send.at[1, b], recv.at[1, b], before),
    )


def return_copies(out, back, send, recv, b, before, after):
    return (
        remote(out.at[0:7], back.at[8:15], send.at[0, b], recv.at[0, b], before),
        remote(out.at[9:16], back.at[1:8], send.at[1, b], recv.at[1, b], after),
    )


def column_shifts(flat):
    count = flat.shape[0]
    col = lax.broadcasted_iota(jnp.int32, flat.shape, 0) % COLS
    left = jnp.where(col == 0, 0.0, pltpu.roll(flat, 1, 0))
    right = jnp.where(col == COLS - 1, 0.0, pltpu.roll(flat, count - 1, 0))
    return left, right


ORDERS = (("x", "y", "z"), ("y", "z", "x"), ("z", "x", "y"))


def place_of(tm, row):
    return {"y": tm // 8, "x": (row // 2) * 2 + (tm // 4) % 2, "z": tm % 4, "core": row % 2}


def device_at(at):
    return (at["y"] * 8 + (at["x"] % 2) * 4 + at["z"], (at["x"] // 2) * 2 + at["core"])


def cell_groups(block):
    wide = block.astype(F32)
    return [wide[:, 8 * g : 8 * g + 8].reshape(128, wide.shape[2]) for g in range(BG)]


def from_groups(rows):
    return jnp.concatenate(
        [rows[128 * g : 128 * g + 128].reshape(16, 8, rows.shape[1]) for g in range(BG)], axis=1
    )


def flat_line(sums, line, half):
    lane = lax.broadcasted_iota(jnp.int32, (8, 128), 1)
    even = [sums[p, pl.ds(0, 8, stride=2), :] for p in range(3)]
    odd = [sums[p, pl.ds(1, 8, stride=2), :] for p in range(3)]
    turned = [pltpu.roll(x, 64, 1) for x in odd]
    low = lane < 64
    pieces = (
        even[0],
        even[1],
        jnp.where(low, even[2], turned[0]),
        jnp.where(low, turned[0], turned[1]),
        jnp.where(low, turned[1], turned[2]),
    )
    line[40:48, :] = jnp.zeros((8, 128), F32)
    for j, piece in enumerate(pieces):
        line[pl.ds(j, 8, stride=5), :] = piece
    lane = lax.broadcasted_iota(jnp.int32, (32, 128), 1)
    later = jnp.where(
        lane < 96, pltpu.roll(line[1:33, :], 96, 1), pltpu.roll(line[2:34, :], 96, 1)
    )
    return jnp.where(half, later, line[0:32, :])


def copy_kernel(out_in, gin_in, line_in, out_ref, gin_ref, line_ref, sems):
    copies = [
        pltpu.make_async_copy(out_in, out_ref, sems.at[0]),
        pltpu.make_async_copy(gin_in, gin_ref, sems.at[1]),
    ]
    for copy in copies:
        copy.start()
    for j in range(31):
        line_ref[128 * j : 128 * j + 128] = line_in[j]
    line_ref[3968:4000] = line_in[31, 0:32]
    for copy in copies:
        copy.wait()


def scratch_list():
    dma = pltpu.SemaphoreType.DMA
    plane = VMEM((FR, COLS, CH), BF)
    tile = (16, 128)
    return {
        "wo32": VMEM((PADQ, CH), F32),
        "wp": VMEM((CH, PADZ), BF),
        "wop": VMEM((PADQ, CH), BF),
        **{f"hext{b}": VMEM((24, BC, CH), BF) for b in range(BLOCKS)},
        **{f"wout{b}": VMEM((16, BC, CH), BF) for b in range(BLOCKS)},
        **{f"back{b}": VMEM((16, BC, CH), BF) for b in range(BLOCKS)},
        **{f"cext{b}": VMEM((24, BC, CH), BF) for b in range(BLOCKS)},
        **{f"dh{b}": VMEM((16, BC, CH), BF) for b in range(BLOCKS)},
        **{f"dback{b}": VMEM((16, BC, CH), BF) for b in range(BLOCKS)},
        "z": VMEM((1024, PADZ), BF),
        "hall": VMEM((1024, 384), BF),
        "mall": VMEM((1024, PADQ), BF),
        "call": VMEM((1024, CH), BF),
        "dz": VMEM((1024, PADZ), BF),
        "pt": VMEM((32, 256, 128), BF),
        "motion": VMEM((FR, CELLS, CH), BF),
        "normed": VMEM((FR, CELLS, CH), BF),
        "dmot": VMEM((FR, CELLS, CH), F32),
        "wbuf": VMEM((3, 1024, HID), BF),
        "x3": VMEM((FR, 4, COLS, 1024), BF),
        "top": plane,
        "bot": plane,
        "pre": VMEM((FR * CELLS, HID), F32),
        "dpre": VMEM((FR * CELLS, HID), BF),
        "gtop": plane,
        "gbot": plane,
        "stop": plane,
        "sbot": plane,
        "keep": VMEM((FR, 2, COLS, CH), F32),
        **{f"flat{j}": VMEM((1608, 128), F32) for j in range(3)},
        **{f"a0{j}": VMEM((2, 64) + tile, BF) for j in range(3)},
        **{f"r0{j}": VMEM((64,) + tile, BF) for j in range(3)},
        **{f"a1{j}": VMEM((64,) + tile, BF) for j in range(3)},
        **{f"r1{j}": VMEM((3, 16) + tile, BF) for j in range(3)},
        **{f"a2{j}": VMEM((16,) + tile, BF) for j in range(3)},
        **{f"r2{j}": VMEM((3, 4) + tile, BF) for j in range(3)},
        **{f"a3{j}": VMEM((4,) + tile, BF) for j in range(3)},
        **{f"r3{j}": VMEM((3, 1) + tile, BF) for j in range(3)},
        "act": VMEM((FR * CELLS, HID), BF),
        "dact": VMEM((FR * CELLS, HID), F32),
        "hallt": VMEM((384, 1024), BF),
        "kt": VMEM((PADQ, 1024), BF),
        "mallt": VMEM((PADQ, 1024), BF),
        "pick": VMEM((PADQ, 384), BF),
        "tw": VMEM((CH, CH), F32),
        "w": VMEM((CH, 3 * CH), BF),
        "wo": VMEM((CH, CH), BF),
        "projt": VMEM((CH, HID), BF),
        "cot": VMEM((FR, CELLS, CH), BF),
        "line": VMEM((48, 128), F32),
        "sums": VMEM((3, 16, 128), F32),
        "osem": dma((5,)),
        "wsem": dma((18,)),
        **{name: dma((2, BLOCKS)) for name in ("s1", "q1", "s2", "q2", "s3", "q3", "s4", "q4")},
        "srow": dma((4,)),
        "qrow": dma((4,)),
        "ssum": dma((3, 10)),
        "qsum": dma((3, 10)),
    }


def step_kernel(
    shift_ref, lat_ref, mgain_ref, sgain_ref, emb_ref, tw_hbm, w_hbm, wo_hbm, conv_ref, projt_hbm, cot_hbm,
    out_ref, gin_ref, sum_ref, *rest,
):
    m = dict(zip(scratch_list(), rest))
    blocks = {name: [m[f"{name}{b}"] for b in range(BLOCKS)] for name in ("hext", "wout", "back", "cext", "dh", "dback")}
    wp, wop, wbuf, x3, dpre = m["wp"], m["wop"], m["wbuf"], m["x3"], m["dpre"]
    tm, row = lax.axis_index("tm"), lax.axis_index("row")
    rows = lax.axis_size("row")
    before, after = ring()
    above, below = (tm, row - 1), (tm, row + 1)
    has_above, has_below = row > 0, row < rows - 1
    me = place_of(tm, row)
    twin = device_at({**me, "core": 1 - me["core"]})
    peers = {
        axis: [device_at({**me, axis: (me[axis] + d) % 4}) for d in (1, 2, 3)] for axis in "xyz"
    }
    shift = shift_ref[0]
    mgain, sgain = mgain_ref[...].reshape(1, CH), sgain_ref[...].reshape(1, CH)

    barrier = pltpu.get_barrier_semaphore()
    neighbours = (before, after, (tm, (row + 1) % rows), (tm, (row + rows - 1) % rows), twin)
    neighbours += tuple(peers["x"] + peers["y"] + peers["z"])
    greet(barrier, neighbours)
    small = {}
    for j, (name, ref) in enumerate(
        (("w", w_hbm), ("wo", wo_hbm), ("tw", tw_hbm), ("cot", cot_hbm), ("projt", projt_hbm))
    ):
        small[name] = pltpu.make_async_copy(ref, m[name], m["osem"].at[j])
        small[name].start()
    w_ref, wo_ref, tw_ref, cot_ref, projt_ref = (m[k] for k in ("w", "wo", "tw", "cot", "projt"))
    loads = []
    for dy in (1, 0, 2):
        for t in range(3):
            loads.append((conv_ref.at[3 * dy + t, 0:256, :], wbuf.at[dy, 256 * t : 256 * t + 256, :]))
            loads.append((conv_ref.at[3 * dy + t, 256:320, :], wbuf.at[dy, 768 + 64 * t : 832 + 64 * t, :]))
    loads = [pltpu.make_async_copy(a, c, m["wsem"].at[j]) for j, (a, c) in enumerate(loads)]
    for load in loads:
        load.start()

    for b in range(BLOCKS):
        x = lat_ref[:, BC * b : BC * b + BC, :].astype(F32)
        blocks["hext"][b][8:16] = (x * rms_scale(x) * mgain).astype(BF)
    pl.semaphore_wait(barrier, len(neighbours))
    sends = []

    def start(*copies):
        for copy in copies:
            copy.start()
        sends.extend(copies)
        return copies

    def halos(name, send, recv):
        return [
            start(*halo_copies(blocks[name][b], m[send], m[recv], b, before, after))
            for b in range(BLOCKS)
        ]

    def arrive(pair):
        for copy in pair:
            copy.wait_recv()

    ins = halos("hext", "s1", "q1")
    small["w"].wait()
    wp[...] = jnp.zeros_like(wp)
    for j in range(3 * HEADS):
        wp[:, HP * j : HP * j + HD] = w_ref[:, HD * j : HD * j + HD]
    m["wo32"][...] = jnp.zeros_like(m["wo32"])
    small["wo"].wait()
    wo_f = wo_ref[...].astype(F32)
    for h in range(HEADS):
        m["wo32"][HP * h : HP * h + HD, :] = wo_f[HD * h : HD * h + HD]
    wop[...] = m["wo32"][...].astype(BF)
    small["tw"].wait()
    emb = emb_ref[...]
    three = stack_parts(emb)
    extra = sum(mm(three, part.astype(BF)) for part in parts_of(tw_ref[...]))
    extra = jnp.sum(extra, axis=0, keepdims=True)
    off = jnp.sum(mm(stack_parts(extra), wp[...]), axis=0, keepdims=True)
    for dy in range(3):
        wbuf[dy, 960:1024, :] = jnp.zeros((64, HID), BF)
    first, same = pair_masks(), same_cell()
    same_t = (
        lax.broadcasted_iota(jnp.int32, (256, 128), 0) % 8
        == lax.broadcasted_iota(jnp.int32, (256, 128), 1) % 8
    )
    at = lax.broadcasted_iota(jnp.int32, (PADQ, 384), 0)
    lane = lax.broadcasted_iota(jnp.int32, (PADQ, 384), 1)
    pick = (lane == HD * (at // HP) + at % HP) & (at % HP < HD)
    m["pick"][...] = jnp.where(pick, 1.0, 0.0).astype(BF)
    lane = lax.broadcasted_iota(jnp.int32, (BR, 64), 1)
    ones = jnp.where(lane == 0, 1.0, 0.0).astype(BF)

    def z_pair(g, i, part):
        return m["z"][128 * g : 128 * g + 128, PADQ * part + 128 * i : PADQ * part + 128 * i + 128]

    small["cot"].wait()
    small["projt"].wait()
    cot = cot_ref[...].reshape(FR * CELLS, CH)
    for n in range(5):
        m["dact"][:, 256 * n : 256 * n + 256] = mm(cot, projt_ref[:, 256 * n : 256 * n + 256])
    outs = []
    for b in range(BLOCKS):
        arrive(ins[b])
        for g, found in enumerate(cell_groups(blocks["hext"][b][pl.ds(shift, 16)])):
            m["hall"][BR * b + 128 * g : BR * b + 128 * g + 128, 0:CH] = found.astype(BF)
        m["hall"][BR * b : BR * b + BR, CH:384] = ones
        m["z"][BR * b : BR * b + BR, :] = (
            mm(m["hall"][BR * b : BR * b + BR, 0:CH], wp[...]) + off
        ).astype(BF)
        for g in range(BG * b, BG * b + BG):
            for i in range(HEADS // 2):
                p = pair_probs(z_pair(g, i, 0), both_heads(z_pair(g, i, 1), first), same).astype(BF)
                m["mall"][128 * g : 128 * g + 128, 128 * i : 128 * i + 128] = mm(
                    p, both_heads(z_pair(g, i, 2), first)
                ).astype(BF)
        found = mm(m["mall"][BR * b : BR * b + BR, :], wop[...])
        blocks["wout"][b][...] = from_groups(found).astype(BF)
        outs.append(
            start(*return_copies(blocks["wout"][b], blocks["back"][b], m["s2"], m["q2"], b, before, after))
        )

    def transposed_probs(b):
        for g in range(BG * b, BG * b + BG):
            for i in range(HEADS // 2):
                s = mm_nt(both_heads(z_pair(g, i, 1), first), z_pair(g, i, 0))
                e = jnp.where(same_t, jnp.exp2(s * EXP2), 0.0)
                ea, eb = e[:128], e[128:]
                ea = ea * (1.0 / jnp.sum(ea, axis=0, keepdims=True))
                eb = eb * (1.0 / jnp.sum(eb, axis=0, keepdims=True))
                m["pt"][4 * g + i, 0:128] = ea.astype(BF)
                m["pt"][4 * g + i, 128:256] = eb.astype(BF)

    m["hallt"][...] = m["hall"][...].T
    m["mallt"][...] = m["mall"][...].T
    m["kt"][...] = m["z"][:, PADQ : 2 * PADQ].T
    for b in range(HALF, BLOCKS):
        transposed_probs(b)

    up = remote(m["normed"].at[:, 0:32, :], m["bot"], m["srow"].at[0], m["qrow"].at[0], above)
    down = remote(m["normed"].at[:, 32:64, :], m["top"], m["srow"].at[1], m["qrow"].at[1], below)
    gup = remote(m["stop"], m["gbot"], m["srow"].at[2], m["qrow"].at[2], above)
    gdown = remote(m["sbot"], m["gtop"], m["srow"].at[3], m["qrow"].at[3], below)
    def place(at, plane):
        flat = plane.astype(F32).reshape(FR * COLS, CH)
        left, right = column_shifts(flat)
        for t, values in enumerate((left, flat, right)):
            values = values.astype(BF).reshape(FR, COLS, CH)
            x3[:, at, :, 256 * t : 256 * t + 256] = values[:, :, :256]
            x3[:, at, :, 768 + 64 * t : 832 + 64 * t] = values[:, :, 256:]
        x3[:, at, :, 960:1024] = jnp.zeros((FR, COLS, 64), BF)

    for b in range(BLOCKS):
        arrive(outs[b])
        x = lat_ref[:, BC * b : BC * b + BC, :].astype(F32)
        both = blocks["wout"][b][pl.ds(8 - shift, 8)].astype(F32)
        both = both + blocks["back"][b][pl.ds(8 - shift, 8)].astype(F32)
        moved = (x + 0.5 * both).astype(BF)
        m["motion"][:, BC * b : BC * b + BC, :] = moved
        moved = moved.astype(F32)
        m["normed"][:, BC * b : BC * b + BC, :] = (moved * rms_scale(moved) * sgain).astype(BF)
        if b == BLOCKS // 2 - 1:
            pl.when(has_above)(lambda: up.start())
            place(1, m["normed"][:, 0:32, :])
        if b == BLOCKS - 1:
            pl.when(has_below)(lambda: down.start())

    place(2, m["normed"][:, 32:64, :])

    def add_taps(dy, n):
        taps = x3[:, dy : dy + 2].reshape(FR * CELLS, 1024)
        return mm(taps, wbuf[dy, :, 256 * n : 256 * n + 256])

    for load in loads[:6]:
        load.wait()
    for n in range(5):
        m["pre"][:, 256 * n : 256 * n + 256] = add_taps(1, n)

    @pl.when(has_below)
    def _():
        remote(m["normed"].at[:, 0:32, :], m["bot"], m["srow"].at[0], m["qrow"].at[0], below).wait_recv()
        place(3, m["bot"][...])

    @pl.when(jnp.logical_not(has_below))
    def _():
        x3[:, 3] = jnp.zeros((FR, COLS, 1024), BF)

    @pl.when(has_above)
    def _():
        remote(m["normed"].at[:, 32:64, :], m["top"], m["srow"].at[1], m["qrow"].at[1], above).wait_recv()
        place(0, m["top"][...])

    @pl.when(jnp.logical_not(has_above))
    def _():
        x3[:, 0] = jnp.zeros((FR, COLS, 1024), BF)

    for load in loads[6:]:
        load.wait()
    c0, c1 = math.sqrt(2.0 / math.pi), 0.044715
    for n in range(5):
        u = m["pre"][:, 256 * n : 256 * n + 256] + add_taps(0, n) + add_taps(2, n)
        dact = m["dact"][:, 256 * n : 256 * n + 256]
        sq = u * u
        th = jnp.tanh(c0 * u * (1.0 + c1 * sq))
        half = 0.5 + 0.5 * th
        act = u * half
        slope = half + 0.5 * u * (1.0 - th * th) * (c0 + (3.0 * c0 * c1) * sq)
        dpre[:, 256 * n : 256 * n + 256] = (slope * dact).astype(BF)
        m["act"][:, 256 * n : 256 * n + 256] = act.astype(BF)

    def back_taps(dy):
        g = [mm_nt(dpre[...], wbuf[dy, 256 * j : 256 * j + 256, :]) for j in range(4)]
        col = lax.broadcasted_iota(jnp.int32, (FR * CELLS, 256), 0) % COLS
        count = FR * CELLS

        def from_right(x, c):
            return jnp.where(c == COLS - 1, 0.0, pltpu.roll(x, count - 1, 0))

        def from_left(x, c):
            return jnp.where(c == 0, 0.0, pltpu.roll(x, 1, 0))

        low = from_right(g[0], col) + g[1] + from_left(g[2], col)
        high = (
            from_right(g[3][:, :64], col[:, :64])
            + g[3][:, 64:128]
            + from_left(g[3][:, 128:192], col[:, :64])
        )
        return jnp.concatenate([low, high], axis=1).reshape(FR, 2, COLS, CH)

    keep = m["keep"]
    y = back_taps(0)
    m["stop"][...] = y[:, 0].astype(BF)
    pl.when(has_above)(lambda: gup.start())
    keep[:, 0] = y[:, 1]
    y = back_taps(2)
    m["sbot"][...] = y[:, 1].astype(BF)
    pl.when(has_below)(lambda: gdown.start())
    keep[:, 1] = y[:, 0]
    keep[...] = keep[...] + back_taps(1)

    def row_cotangent(r):
        cells = slice(32 * r, 32 * r + 32)
        d = cot_ref[:, cells, :].astype(F32) + rms_back(
            m["motion"][:, cells, :].astype(F32), sgain, keep[:, r]
        )
        m["dmot"][:, cells, :] = d
        d = (0.5 * d).astype(BF)
        for j in range(HALF):
            blocks["cext"][HALF * r + j][8:16] = d[:, BC * j : BC * j + BC]

    def send_halo(b):
        return start(*halo_copies(blocks["cext"][b], m["s3"], m["q3"], b, before, after))

    @pl.when(has_below)
    def _():
        remote(m["stop"], m["gbot"], m["srow"].at[2], m["qrow"].at[2], below).wait_recv()
        keep[:, 1] = keep[:, 1] + m["gbot"][...].astype(F32)

    row_cotangent(1)
    ins = {b: send_halo(b) for b in range(HALF, BLOCKS)}

    @pl.when(has_above)
    def _():
        remote(m["sbot"], m["gtop"], m["srow"].at[3], m["qrow"].at[3], above).wait_recv()
        keep[:, 0] = keep[:, 0] + m["gtop"][...].astype(F32)

    row_cotangent(0)
    ins.update({b: send_halo(b) for b in range(HALF)})

    total = mm_nt(m["act"][...], projt_ref[...]).reshape(FR, CELLS, CH)
    out_ref[...] = (m["motion"][...].astype(F32) + total).astype(BF)

    for b in range(HALF):
        transposed_probs(b)
    outs = {}

    def give_back(b):
        found = mm_nt(m["dz"][BR * b : BR * b + BR, :], wp[...])
        blocks["dh"][b][...] = from_groups(found).astype(BF)
        outs[b] = start(
            *return_copies(blocks["dh"][b], blocks["dback"][b], m["s4"], m["q4"], b, before, after)
        )

    for b in (*range(HALF, BLOCKS), *range(HALF)):
        arrive(ins[b])
        for g, found in enumerate(cell_groups(blocks["cext"][b][pl.ds(shift, 16)])):
            m["call"][BR * b + 128 * g : BR * b + 128 * g + 128, :] = found.astype(BF)
        dm = mm_nt(m["call"][BR * b : BR * b + BR, :], wop[...]).astype(BF)
        for g in range(BG * b, BG * b + BG):
            at = slice(128 * g, 128 * g + 128)
            pairs = range(HEADS // 2)
            dmi = [
                dm[128 * (g - BG * b) : 128 * (g - BG * b) + 128, 128 * i : 128 * i + 128]
                for i in pairs
            ]
            dps = [mm_nt(both_heads(z_pair(g, i, 2), first), dmi[i]) for i in pairs]
            dss = []
            for i in pairs:
                pf = m["pt"][4 * g + i].astype(F32)
                t = pf * dps[i]
                ds = [
                    (t[h] - pf[h] * jnp.sum(t[h], axis=0, keepdims=True)) * SCALE
                    for h in (slice(0, 128), slice(128, 256))
                ]
                dss.append(jnp.concatenate(ds, axis=0).astype(BF))
            for i in pairs:
                dv = mm(m["pt"][4 * g + i], dmi[i])
                m["dz"][at, 2 * PADQ + 128 * i : 2 * PADQ + 128 * i + 128] = jnp.where(
                    first, dv[:128], dv[128:]
                ).astype(BF)
            for i in pairs:
                ds = dss[i]
                kt = m["kt"][128 * i : 128 * i + 128, at]
                dq = jnp.concatenate([mm(kt[:HP], ds[:128]), mm(kt[HP:], ds[128:])], axis=0)
                m["dz"][at, 128 * i : 128 * i + 128] = dq.T.astype(BF)
                dk = mm(ds, z_pair(g, i, 0))
                m["dz"][at, PADQ + 128 * i : PADQ + 128 * i + 128] = jnp.where(
                    first, dk[:128], dk[128:]
                ).astype(BF)
        give_back(b)

    flats = [m[f"flat{j}"] for j in range(3)]
    dw = mm(m["hallt"][...], m["dz"][...])
    doff = dw[CH : CH + 1]
    dwq = dw[:CH] + outer(extra, doff)
    for part in range(3):
        block = mm(dwq[:, PADQ * part : PADQ * part + PADQ].astype(BF), m["pick"][...])
        for j in range(3):
            flats[j][pl.ds(part, CH, stride=3), :] = block[:, 128 * j : 128 * j + 128]
    zeros = jnp.zeros((CH, 64), F32)
    dwo = mm(m["mallt"][...], m["call"][...])
    dext = jnp.sum(mm_nt(stack_parts(doff), wp[...]), axis=0, keepdims=True)
    dtime = outer(emb, dext)
    for j in range(3):
        wide = 128 if j < 2 else 64
        for h in range(HEADS):
            flats[j][960 + HD * h : 960 + HD * h + HD, 0:wide] = dwo[
                HP * h : HP * h + HD, 128 * j : 128 * j + wide
            ]
        flats[j][1280:1600, 0:wide] = dtime[:, 128 * j : 128 * j + wide]
        flats[j][1600:1608, :] = jnp.zeros((8, 128), F32)
    flats[2][960:1280, 64:128] = zeros
    flats[2][1280:1600, 64:128] = zeros

    a = [[m[f"a{k}{j}"] for j in range(3)] for k in range(4)]
    r = [[m[f"r{k}{j}"] for j in range(3)] for k in range(4)]

    core = me["core"]
    stage = []
    for p, order in enumerate(ORDERS):
        for j in range(64):
            to = place_of(j // 2, (j % 2) * 2)
            index = (to[order[0]] * 4 + to[order[1]]) * 4 + to[order[2]]
            for c in range(2):
                first_row = 25 * j + 12 * c
                a[0][p][c, index] = flats[p][first_row : first_row + 16, :].astype(BF)
        stage.append(
            start(
                remote(a[0][p].at[1 - core], r[0][p], m["ssum"].at[p, 0], m["qsum"].at[p, 0], twin)
            )
        )

    def fan_out(part, level):
        axis = ORDERS[part][level - 1]
        step = 16 >> (2 * (level - 1))
        copies = []
        for d in range(3):
            to = (me[axis] + d + 1) % 4
            sem = 3 * level - 2 + d
            copies.append(
                remote(
                    a[level][part].at[pl.ds(to * step, step)], r[level][part].at[d],
                    m["ssum"].at[part, sem], m["qsum"].at[part, sem], peers[axis][d],
                )
            )
        return start(*copies)

    def gathered(part, level):
        step = 16 >> (2 * (level - 1))
        own = me[ORDERS[part][level - 1]]
        total = a[level][part][pl.ds(own * step, step)].astype(F32)
        for d in range(3):
            total = total + r[level][part][d].astype(F32)
        return total

    def finish(b):
        arrive(outs[b])
        d_hidden = blocks["dh"][b][pl.ds(8 - shift, 8)].astype(F32)
        d_hidden = d_hidden + blocks["dback"][b][pl.ds(8 - shift, 8)].astype(F32)
        x = lat_ref[:, BC * b : BC * b + BC, :].astype(F32)
        gin_ref[:, BC * b : BC * b + BC, :] = m["dmot"][:, BC * b : BC * b + BC, :] + rms_back(
            x, mgain, d_hidden
        )

    for p in range(3):
        arrive(stage[p])
        a[1][p][...] = (a[0][p][core].astype(F32) + r[0][p][...].astype(F32)).astype(BF)
        stage[p] = fan_out(p, 1)
    for b in range(HALF, BLOCKS):
        finish(b)
    for level in (2, 3):
        for p in range(3):
            arrive(stage[p])
            a[level][p][...] = gathered(p, level - 1).astype(BF)
            stage[p] = fan_out(p, level)
        if level - 2 < HALF:
            finish(level - 2)
    for p in range(3):
        arrive(stage[p])
        m["sums"][p] = gathered(p, 3)[0] * (1.0 / 256.0)
    sum_ref[...] = flat_line(m["sums"], m["line"], core == 1)
    for copy in sends:
        copy.wait_send()

    @pl.when(has_above)
    def _():
        up.wait_send()
        gup.wait_send()

    @pl.when(has_below)
    def _():
        down.wait_send()
        gdown.wait_send()


def embedding(timestep_ids, channels):
    half_width = channels // 2
    frequency = jnp.exp(-math.log(10000.0) * jnp.arange(half_width, dtype=F32) / half_width)
    angles = timestep_ids.astype(F32)[:, None] * frequency[None, :]
    return jnp.concatenate([jnp.cos(angles), jnp.sin(angles)], axis=-1)


def vmem(count):
    return [pl.BlockSpec(memory_space=VMEM)] * count


def anywhere(count):
    return [pl.BlockSpec(memory_space=pl.ANY)] * count


def params(ident):
    return pltpu.CompilerParams(
        collective_id=ident, has_side_effects=True, vmem_limit_bytes=VLIM
    )


def shaped(*shape, dtype=BF):
    return jax.ShapeDtypeStruct(shape, dtype)


def on_device(
    latents,
    window_shift,
    timesteps,
    motion_gain,
    time_weight,
    qkv_weight,
    attn_out_weight,
    spatial_gain,
    conv_weight,
    proj_weight,
    out_cotangent,
):
    smem = pl.BlockSpec(memory_space=pltpu.SMEM)
    block_output, grad_input, total = pl.pallas_call(
        step_kernel,
        out_shape=(
            VMEM((FR, CELLS, CH), BF), VMEM((FR, CELLS, CH), F32), VMEM((32, 128), F32),
        ),
        in_specs=[smem] + vmem(4) + anywhere(6),
        out_specs=tuple(vmem(3)),
        scratch_shapes=list(scratch_list().values()),
        compiler_params=params(0),
        name="step",
    )(
        window_shift, latents.reshape(FR, CELLS, CH), motion_gain, spatial_gain,
        embedding(timesteps, CH), time_weight, qkv_weight, attn_out_weight, conv_weight,
        proj_weight.T, out_cotangent.reshape(FR, CELLS, CH),
    )
    block_output, grad_input, grad_weights = pl.pallas_call(
        copy_kernel,
        out_shape=(
            shaped(FR, CELLS, CH), shaped(FR, CELLS, CH, dtype=F32), shaped(4000, dtype=F32),
        ),
        in_specs=vmem(3),
        out_specs=tuple(anywhere(2) + vmem(1)),
        scratch_shapes=[pltpu.SemaphoreType.DMA((2,))],
        compiler_params=pltpu.CompilerParams(vmem_limit_bytes=4 * 1024 * 1024),
        name="results",
    )(*(pltpu.with_memory_space_constraint(x, VMEM) for x in (block_output, grad_input, total)))
    return (
        block_output.reshape(latents.shape),
        grad_input.reshape(latents.shape),
        grad_weights,
    )


def solution(mesh):
    placed = (
        P("tm", "row", None, None),
        P(),
        P("tm"),
        P(),
        P(),
        P(),
        P(),
        P(),
        P(),
        P(),
        P("tm", "row", None, None),
    )
    return jax.shard_map(
        on_device,
        mesh=mesh,
        in_specs=placed,
        out_specs=(P("tm", "row", None, None), P("tm", "row", None, None), P(("tm", "row"))),
        check_vma=False,
    )
```

```python
import math

import jax
import jax.numpy as jnp
from jax import lax
from jax.experimental import pallas as pl
from jax.experimental.pallas import tpu as pltpu
from jax.sharding import PartitionSpec as P

BF = jnp.bfloat16
F32 = jnp.float32
MESH = pl.DeviceIdType.MESH
VMEM = pltpu.VMEM

FR = 8
CELLS = 64
COLS = 32
CH = 320
HID = 1280
HEADS = 8
HD = 40
HP = 64
BLOCKS = 4
HALF = BLOCKS // 2
BC = CELLS // BLOCKS
BG = BC // 8
BR = 16 * BC
PADQ = HEADS * HP
PADZ = 3 * PADQ
SCALE = 1.0 / math.sqrt(HD)
EXP2 = SCALE * math.log2(math.e)
EPS = 1e-06
VLIM = 60 * 1024 * 1024


def mm(a, b):
    return jnp.dot(a, b, preferred_element_type=F32)


def mm_nt(a, b):
    return lax.dot_general(a, b, (((1,), (1,)), ((), ())), preferred_element_type=F32)


def mm_tn(a, b):
    return lax.dot_general(a, b, (((0,), (0,)), ((), ())), preferred_element_type=F32)


def rms_scale(values):
    return lax.rsqrt(jnp.mean(values * values, axis=-1, keepdims=True) + EPS)


def rms_back(values, gain, cotangent):
    r = rms_scale(values)
    g = cotangent * gain
    return r * g - values * (r * r * r) * jnp.mean(g * values, axis=-1, keepdims=True)


def parts_of(row):
    first = row.astype(BF).astype(F32)
    rest = row - first
    second = rest.astype(BF).astype(F32)
    return first, second, rest - second


def stack_parts(row):
    a, b, c = parts_of(row)
    at = lax.broadcasted_iota(jnp.int32, (16, row.shape[1]), 0)
    return jnp.where(at == 0, a, jnp.where(at == 1, b, jnp.where(at == 2, c, 0.0))).astype(BF)


def outer(left, right):
    a, b, _ = parts_of(left)
    c, d, _ = parts_of(right)
    at = lax.broadcasted_iota(jnp.int32, (16, left.shape[1]), 0)
    lhs = jnp.where(at < 4, jnp.where(at % 2 == 0, a, b), 0.0).astype(BF)
    at = lax.broadcasted_iota(jnp.int32, (16, right.shape[1]), 0)
    rhs = jnp.where(at < 4, jnp.where(at < 2, c, d), 0.0).astype(BF)
    return mm_tn(lhs, rhs)


def greet(barrier, peers):
    for peer in peers:
        pl.semaphore_signal(barrier, inc=1, device_id=peer, device_id_type=MESH)


def remote(src, dst, send, recv, peer):
    return pltpu.make_async_remote_copy(
        src_ref=src, dst_ref=dst, send_sem=send, recv_sem=recv, device_id=peer, device_id_type=MESH
    )


def ring():
    at, count = lax.axis_index("tm"), lax.axis_size("tm")
    row = lax.axis_index("row")
    return ((at + count - 1) % count, row), ((at + 1) % count, row)


def pair_masks():
    lane = lax.broadcasted_iota(jnp.int32, (128, 128), 1)
    return lane < HP


def both_heads(x, first):
    zero = jnp.zeros_like(x)
    return jnp.concatenate([jnp.where(first, x, zero), jnp.where(first, zero, x)], axis=0)


def pair_probs(q, kst, same):
    s = mm_nt(q, kst)
    e = jnp.where(same, jnp.exp2(s * EXP2), 0.0)
    ea, eb = e[:, :128], e[:, 128:]
    return jnp.concatenate(
        [
            ea * (1.0 / jnp.sum(ea, axis=-1, keepdims=True)),
            eb * (1.0 / jnp.sum(eb, axis=-1, keepdims=True)),
        ],
        axis=1,
    )


def same_cell():
    row = lax.broadcasted_iota(jnp.int32, (128, 256), 0)
    lane = lax.broadcasted_iota(jnp.int32, (128, 256), 1)
    return row % 8 == lane % 8


def halo_copies(ext, send, recv, b, before, after):
    return (
        remote(ext.at[9:16], ext.at[1:8], send.at[0, b], recv.at[0, b], after),
        remote(ext.at[8:15], ext.at[16:23], send.at[1, b], recv.at[1, b], before),
    )


def return_copies(out, back, send, recv, b, before, after):
    return (
        remote(out.at[0:7], back.at[8:15], send.at[0, b], recv.at[0, b], before),
        remote(out.at[9:16], back.at[1:8], send.at[1, b], recv.at[1, b], after),
    )


def column_shifts(flat):
    count = flat.shape[0]
    col = lax.broadcasted_iota(jnp.int32, flat.shape, 0) % COLS
    left = jnp.where(col == 0, 0.0, pltpu.roll(flat, 1, 0))
    right = jnp.where(col == COLS - 1, 0.0, pltpu.roll(flat, count - 1, 0))
    return left, right


ORDERS = (("x", "y", "z"), ("y", "z", "x"), ("z", "x", "y"))


def place_of(tm, row):
    return {"y": tm // 8, "x": (row // 2) * 2 + (tm // 4) % 2, "z": tm % 4, "core": row % 2}


def device_at(at):
    return (at["y"] * 8 + (at["x"] % 2) * 4 + at["z"], (at["x"] // 2) * 2 + at["core"])


def cell_groups(block):
    wide = block.astype(F32)
    return [wide[:, 8 * g : 8 * g + 8].reshape(128, wide.shape[2]) for g in range(BG)]


def from_groups(rows):
    return jnp.concatenate(
        [rows[128 * g : 128 * g + 128].reshape(16, 8, rows.shape[1]) for g in range(BG)], axis=1
    )


def flat_line(sums, line, half):
    lane = lax.broadcasted_iota(jnp.int32, (8, 128), 1)
    even = [sums[p, pl.ds(0, 8, stride=2), :] for p in range(3)]
    odd = [sums[p, pl.ds(1, 8, stride=2), :] for p in range(3)]
    turned = [pltpu.roll(x, 64, 1) for x in odd]
    low = lane < 64
    pieces = (
        even[0],
        even[1],
        jnp.where(low, even[2], turned[0]),
        jnp.where(low, turned[0], turned[1]),
        jnp.where(low, turned[1], turned[2]),
    )
    line[40:48, :] = jnp.zeros((8, 128), F32)
    for j, piece in enumerate(pieces):
        line[pl.ds(j, 8, stride=5), :] = piece
    lane = lax.broadcasted_iota(jnp.int32, (32, 128), 1)
    later = jnp.where(
        lane < 96, pltpu.roll(line[1:33, :], 96, 1), pltpu.roll(line[2:34, :], 96, 1)
    )
    return jnp.where(half, later, line[0:32, :])


def copy_kernel(out_in, gin_in, line_in, out_ref, gin_ref, line_ref, sems):
    copies = [
        pltpu.make_async_copy(out_in, out_ref, sems.at[0]),
        pltpu.make_async_copy(gin_in, gin_ref, sems.at[1]),
    ]
    for copy in copies:
        copy.start()
    for j in range(31):
        line_ref[128 * j : 128 * j + 128] = line_in[j]
    line_ref[3968:4000] = line_in[31, 0:32]
    for copy in copies:
        copy.wait()


def scratch_list():
    dma = pltpu.SemaphoreType.DMA
    plane = VMEM((FR, COLS, CH), BF)
    tile = (16, 128)
    return {
        "wo32": VMEM((PADQ, CH), F32),
        "wp": VMEM((CH, PADZ), BF),
        "wop": VMEM((PADQ, CH), BF),
        **{f"hext{b}": VMEM((24, BC, CH), BF) for b in range(BLOCKS)},
        **{f"wout{b}": VMEM((16, BC, CH), BF) for b in range(BLOCKS)},
        **{f"back{b}": VMEM((16, BC, CH), BF) for b in range(BLOCKS)},
        **{f"cext{b}": VMEM((24, BC, CH), BF) for b in range(BLOCKS)},
        **{f"dh{b}": VMEM((16, BC, CH), BF) for b in range(BLOCKS)},
        **{f"dback{b}": VMEM((16, BC, CH), BF) for b in range(BLOCKS)},
        "z": VMEM((1024, PADZ), BF),
        "hall": VMEM((1024, 384), BF),
        "mall": VMEM((1024, PADQ), BF),
        "call": VMEM((1024, CH), BF),
        "dz": VMEM((1024, PADZ), BF),
        "pt": VMEM((32, 256, 128), BF),
        "motion": VMEM((FR, CELLS, CH), BF),
        "normed": VMEM((FR, CELLS, CH), BF),
        "dmot": VMEM((FR, CELLS, CH), F32),
        "wbuf": VMEM((3, 1024, HID), BF),
        "x3": VMEM((FR, 4, COLS, 1024), BF),
        "top": plane,
        "bot": plane,
        "pre": VMEM((FR * CELLS, HID), F32),
        "dpre": VMEM((FR * CELLS, HID), BF),
        "gtop": plane,
        "gbot": plane,
        "stop": plane,
        "sbot": plane,
        "keep": VMEM((FR, 2, COLS, CH), F32),
        **{f"flat{j}": VMEM((1608, 128), F32) for j in range(3)},
        **{f"a0{j}": VMEM((2, 64) + tile, BF) for j in range(3)},
        **{f"r0{j}": VMEM((64,) + tile, BF) for j in range(3)},
        **{f"a1{j}": VMEM((64,) + tile, BF) for j in range(3)},
        **{f"r1{j}": VMEM((3, 16) + tile, BF) for j in range(3)},
        **{f"a2{j}": VMEM((16,) + tile, BF) for j in range(3)},
        **{f"r2{j}": VMEM((3, 4) + tile, BF) for j in range(3)},
        **{f"a3{j}": VMEM((4,) + tile, BF) for j in range(3)},
        **{f"r3{j}": VMEM((3, 1) + tile, BF) for j in range(3)},
        "act": VMEM((FR * CELLS, HID), BF),
        "dact": VMEM((FR * CELLS, HID), F32),
        "hallt": VMEM((384, 1024), BF),
        "kt": VMEM((PADQ, 1024), BF),
        "mallt": VMEM((PADQ, 1024), BF),
        "pick": VMEM((PADQ, 384), BF),
        "tw": VMEM((CH, CH), F32),
        "w": VMEM((CH, 3 * CH), BF),
        "wo": VMEM((CH, CH), BF),
        "projt": VMEM((CH, HID), BF),
        "cot": VMEM((FR, CELLS, CH), BF),
        "line": VMEM((48, 128), F32),
        "sums": VMEM((3, 24, 128), F32),
        "osem": dma((5,)),
        "wsem": dma((18,)),
        **{name: dma((2, BLOCKS)) for name in ("s1", "q1", "s2", "q2", "s3", "q3", "s4", "q4")},
        "srow": dma((4,)),
        "qrow": dma((4,)),
        "ssum": dma((3, 10)),
        "qsum": dma((3, 10)),
    }


def step_kernel(
    shift_ref, lat_ref, mgain_ref, sgain_ref, emb_ref, tw_hbm, w_hbm, wo_hbm, conv_ref, projt_hbm, cot_hbm,
    out_ref, gin_ref, sum_ref, *rest,
):
    m = dict(zip(scratch_list(), rest))
    blocks = {name: [m[f"{name}{b}"] for b in range(BLOCKS)] for name in ("hext", "wout", "back", "cext", "dh", "dback")}
    wp, wop, wbuf, x3, dpre = m["wp"], m["wop"], m["wbuf"], m["x3"], m["dpre"]
    tm, row = lax.axis_index("tm"), lax.axis_index("row")
    rows = lax.axis_size("row")
    before, after = ring()
    above, below = (tm, row - 1), (tm, row + 1)
    has_above, has_below = row > 0, row < rows - 1
    me = place_of(tm, row)
    twin = device_at({**me, "core": 1 - me["core"]})
    peers = {
        axis: [device_at({**me, axis: (me[axis] + d) % 4}) for d in (1, 2, 3)] for axis in "xyz"
    }
    shift = shift_ref[0]
    mgain, sgain = mgain_ref[...].reshape(1, CH), sgain_ref[...].reshape(1, CH)

    barrier = pltpu.get_barrier_semaphore()
    neighbours = (before, after, (tm, (row + 1) % rows), (tm, (row + rows - 1) % rows), twin)
    neighbours += tuple(peers["x"] + peers["y"] + peers["z"])
    greet(barrier, neighbours)
    small = {}
    for j, (name, ref) in enumerate(
        (("w", w_hbm), ("wo", wo_hbm), ("tw", tw_hbm), ("cot", cot_hbm), ("projt", projt_hbm))
    ):
        small[name] = pltpu.make_async_copy(ref, m[name], m["osem"].at[j])
        small[name].start()
    w_ref, wo_ref, tw_ref, cot_ref, projt_ref = (m[k] for k in ("w", "wo", "tw", "cot", "projt"))
    loads = []
    for dy in (1, 0, 2):
        for t in range(3):
            loads.append((conv_ref.at[3 * dy + t, 0:256, :], wbuf.at[dy, 256 * t : 256 * t + 256, :]))
            loads.append((conv_ref.at[3 * dy + t, 256:320, :], wbuf.at[dy, 768 + 64 * t : 832 + 64 * t, :]))
    loads = [pltpu.make_async_copy(a, c, m["wsem"].at[j]) for j, (a, c) in enumerate(loads)]
    for load in loads:
        load.start()

    for b in range(BLOCKS):
        x = lat_ref[:, BC * b : BC * b + BC, :].astype(F32)
        blocks["hext"][b][8:16] = (x * rms_scale(x) * mgain).astype(BF)
    pl.semaphore_wait(barrier, len(neighbours))
    sends = []

    def start(*copies):
        for copy in copies:
            copy.start()
        sends.extend(copies)
        return copies

    def halos(name, send, recv):
        return [
            start(*halo_copies(blocks[name][b], m[send], m[recv], b, before, after))
            for b in range(BLOCKS)
        ]

    def arrive(pair):
        for copy in pair:
            copy.wait_recv()

    ins = halos("hext", "s1", "q1")
    small["w"].wait()
    wp[...] = jnp.zeros_like(wp)
    for j in range(3 * HEADS):
        wp[:, HP * j : HP * j + HD] = w_ref[:, HD * j : HD * j + HD]
    m["wo32"][...] = jnp.zeros_like(m["wo32"])
    small["wo"].wait()
    wo_f = wo_ref[...].astype(F32)
    for h in range(HEADS):
        m["wo32"][HP * h : HP * h + HD, :] = wo_f[HD * h : HD * h + HD]
    wop[...] = m["wo32"][...].astype(BF)
    small["tw"].wait()
    emb = emb_ref[...]
    three = stack_parts(emb)
    extra = sum(mm(three, part.astype(BF)) for part in parts_of(tw_ref[...]))
    extra = jnp.sum(extra, axis=0, keepdims=True)
    off = jnp.sum(mm(stack_parts(extra), wp[...]), axis=0, keepdims=True)
    for dy in range(3):
        wbuf[dy, 960:1024, :] = jnp.zeros((64, HID), BF)
    first, same = pair_masks(), same_cell()
    same_t = (
        lax.broadcasted_iota(jnp.int32, (256, 128), 0) % 8
        == lax.broadcasted_iota(jnp.int32, (256, 128), 1) % 8
    )
    at = lax.broadcasted_iota(jnp.int32, (PADQ, 384), 0)
    lane = lax.broadcasted_iota(jnp.int32, (PADQ, 384), 1)
    pick = (lane == HD * (at // HP) + at % HP) & (at % HP < HD)
    m["pick"][...] = jnp.where(pick, 1.0, 0.0).astype(BF)
    lane = lax.broadcasted_iota(jnp.int32, (BR, 64), 1)
    ones = jnp.where(lane == 0, 1.0, 0.0).astype(BF)

    def z_pair(g, i, part):
        return m["z"][128 * g : 128 * g + 128, PADQ * part + 128 * i : PADQ * part + 128 * i + 128]

    small["cot"].wait()
    small["projt"].wait()
    cot = cot_ref[...].reshape(FR * CELLS, CH)
    for n in range(5):
        m["dact"][:, 256 * n : 256 * n + 256] = mm(cot, projt_ref[:, 256 * n : 256 * n + 256])
    outs = []
    for b in range(BLOCKS):
        arrive(ins[b])
        for g, found in enumerate(cell_groups(blocks["hext"][b][pl.ds(shift, 16)])):
            m["hall"][BR * b + 128 * g : BR * b + 128 * g + 128, 0:CH] = found.astype(BF)
        m["hall"][BR * b : BR * b + BR, CH:384] = ones
        m["z"][BR * b : BR * b + BR, :] = (
            mm(m["hall"][BR * b : BR * b + BR, 0:CH], wp[...]) + off
        ).astype(BF)
        for g in range(BG * b, BG * b + BG):
            for i in range(HEADS // 2):
                p = pair_probs(z_pair(g, i, 0), both_heads(z_pair(g, i, 1), first), same).astype(BF)
                m["mall"][128 * g : 128 * g + 128, 128 * i : 128 * i + 128] = mm(
                    p, both_heads(z_pair(g, i, 2), first)
                ).astype(BF)
        found = mm(m["mall"][BR * b : BR * b + BR, :], wop[...])
        blocks["wout"][b][...] = from_groups(found).astype(BF)
        outs.append(
            start(*return_copies(blocks["wout"][b], blocks["back"][b], m["s2"], m["q2"], b, before, after))
        )

    def transposed_probs(b):
        for g in range(BG * b, BG * b + BG):
            for i in range(HEADS // 2):
                s = mm_nt(both_heads(z_pair(g, i, 1), first), z_pair(g, i, 0))
                e = jnp.where(same_t, jnp.exp2(s * EXP2), 0.0)
                ea, eb = e[:128], e[128:]
                ea = ea * (1.0 / jnp.sum(ea, axis=0, keepdims=True))
                eb = eb * (1.0 / jnp.sum(eb, axis=0, keepdims=True))
                m["pt"][4 * g + i, 0:128] = ea.astype(BF)
                m["pt"][4 * g + i, 128:256] = eb.astype(BF)

    m["hallt"][...] = m["hall"][...].T
    m["mallt"][...] = m["mall"][...].T
    m["kt"][...] = m["z"][:, PADQ : 2 * PADQ].T
    for b in range(HALF, BLOCKS):
        transposed_probs(b)

    up = remote(m["normed"].at[:, 0:32, :], m["bot"], m["srow"].at[0], m["qrow"].at[0], above)
    down = remote(m["normed"].at[:, 32:64, :], m["top"], m["srow"].at[1], m["qrow"].at[1], below)
    gup = remote(m["stop"], m["gbot"], m["srow"].at[2], m["qrow"].at[2], above)
    gdown = remote(m["sbot"], m["gtop"], m["srow"].at[3], m["qrow"].at[3], below)
    def place(at, plane):
        flat = plane.astype(F32).reshape(FR * COLS, CH)
        left, right = column_shifts(flat)
        for t, values in enumerate((left, flat, right)):
            values = values.astype(BF).reshape(FR, COLS, CH)
            x3[:, at, :, 256 * t : 256 * t + 256] = values[:, :, :256]
            x3[:, at, :, 768 + 64 * t : 832 + 64 * t] = values[:, :, 256:]
        x3[:, at, :, 960:1024] = jnp.zeros((FR, COLS, 64), BF)

    for b in range(BLOCKS):
        arrive(outs[b])
        x = lat_ref[:, BC * b : BC * b + BC, :].astype(F32)
        both = blocks["wout"][b][pl.ds(8 - shift, 8)].astype(F32)
        both = both + blocks["back"][b][pl.ds(8 - shift, 8)].astype(F32)
        moved = (x + 0.5 * both).astype(BF)
        m["motion"][:, BC * b : BC * b + BC, :] = moved
        moved = moved.astype(F32)
        m["normed"][:, BC * b : BC * b + BC, :] = (moved * rms_scale(moved) * sgain).astype(BF)
        if b == BLOCKS // 2 - 1:
            pl.when(has_above)(lambda: up.start())
            place(1, m["normed"][:, 0:32, :])
        if b == BLOCKS - 1:
            pl.when(has_below)(lambda: down.start())

    place(2, m["normed"][:, 32:64, :])

    def add_taps(dy, n):
        taps = x3[:, dy : dy + 2].reshape(FR * CELLS, 1024)
        return mm(taps, wbuf[dy, :, 256 * n : 256 * n + 256])

    for load in loads[:6]:
        load.wait()
    for n in range(5):
        m["pre"][:, 256 * n : 256 * n + 256] = add_taps(1, n)

    @pl.when(has_below)
    def _():
        remote(m["normed"].at[:, 0:32, :], m["bot"], m["srow"].at[0], m["qrow"].at[0], below).wait_recv()
        place(3, m["bot"][...])

    @pl.when(jnp.logical_not(has_below))
    def _():
        x3[:, 3] = jnp.zeros((FR, COLS, 1024), BF)

    @pl.when(has_above)
    def _():
        remote(m["normed"].at[:, 32:64, :], m["top"], m["srow"].at[1], m["qrow"].at[1], above).wait_recv()
        place(0, m["top"][...])

    @pl.when(jnp.logical_not(has_above))
    def _():
        x3[:, 0] = jnp.zeros((FR, COLS, 1024), BF)

    for load in loads[6:]:
        load.wait()
    c0, c1 = math.sqrt(2.0 / math.pi), 0.044715
    for n in range(5):
        u = m["pre"][:, 256 * n : 256 * n + 256] + add_taps(0, n) + add_taps(2, n)
        dact = m["dact"][:, 256 * n : 256 * n + 256]
        sq = u * u
        th = jnp.tanh(c0 * u * (1.0 + c1 * sq))
        half = 0.5 + 0.5 * th
        act = u * half
        slope = half + act * (1.0 - half) * (2.0 * c0 + (6.0 * c0 * c1) * sq)
        dpre[:, 256 * n : 256 * n + 256] = (slope * dact).astype(BF)
        m["act"][:, 256 * n : 256 * n + 256] = act.astype(BF)

    def back_taps(dy):
        g = [mm_nt(dpre[...], wbuf[dy, 256 * j : 256 * j + 256, :]) for j in range(4)]
        col = lax.broadcasted_iota(jnp.int32, (FR * CELLS, 256), 0) % COLS
        count = FR * CELLS

        def from_right(x, c):
            return jnp.where(c == COLS - 1, 0.0, pltpu.roll(x, count - 1, 0))

        def from_left(x, c):
            return jnp.where(c == 0, 0.0, pltpu.roll(x, 1, 0))

        low = from_right(g[0], col) + g[1] + from_left(g[2], col)
        high = (
            from_right(g[3][:, :64], col[:, :64])
            + g[3][:, 64:128]
            + from_left(g[3][:, 128:192], col[:, :64])
        )
        return jnp.concatenate([low, high], axis=1).reshape(FR, 2, COLS, CH)

    keep = m["keep"]
    y = back_taps(0)
    m["stop"][...] = y[:, 0].astype(BF)
    pl.when(has_above)(lambda: gup.start())
    keep[:, 0] = y[:, 1]
    y = back_taps(2)
    m["sbot"][...] = y[:, 1].astype(BF)
    pl.when(has_below)(lambda: gdown.start())
    keep[:, 1] = y[:, 0]
    keep[...] = keep[...] + back_taps(1)

    def row_cotangent(r):
        cells = slice(32 * r, 32 * r + 32)
        d = cot_ref[:, cells, :].astype(F32) + rms_back(
            m["motion"][:, cells, :].astype(F32), sgain, keep[:, r]
        )
        m["dmot"][:, cells, :] = d
        d = (0.5 * d).astype(BF)
        for j in range(HALF):
            blocks["cext"][HALF * r + j][8:16] = d[:, BC * j : BC * j + BC]

    def send_halo(b):
        return start(*halo_copies(blocks["cext"][b], m["s3"], m["q3"], b, before, after))

    @pl.when(has_below)
    def _():
        remote(m["stop"], m["gbot"], m["srow"].at[2], m["qrow"].at[2], below).wait_recv()
        keep[:, 1] = keep[:, 1] + m["gbot"][...].astype(F32)

    row_cotangent(1)
    ins = {b: send_halo(b) for b in range(HALF, BLOCKS)}

    @pl.when(has_above)
    def _():
        remote(m["sbot"], m["gtop"], m["srow"].at[3], m["qrow"].at[3], above).wait_recv()
        keep[:, 0] = keep[:, 0] + m["gtop"][...].astype(F32)

    row_cotangent(0)
    ins.update({b: send_halo(b) for b in range(HALF)})

    total = mm_nt(m["act"][...], projt_ref[...]).reshape(FR, CELLS, CH)
    out_ref[...] = (m["motion"][...].astype(F32) + total).astype(BF)

    for b in range(HALF):
        transposed_probs(b)
    outs = {}

    def give_back(b):
        found = mm_nt(m["dz"][BR * b : BR * b + BR, :], wp[...])
        blocks["dh"][b][...] = from_groups(found).astype(BF)
        outs[b] = start(
            *return_copies(blocks["dh"][b], blocks["dback"][b], m["s4"], m["q4"], b, before, after)
        )

    for b in (*range(HALF, BLOCKS), *range(HALF)):
        arrive(ins[b])
        for g, found in enumerate(cell_groups(blocks["cext"][b][pl.ds(shift, 16)])):
            m["call"][BR * b + 128 * g : BR * b + 128 * g + 128, :] = found.astype(BF)
        dm = mm_nt(m["call"][BR * b : BR * b + BR, :], wop[...]).astype(BF)
        for g in range(BG * b, BG * b + BG):
            at = slice(128 * g, 128 * g + 128)
            pairs = range(HEADS // 2)
            dmi = [
                dm[128 * (g - BG * b) : 128 * (g - BG * b) + 128, 128 * i : 128 * i + 128]
                for i in pairs
            ]
            dps = [mm_nt(both_heads(z_pair(g, i, 2), first), dmi[i]) for i in pairs]
            dss = []
            for i in pairs:
                pf = m["pt"][4 * g + i].astype(F32)
                t = pf * dps[i]
                ds = [
                    (t[h] - pf[h] * jnp.sum(t[h], axis=0, keepdims=True)) * SCALE
                    for h in (slice(0, 128), slice(128, 256))
                ]
                dss.append(jnp.concatenate(ds, axis=0).astype(BF))
            for i in pairs:
                dv = mm(m["pt"][4 * g + i], dmi[i])
                m["dz"][at, 2 * PADQ + 128 * i : 2 * PADQ + 128 * i + 128] = jnp.where(
                    first, dv[:128], dv[128:]
                ).astype(BF)
            for i in pairs:
                ds = dss[i]
                kt = m["kt"][128 * i : 128 * i + 128, at]
                dq = jnp.concatenate([mm(kt[:HP], ds[:128]), mm(kt[HP:], ds[128:])], axis=0)
                m["dz"][at, 128 * i : 128 * i + 128] = dq.T.astype(BF)
                dk = mm(ds, z_pair(g, i, 0))
                m["dz"][at, PADQ + 128 * i : PADQ + 128 * i + 128] = jnp.where(
                    first, dk[:128], dk[128:]
                ).astype(BF)
        give_back(b)

    flats = [m[f"flat{j}"] for j in range(3)]
    dw = mm(m["hallt"][...], m["dz"][...])
    doff = dw[CH : CH + 1]
    dwq = dw[:CH] + outer(extra, doff)
    for part in range(3):
        block = mm(dwq[:, PADQ * part : PADQ * part + PADQ].astype(BF), m["pick"][...])
        for j in range(3):
            flats[j][pl.ds(part, CH, stride=3), :] = block[:, 128 * j : 128 * j + 128]
    zeros = jnp.zeros((CH, 64), F32)
    dwo = mm(m["mallt"][...], m["call"][...])
    dext = jnp.sum(mm_nt(stack_parts(doff), wp[...]), axis=0, keepdims=True)
    dtime = outer(emb, dext)
    for j in range(3):
        wide = 128 if j < 2 else 64
        for h in range(HEADS):
            flats[j][960 + HD * h : 960 + HD * h + HD, 0:wide] = dwo[
                HP * h : HP * h + HD, 128 * j : 128 * j + wide
            ]
        flats[j][1280:1600, 0:wide] = dtime[:, 128 * j : 128 * j + wide]
        flats[j][1600:1608, :] = jnp.zeros((8, 128), F32)
    flats[2][960:1280, 64:128] = zeros
    flats[2][1280:1600, 64:128] = zeros

    a = [[m[f"a{k}{j}"] for j in range(3)] for k in range(4)]
    r = [[m[f"r{k}{j}"] for j in range(3)] for k in range(4)]

    core = me["core"]
    stage = []
    for p, order in enumerate(ORDERS):
        for j in range(64):
            to = place_of(j // 2, (j % 2) * 2)
            index = (to[order[0]] * 4 + to[order[1]]) * 4 + to[order[2]]
            for c in range(2):
                first_row = 25 * j + 12 * c
                a[0][p][c, index] = flats[p][first_row : first_row + 16, :].astype(BF)
        stage.append(
            start(
                remote(a[0][p].at[1 - core], r[0][p], m["ssum"].at[p, 0], m["qsum"].at[p, 0], twin)
            )
        )

    def fan_out(part, level):
        axis = ORDERS[part][level - 1]
        step = 16 >> (2 * (level - 1))
        copies = []
        for d in range(3):
            to = (me[axis] + d + 1) % 4
            sem = 3 * level - 2 + d
            copies.append(
                remote(
                    a[level][part].at[pl.ds(to * step, step)], r[level][part].at[d],
                    m["ssum"].at[part, sem], m["qsum"].at[part, sem], peers[axis][d],
                )
            )
        return start(*copies)

    def gathered(part, level):
        step = 16 >> (2 * (level - 1))
        own = me[ORDERS[part][level - 1]]
        total = a[level][part][pl.ds(own * step, step)].astype(F32)
        for d in range(3):
            total = total + r[level][part][d].astype(F32)
        return total

    def finish(b):
        arrive(outs[b])
        d_hidden = blocks["dh"][b][pl.ds(8 - shift, 8)].astype(F32)
        d_hidden = d_hidden + blocks["dback"][b][pl.ds(8 - shift, 8)].astype(F32)
        x = lat_ref[:, BC * b : BC * b + BC, :].astype(F32)
        gin_ref[:, BC * b : BC * b + BC, :] = m["dmot"][:, BC * b : BC * b + BC, :] + rms_back(
            x, mgain, d_hidden
        )

    for p in range(3):
        arrive(stage[p])
        a[1][p][...] = (a[0][p][core].astype(F32) + r[0][p][...].astype(F32)).astype(BF)
        stage[p] = fan_out(p, 1)
    for b in range(HALF, BLOCKS):
        finish(b)
    for level in (2, 3):
        for p in range(3):
            arrive(stage[p])
            a[level][p][...] = gathered(p, level - 1).astype(BF)
            stage[p] = fan_out(p, level)
        if level - 2 < HALF:
            finish(level - 2)
    for p in range(3):
        arrive(stage[p])
        m["sums"][p, 0:16] = gathered(p, 3)[0] * (1.0 / 256.0)
    sum_ref[...] = flat_line(m["sums"], m["line"], core == 1)
    for copy in sends:
        copy.wait_send()

    @pl.when(has_above)
    def _():
        up.wait_send()
        gup.wait_send()

    @pl.when(has_below)
    def _():
        down.wait_send()
        gdown.wait_send()


def embedding(timestep_ids, channels):
    half_width = channels // 2
    frequency = jnp.exp(-math.log(10000.0) * jnp.arange(half_width, dtype=F32) / half_width)
    angles = timestep_ids.astype(F32)[:, None] * frequency[None, :]
    return jnp.concatenate([jnp.cos(angles), jnp.sin(angles)], axis=-1)


def vmem(count):
    return [pl.BlockSpec(memory_space=VMEM)] * count


def anywhere(count):
    return [pl.BlockSpec(memory_space=pl.ANY)] * count


def params(ident):
    return pltpu.CompilerParams(
        collective_id=ident, has_side_effects=True, vmem_limit_bytes=VLIM
    )


def shaped(*shape, dtype=BF):
    return jax.ShapeDtypeStruct(shape, dtype)


def on_device(
    latents,
    window_shift,
    timesteps,
    motion_gain,
    time_weight,
    qkv_weight,
    attn_out_weight,
    spatial_gain,
    conv_weight,
    proj_weight,
    out_cotangent,
):
    smem = pl.BlockSpec(memory_space=pltpu.SMEM)
    block_output, grad_input, total = pl.pallas_call(
        step_kernel,
        out_shape=(
            VMEM((FR, CELLS, CH), BF), VMEM((FR, CELLS, CH), F32), VMEM((32, 128), F32),
        ),
        in_specs=[smem] + vmem(4) + anywhere(6),
        out_specs=tuple(vmem(3)),
        scratch_shapes=list(scratch_list().values()),
        compiler_params=params(0),
        name="step",
    )(
        window_shift, latents.reshape(FR, CELLS, CH), motion_gain, spatial_gain,
        embedding(timesteps, CH), time_weight, qkv_weight, attn_out_weight, conv_weight,
        proj_weight.T, out_cotangent.reshape(FR, CELLS, CH),
    )
    block_output, grad_input, grad_weights = pl.pallas_call(
        copy_kernel,
        out_shape=(
            shaped(FR, CELLS, CH), shaped(FR, CELLS, CH, dtype=F32), shaped(4000, dtype=F32),
        ),
        in_specs=vmem(3),
        out_specs=tuple(anywhere(2) + vmem(1)),
        scratch_shapes=[pltpu.SemaphoreType.DMA((2,))],
        compiler_params=pltpu.CompilerParams(vmem_limit_bytes=4 * 1024 * 1024),
        name="results",
    )(*(pltpu.with_memory_space_constraint(x, VMEM) for x in (block_output, grad_input, total)))
    return (
        block_output.reshape(latents.shape),
        grad_input.reshape(latents.shape),
        grad_weights,
    )


def solution(mesh):
    placed = (
        P("tm", "row", None, None),
        P(),
        P("tm"),
        P(),
        P(),
        P(),
        P(),
        P(),
        P(),
        P(),
        P("tm", "row", None, None),
    )
    return jax.shard_map(
        on_device,
        mesh=mesh,
        in_specs=placed,
        out_specs=(P("tm", "row", None, None), P("tm", "row", None, None), P(("tm", "row"))),
        check_vma=False,
    )
```
